32 devices in a mesh: seq: 8 (over z, x), mp: 4 (over y, core).
Axes of the slice: x: 2, y: 2, z: 4, core: 2. Of those that a mesh axis runs over, the one named last changes fastest.
Arguments:
- scan_points: bfloat16 [16384, 512], P('seq'), may hold values from -6 to 6
- send_order: int32 [16384], P('seq'), may hold values from 0 to 2047, as said below
- arrive_order: int32 [16384], P('seq'), may hold values from 0 to 2047, as said below
- qkv_weight: bfloat16 [512, 3, 512], P(None, None, 'mp')
- out_weight: bfloat16 [512, 512], P(None, 'mp'), may hold values from -0.25 to 0.25
- voxel_grads: bfloat16 [16384, 512], P('seq'), may hold values from -6 to 6
- voxel_shard: int32 [16384, 1], P('seq'), may hold values from 0 to 7; in each aligned block of 2048 rows (0 to 2047, 2048 to 4095, ...) at most 512 rows name the same one
- voxel_point: int32 [16384], P('seq'), may hold values from 0 to 2047
Outputs:
- d_points: float32 [16384, 512], P('seq', 'mp')
- grad_qkv: float32 [512, 3, 512], P('seq', None, 'mp')
- grad_out: float32 [512, 512], P('seq', 'mp')
The draws below stay inside these ranges and needn't reach their ends.
Inputs may be any that keep to these rules, and one draw needn't show every extreme that they name: `send_order`: each aligned block of 2048 entries is a permutation of the numbers 0 to 2047. `arrive_order`: each aligned block of 2048 entries is a permutation of the numbers 0 to 2047. `voxel_shard`: among the rows of one device, at most 512 name the same shard.
All inputs are finite; a program needn't handle non-finite values.
Results may differ from the reference program's by a relative error of at most 0.035.
The reference program's roundings to bfloat16 on the way (of `points`, `hidden`, `projected`, `d_out`, `d_attended`, `attended` and `d_projected`) count: a program that leaves them out, or rounds other values in their place, can miss the bound.
Values may be sent and summed in bfloat16 or wider, within the bound.
No kernel may reach another device: no remote copies, remote signals or barrier semaphores. Data moves between devices by JAX's collectives and lax.ppermute only.
A program may use at most 192 MiB of HBM per device.

```python
import math
import jax
import jax.numpy as jnp
import numpy as np
from jax import lax

D = 512
HD = 16
PATCH = 1024
P_DEV = 2048
V_DEV = 2048
POINTS = 16384
VOXELS = 16384
N_SEQ = 8
N_MP = 4


def block_permutation(subkey):
    return jax.random.permutation(subkey, P_DEV)


def draw_send_order(key, part):
    subkeys = jax.random.split(jax.random.fold_in(key, 11), POINTS // P_DEV)
    return jax.vmap(block_permutation)(subkeys).reshape(-1).astype(jnp.int32)


def draw_arrive_order(key, part):
    subkeys = jax.random.split(jax.random.fold_in(key, 23), POINTS // P_DEV)
    return jax.vmap(block_permutation)(subkeys).reshape(-1).astype(jnp.int32)


def draw_qkv_weight(key, part):
    base = jax.random.normal(jax.random.fold_in(key, 37), (D, 3, D), jnp.float32) * D ** (-0.5)
    return base.astype(jnp.bfloat16)


def with_ends(result, own_key, low, high):
    longest = result.shape.index(max(result.shape))
    spots = []
    for shift in (0, 1):
        where = [jax.random.randint(jax.random.fold_in(own_key, axis), (), 0, length) for axis, length in enumerate(result.shape)]
        where[longest] = (where[longest] + shift) % result.shape[longest]
        spots.append(tuple(where))
    return result.at[spots[0]].set(low).at[spots[1]].set(high)


def levels(stream_key, dims, pieces, low, high):
    def one(position, shards_of):
        draws = jax.random.uniform(jax.random.fold_in(jax.random.fold_in(stream_key, 6), position), (shards_of,), jnp.float32, low / len(pieces), high / len(pieces))
        return jnp.repeat(jnp.exp(draws), dims[position] // shards_of).reshape((-1,) + (1,) * (len(dims) - position - 1))

    factor_of = one(*pieces[0])
    for cut in pieces[1:]:
        factor_of = factor_of * one(*cut)
    return factor_of


def assign_block(rng, own, number, rows, count, top, most, skew):
    order = jax.random.permutation(rng, count)
    heavy_load, usual = portions_of(count, rows * top, most, skew, True), portions_of(count, rows * top, most, skew, False)
    places = jnp.arange(count)

    def named(lengths, turn):
        used = int((lengths > 0).sum())
        fixed = max(1, used // 4)
        moved = fixed + (places - fixed + turn * (used - fixed)) % max(1, count - fixed)
        return jnp.zeros((count,), jnp.int32).at[order[jnp.where(places < fixed, places, moved)]].set(jnp.asarray(lengths, jnp.int32))

    lengths = jnp.where(number % 4 == 0, named(heavy_load, number // 4), named(usual, number - number // 4 - 1))
    mixed = jax.random.permutation(jax.random.fold_in(own, 3), count)
    source_of, receiver = mixed[0:count // 2 * 2:2], mixed[1:count // 2 * 2:2]
    room = jnp.minimum(lengths[source_of] - 1, most - lengths[receiver]) // 2
    room = jnp.where((source_of == order[0]) | (receiver == order[0]) | (lengths[receiver] == 0), 0, jnp.maximum(room, 0))
    moved = jax.random.randint(jax.random.fold_in(own, 4), (count // 2,), 0, 1 << 20) % (room + 1)
    lengths = lengths.at[source_of].add(-moved).at[receiver].add(moved)
    items = jnp.searchsorted(jnp.cumsum(lengths), jnp.arange(rows * top), side="right").astype(jnp.int32)
    table = items.reshape(top, rows).T
    table = table[jax.random.permutation(jax.random.fold_in(own, 1), rows)]
    turn = jax.random.randint(jax.random.fold_in(own, 2), (rows, 1), 0, top)
    return jnp.take_along_axis(table, (jnp.arange(top)[None, :] + turn) % top, axis=1)


def portions_of(amount, total, reach, slope, full):
    loads = [(1 << 20) // math.isqrt(rank ** slope) + 1 for rank in range(1, amount + 1)]
    largest = reach if full else min(reach, max(-(-total // amount), total * loads[0] // sum(loads)))
    least = 1 if total - largest >= amount - 1 else 0
    given, spare = [largest] + [least] * (amount - 1), total - largest - least * (amount - 1)
    while spare > 0:
        free = [i for i in range(1, amount) if given[i] < largest] or [i for i in range(1, amount) if given[i] < reach]
        pool, budget = sum([loads[i] for i in free]), spare
        for i in free:
            extra = min(reach - given[i], max(1, budget * loads[i] // pool), spare)
            given[i] = given[i] + extra
            spare = spare - extra
    return np.array(given)


def normal_values(rng, dims, width, most, cuts=(), dtype=jnp.bfloat16):
    entries = width * jax.random.normal(rng, dims, jnp.float32)
    if cuts:
        entries = entries * levels(rng, dims, cuts, -0.22, 0.18)
    return jnp.clip(entries, -most, most).astype(dtype)


def setup_inputs(seed: int = 0) -> dict:
    arg_keys = jax.random.split(jax.random.key(seed), 9)
    scan_points = normal_values(arg_keys[0], (POINTS, D), 1.0, 6.0, ((0, 8),))
    send_order = draw_send_order(jax.random.fold_in(arg_keys[8], 71), 0)
    arrive_order = draw_arrive_order(jax.random.fold_in(arg_keys[8], 71), 0)
    qkv_weight = draw_qkv_weight(jax.random.fold_in(arg_keys[8], 71), 0)
    out_weight = normal_values(arg_keys[4], (D, D), D ** -0.5, 0.25, ((1, 4),))
    voxel_grads = normal_values(arg_keys[5], (VOXELS, D), 1.0, 6.0, ((0, 8),))
    voxel_shard_keys = jax.random.split(jax.random.fold_in(arg_keys[6], 1), VOXELS // V_DEV)
    voxel_shard_turns = jax.random.permutation(jax.random.fold_in(arg_keys[6], 3), VOXELS // V_DEV)
    voxel_shard = jax.vmap(lambda own, number: assign_block(jax.random.fold_in(arg_keys[6], 2), own, number, V_DEV, N_SEQ, 1, 2 * V_DEV // N_SEQ, 2))(voxel_shard_keys, voxel_shard_turns).reshape((VOXELS, 1))
    voxel_point = with_ends(jax.random.randint(arg_keys[7], (VOXELS,), 0, P_DEV), jax.random.fold_in(arg_keys[7], 1), 0, P_DEV - 1).astype(jnp.int32)
    return {"scan_points": scan_points, "send_order": send_order, "arrive_order": arrive_order, "qkv_weight": qkv_weight, "out_weight": out_weight, "voxel_grads": voxel_grads, "voxel_shard": voxel_shard, "voxel_point": voxel_point}


score_scale = 0.25
epsilon = 1e-05

def patch_pass(queries, key_rows, values, d_attended):
    row_count = queries.shape[0]
    head_count = queries.shape[1] // HD
    query_heads = queries.reshape(row_count, head_count, HD).astype(jnp.float32)
    key_heads = key_rows.reshape(row_count, head_count, HD).astype(jnp.float32)
    value_heads = values.reshape(row_count, head_count, HD).astype(jnp.float32)
    scores = jnp.einsum('qhc,khc->hqk', query_heads, key_heads) * score_scale
    row_max = lax.optimization_barrier(jnp.max(scores, axis=2, keepdims=True))
    weights_exp = jnp.exp(scores - row_max)
    probabilities = weights_exp / lax.optimization_barrier(jnp.sum(weights_exp, axis=2, keepdims=True))
    prob_rounded = probabilities.astype(jnp.bfloat16).astype(jnp.float32)
    attended = jnp.einsum('hqk,khc->qhc', prob_rounded, value_heads).astype(jnp.bfloat16)
    grad_heads = d_attended.reshape(row_count, head_count, HD).astype(jnp.float32)
    d_probabilities = jnp.einsum('qhc,khc->hqk', grad_heads, value_heads)
    d_values = jnp.einsum('hqk,qhc->khc', prob_rounded, grad_heads).astype(jnp.bfloat16)
    row_delta = lax.optimization_barrier(jnp.sum(grad_heads * attended.astype(jnp.float32), axis=2))
    d_scores = (probabilities * (d_probabilities - row_delta.T[:, :, None]) * score_scale).astype(jnp.bfloat16).astype(jnp.float32)
    d_query = jnp.einsum('hqk,khc->qhc', d_scores, key_heads).astype(jnp.bfloat16)
    d_keys = jnp.einsum('hqk,qhc->khc', d_scores, query_heads).astype(jnp.bfloat16)
    stacked = jnp.stack([d_query, d_keys, d_values], axis=1).reshape(row_count, 3, head_count * HD)
    return (attended.reshape(row_count, head_count * HD), stacked)

def take_rows(block, order):
    return block[order]

def reference(scan_points, send_order, arrive_order, qkv_weight, out_weight, voxel_grads, voxel_shard, voxel_point):
    shards = N_SEQ
    bucket = P_DEV // shards
    total = P_DEV * shards
    blocks = scan_points.reshape(shards, P_DEV, D)
    picked = jax.vmap(take_rows)(blocks, send_order.reshape(shards, P_DEV).astype(jnp.int32))
    picked = picked.reshape(shards, shards, bucket, D).transpose(1, 0, 2, 3).reshape(shards, P_DEV, D)
    points = jax.vmap(take_rows)(picked, arrive_order.reshape(shards, P_DEV).astype(jnp.int32)).reshape(total, D)
    point_float = points.astype(jnp.float32)
    row_mean = lax.optimization_barrier(jnp.mean(point_float, axis=1, keepdims=True))
    centered = point_float - row_mean
    row_var = lax.optimization_barrier(jnp.mean(centered * centered, axis=1, keepdims=True))
    inv_scale = lax.rsqrt(row_var + epsilon)
    normed = centered * inv_scale
    hidden = normed.astype(jnp.bfloat16)
    projected = jnp.einsum('pd,dtc->ptc', hidden.astype(jnp.float32), qkv_weight.astype(jnp.float32)).astype(jnp.bfloat16)
    global_row = (voxel_shard[:, 0] * P_DEV + voxel_point).astype(jnp.int32)
    d_sum = jax.ops.segment_sum(voxel_grads.astype(jnp.float32), global_row, num_segments=total)
    d_out = d_sum.astype(jnp.bfloat16)
    d_attended = jnp.dot(d_out, out_weight, preferred_element_type=jnp.float32).astype(jnp.bfloat16)
    patches = total // PATCH

    def one_patch(operands):
        proj_patch, grad_patch = operands
        return patch_pass(proj_patch[:, 0], proj_patch[:, 1], proj_patch[:, 2], grad_patch)
    attended, d_projected = lax.map(one_patch, (projected.reshape(patches, PATCH, 3, D), d_attended.reshape(patches, PATCH, D)))
    attended = attended.reshape(total, D)
    d_projected = d_projected.reshape(total, 3, D)
    grad_qkv = jnp.einsum('pd,ptc->dtc', hidden.astype(jnp.float32), d_projected.astype(jnp.float32))
    grad_out = jnp.dot(d_out.T, attended, preferred_element_type=jnp.float32)
    group_cols = D // N_MP
    d_hidden = jnp.zeros((total, D), jnp.float32)
    for member in range(N_MP):
        partial_value = jnp.einsum('ptc,dtc->pd', d_projected[:, :, member * group_cols:(member + 1) * group_cols].astype(jnp.float32), qkv_weight[:, :, member * group_cols:(member + 1) * group_cols].astype(jnp.float32))
        partial_value = lax.optimization_barrier(partial_value.astype(jnp.bfloat16)).astype(jnp.float32)
        d_hidden = d_hidden + partial_value
    mean_grad = lax.optimization_barrier(jnp.mean(d_hidden, axis=1, keepdims=True))
    mean_cross = lax.optimization_barrier(jnp.mean(d_hidden * normed, axis=1, keepdims=True))
    d_points = d_out.astype(jnp.float32) + inv_scale * (d_hidden - mean_grad - normed * mean_cross)
    return (d_points, grad_qkv, grad_out)
```

```python
import functools

import jax
import jax.numpy as jnp
from jax import lax
from jax.experimental import pallas as pl
from jax.experimental.pallas import tpu as pltpu
from jax.sharding import PartitionSpec as P

HD = 16
PATCH = 1024
LANES = 128
INDEX_ROWS = 16
INDEX_BASE = 64

score_scale = 0.25
epsilon = 1e-05
log2_e = 1.4426950408889634

f32 = jnp.float32
bf16 = jnp.bfloat16
i32 = jnp.int32

ROWS_BY_ROWS = (((1,), (1,)), ((), ()))


def params(mib):
    return pltpu.CompilerParams(vmem_limit_bytes=mib << 20)


def cost(flops, bytes_accessed, transcendentals=0):
    return pl.CostEstimate(
        flops=int(flops), bytes_accessed=int(bytes_accessed), transcendentals=int(transcendentals)
    )


def dot(a, b):
    return jnp.dot(a, b, preferred_element_type=f32)


def dot_rows(a, b):
    return lax.dot_general(a, b, ROWS_BY_ROWS, preferred_element_type=f32)


def ones_where(mask):
    return jnp.where(mask, 1.0, 0.0).astype(bf16)


def permute_body(column_ref, order_ref, block_ref, out_ref):
    step = pl.program_id(0)
    source_rows = block_ref.shape[0]
    chunks = out_ref.shape[0] // LANES
    lane = lax.broadcasted_iota(i32, (LANES, LANES), 1)
    block = block_ref[...]
    for j in range(chunks):
        wanted = order_ref[pl.ds(step * chunks + j, 1), :].astype(f32)
        wanted = jnp.broadcast_to(wanted, (LANES, LANES)).T.astype(i32)
        onehot = jnp.concatenate(
            [ones_where(wanted == lane + k * LANES) for k in range(source_rows // LANES)], axis=1
        )
        out_ref[j * LANES : (j + 1) * LANES, :] = dot(onehot, block).astype(bf16)


def permute_rows(rows, order, column):
    row_count = order.shape[0]
    step_rows = min(512, row_count)
    return pl.pallas_call(
        permute_body,
        grid_spec=pltpu.PrefetchScalarGridSpec(
            num_scalar_prefetch=1,
            grid=(row_count // step_rows,),
            in_specs=[
                pl.BlockSpec((row_count // LANES, LANES), lambda i, c: (0, 0)),
                pl.BlockSpec((rows.shape[0], LANES), lambda i, c: (0, c[0])),
            ],
            out_specs=pl.BlockSpec((step_rows, LANES), lambda i, c: (i, 0)),
        ),
        out_shape=jax.ShapeDtypeStruct((row_count, LANES), bf16),
        compiler_params=params(32),
        cost_estimate=cost(2 * row_count * row_count * LANES * 4, 3 * row_count * LANES * 2),
        name="permute_rows",
    )(column, order.reshape(row_count // LANES, LANES), rows)


def bucket_body(shards, capacity, column_ref, shard_ref, point_ref, grads_ref, out_ref, place_ref):
    step = pl.program_id(0)
    row_count = grads_ref.shape[0]
    groups = row_count // LANES

    @pl.when(step == 0)
    def _():
        targets = shard_ref[...]
        masks = [ones_where(targets == t) for t in range(shards)]
        stacked = jnp.concatenate(masks, axis=0)
        above = ones_where(
            lax.broadcasted_iota(i32, (LANES, LANES), 0)
            < lax.broadcasted_iota(i32, (LANES, LANES), 1)
        )
        earlier = ones_where(
            lax.broadcasted_iota(i32, (groups, groups), 1)
            < lax.broadcasted_iota(i32, (groups, groups), 0)
        )
        in_row = dot(stacked, above)
        places = jnp.zeros((groups, LANES), f32)
        for t in range(shards):
            rows_before = jnp.sum(dot(earlier, masks[t]), axis=1, keepdims=True)
            place = in_row[t * groups : (t + 1) * groups] + rows_before + float(t * capacity)
            places = jnp.where(targets == t, place, places)
        place_ref[...] = places.astype(i32)

    slot = lax.broadcasted_iota(i32, (capacity, LANES), 0) + step * capacity
    onehot = jnp.concatenate(
        [ones_where(place_ref[j : j + 1, :] == slot) for j in range(groups)], axis=1
    )
    out_ref[0, :capacity, :] = dot(onehot, grads_ref[...]).astype(bf16)
    points = jnp.concatenate([point_ref[j : j + 1, :] for j in range(groups)], axis=1)
    high = points // INDEX_BASE
    low = points - high * INDEX_BASE
    digits = jnp.concatenate(
        [high.astype(f32), low.astype(f32), jnp.zeros((INDEX_ROWS - 2, row_count), f32)], axis=0
    )
    sent = dot_rows(digits.astype(bf16), onehot)
    chunks = capacity // LANES
    rows = [sent[d : d + 1, j * LANES : (j + 1) * LANES] for d in range(2) for j in range(chunks)]
    rows.append(jnp.zeros((INDEX_ROWS - 2 * chunks, LANES), f32))
    out_ref[0, capacity:, :] = jnp.concatenate(rows, axis=0).astype(bf16)


def bucket_rows(grads, targets, points, column, shards, capacity):
    row_count = grads.shape[0]
    groups = row_count // LANES
    return pl.pallas_call(
        functools.partial(bucket_body, shards, capacity),
        grid_spec=pltpu.PrefetchScalarGridSpec(
            num_scalar_prefetch=1,
            grid=(shards,),
            in_specs=[
                pl.BlockSpec((groups, LANES), lambda i, c: (0, 0)),
                pl.BlockSpec((groups, LANES), lambda i, c: (0, 0)),
                pl.BlockSpec((row_count, LANES), lambda i, c: (0, c[0])),
            ],
            out_specs=pl.BlockSpec((1, capacity + INDEX_ROWS, LANES), lambda i, c: (i, 0, 0)),
            scratch_shapes=[pltpu.VMEM((groups, LANES), i32)],
        ),
        out_shape=jax.ShapeDtypeStruct((shards, capacity + INDEX_ROWS, LANES), bf16),
        compiler_params=params(32),
        cost_estimate=cost(
            8 * shards * capacity * row_count * LANES, 3 * shards * capacity * LANES * 2
        ),
        name="bucket_rows",
    )(column, targets.reshape(groups, LANES), points.reshape(groups, LANES), grads)


def segment_body(got_ref, out_ref, total_ref):
    step = pl.program_id(0)
    capacity = got_ref.shape[1] - INDEX_ROWS
    chunks = capacity // LANES
    row_count = out_ref.shape[0]
    digits = got_ref[0, capacity:, :].astype(f32)
    index = (digits[:chunks] * float(INDEX_BASE) + digits[chunks : 2 * chunks]).astype(i32)
    row = lax.broadcasted_iota(i32, (row_count, LANES), 0)
    onehot = jnp.concatenate([ones_where(index[j : j + 1] == row) for j in range(chunks)], axis=1)
    part = dot(onehot, got_ref[0, :capacity, :])

    @pl.when(step == 0)
    def _():
        total_ref[...] = part

    @pl.when(step > 0)
    def _():
        total_ref[...] += part

    @pl.when(step == pl.num_programs(0) - 1)
    def _():
        out_ref[...] = total_ref[...].astype(bf16)


def segment_rows(got, row_count):
    shards, message, _ = got.shape
    return pl.pallas_call(
        segment_body,
        grid=(shards,),
        in_specs=[pl.BlockSpec((1, message, LANES), lambda i: (i, 0, 0))],
        out_specs=pl.BlockSpec((row_count, LANES), lambda i: (0, 0)),
        out_shape=jax.ShapeDtypeStruct((row_count, LANES), bf16),
        scratch_shapes=[pltpu.VMEM((row_count, LANES), f32)],
        compiler_params=params(32),
        cost_estimate=cost(
            8 * shards * message * row_count * LANES, 3 * shards * message * LANES * 2
        ),
        name="segment_rows",
    )(got)


def project_body(
    column_ref,
    x0_ref,
    x1_ref,
    x2_ref,
    x3_ref,
    weight_ref,
    hidden_ref,
    normed_ref,
    inv_ref,
    key_ref,
    value_ref,
    query_t_ref,
    key_t_ref,
    value_t_ref,
):
    me = column_ref[0]
    blocks = [r[...].astype(f32) for r in (x0_ref, x1_ref, x2_ref, x3_ref)]
    features = float(LANES * len(blocks))
    mean = jnp.sum(blocks[0] + blocks[1] + (blocks[2] + blocks[3]), axis=1, keepdims=True) / features
    centered = [b - mean for b in blocks]
    squares = [c * c for c in centered]
    var = jnp.sum(squares[0] + squares[1] + (squares[2] + squares[3]), axis=1, keepdims=True) / features
    inv = lax.rsqrt(var + epsilon)
    normed_ref[...] = centered[0] * inv
    inv_ref[...] = jnp.broadcast_to(inv, inv_ref.shape)
    for block, mask in zip(centered, (0, 2, 1, 3)):
        at = pl.multiple_of((me ^ mask) * LANES, LANES)
        hidden_ref[:, pl.ds(at, LANES)] = (block * inv).astype(bf16)
    projected = dot(hidden_ref[...], weight_ref[...])
    key_ref[...] = projected[:, LANES : 2 * LANES].astype(bf16)
    value_ref[...] = projected[:, 2 * LANES :].astype(bf16)
    query_t_ref[...] = (projected[:, :LANES] * score_scale).T.astype(bf16)
    key_t_ref[...] = projected[:, LANES : 2 * LANES].T.astype(bf16)
    value_t_ref[...] = projected[:, 2 * LANES :].T.astype(bf16)


def project(blocks, weight, column):
    row_count = blocks[0].shape[0]
    step_rows = 512
    features = weight.shape[0]
    width = pl.BlockSpec((step_rows, LANES), lambda i, c: (i, 0))
    tall = pl.BlockSpec((LANES, step_rows), lambda i, c: (0, i))
    normal = lambda t: jax.ShapeDtypeStruct((row_count, LANES), t)
    turned = jax.ShapeDtypeStruct((LANES, row_count), bf16)
    return pl.pallas_call(
        project_body,
        grid_spec=pltpu.PrefetchScalarGridSpec(
            num_scalar_prefetch=1,
            grid=(row_count // step_rows,),
            in_specs=[width] * 4 + [pl.BlockSpec(weight.shape, lambda i, c: (0, 0))],
            out_specs=[
                pl.BlockSpec((step_rows, features), lambda i, c: (i, 0)),
                width,
                width,
                width,
                width,
                tall,
                tall,
                tall,
            ],
        ),
        out_shape=[
            jax.ShapeDtypeStruct((row_count, features), bf16),
            normal(f32),
            normal(f32),
            normal(bf16),
            normal(bf16),
            turned,
            turned,
            turned,
        ],
        compiler_params=params(32),
        cost_estimate=cost(4 * row_count * features * 3 * LANES, row_count * LANES * 40),
        name="project",
    )(column, *blocks, weight)


def forward_body(key_ref, query_t_ref, value_t_ref, exp_ref, attended_ref, inverse_ref):
    head = pl.program_id(1)
    at = pl.multiple_of(head * HD, HD)
    in_head = lax.broadcasted_iota(i32, (LANES, 1), 0) // HD == head
    query = jnp.where(in_head, query_t_ref[...], jnp.zeros((), bf16))
    scores = dot(key_ref[...], query)
    top = jnp.max(scores, axis=0, keepdims=True)
    weights = jnp.exp2((scores - top) * log2_e).astype(bf16)
    exp_ref[0] = weights
    extended = jnp.concatenate([value_t_ref[pl.ds(at, HD), :], jnp.ones((HD, PATCH), bf16)], axis=0)
    sums = dot(extended, weights)
    inverse = 1.0 / sums[HD : HD + 1]
    inverse_ref[0] = inverse
    attended_ref[pl.ds(at, HD), :] = (sums[:HD] * inverse).astype(bf16)


def attention_forward(keys, query_t, value_t):
    row_count = keys.shape[0]
    patches, heads = row_count // PATCH, LANES // HD
    tall = pl.BlockSpec((LANES, PATCH), lambda p, h: (0, p))
    per_head = lambda p, h: (p * heads + h, 0, 0)
    elements = patches * heads * PATCH * PATCH
    return pl.pallas_call(
        forward_body,
        grid=(patches, heads),
        in_specs=[pl.BlockSpec((PATCH, LANES), lambda p, h: (p, 0)), tall, tall],
        out_specs=[
            pl.BlockSpec((1, PATCH, PATCH), per_head),
            tall,
            pl.BlockSpec((1, 1, PATCH), per_head),
        ],
        out_shape=[
            jax.ShapeDtypeStruct((patches * heads, PATCH, PATCH), bf16),
            jax.ShapeDtypeStruct((LANES, row_count), bf16),
            jax.ShapeDtypeStruct((patches * heads, 1, PATCH), f32),
        ],
        compiler_params=params(48),
        cost_estimate=cost(1024 * elements, 2 * elements, elements),
        name="attention_forward",
    )(keys, query_t, value_t)


def backward_body(
    column_ref,
    exp_ref,
    inverse_ref,
    value_ref,
    query_t_ref,
    key_t_ref,
    attended_ref,
    g0_ref,
    g1_ref,
    g2_ref,
    g3_ref,
    weight_ref,
    d_out_ref,
    d_query_ref,
    d_key_ref,
    d_value_ref,
    d_attended_ref,
    key_sum_ref,
    value_sum_ref,
):
    head = pl.program_id(1)
    at = pl.multiple_of(head * HD, HD)
    in_head = lax.broadcasted_iota(i32, (LANES, 1), 0) // HD == head

    @pl.when(head == 0)
    def _():
        me = column_ref[0]
        for block, mask in zip((g0_ref, g1_ref, g2_ref, g3_ref), (0, 2, 1, 3)):
            start = pl.multiple_of((me ^ mask) * LANES, LANES)
            d_out_ref[:, pl.ds(start, LANES)] = block[...]
        d_attended_ref[...] = dot(d_out_ref[...], weight_ref[...]).T.astype(bf16)
        key_sum_ref[...] = jnp.zeros_like(key_sum_ref)
        value_sum_ref[...] = jnp.zeros_like(value_sum_ref)

    weights = exp_ref[0]
    scaled = jnp.where(in_head, d_attended_ref[...].astype(f32) * inverse_ref[0], 0.0).astype(bf16)
    delta = jnp.sum(
        scaled.astype(f32) * attended_ref[...].astype(f32), axis=0, keepdims=True
    )
    delta_high = delta.astype(bf16)
    delta_low = (delta - delta_high.astype(f32)).astype(bf16)
    left = jnp.concatenate([value_ref[...], jnp.full((PATCH, HD), -1.0, bf16)], axis=1)
    right = jnp.concatenate(
        [scaled, delta_high, delta_low, jnp.zeros((HD - 2, PATCH), bf16)], axis=0
    )
    d_scores = (weights.astype(f32) * dot(left, right)).astype(bf16)
    d_query = dot(key_t_ref[pl.ds(at, HD), :], d_scores)
    d_query_ref[pl.ds(at, HD), :] = (d_query * score_scale).astype(bf16)
    query = jnp.where(in_head, query_t_ref[...], jnp.zeros((), bf16))
    value_sum_ref[...] += dot_rows(weights, scaled)
    key_sum_ref[...] += dot_rows(d_scores, query)

    @pl.when(head == pl.num_programs(1) - 1)
    def _():
        d_key_ref[...] = key_sum_ref[...].astype(bf16)
        d_value_ref[...] = value_sum_ref[...].astype(bf16)


def attention_backward(weights, inverse, values, query_t, key_t, attended, grads, out_weight, column):
    row_count = values.shape[0]
    features = out_weight.shape[0]
    patches, heads = row_count // PATCH, LANES // HD
    tall = pl.BlockSpec((LANES, PATCH), lambda p, h, c: (0, p))
    wide = pl.BlockSpec((PATCH, LANES), lambda p, h, c: (p, 0))
    per_head = lambda p, h, c: (p * heads + h, 0, 0)
    elements = patches * heads * PATCH * PATCH
    return pl.pallas_call(
        backward_body,
        grid_spec=pltpu.PrefetchScalarGridSpec(
            num_scalar_prefetch=1,
            grid=(patches, heads),
            in_specs=[
                pl.BlockSpec((1, PATCH, PATCH), per_head),
                pl.BlockSpec((1, 1, PATCH), per_head),
                wide,
                tall,
                tall,
                tall,
                wide,
                wide,
                wide,
                wide,
                pl.BlockSpec(out_weight.shape, lambda p, h, c: (0, 0)),
            ],
            out_specs=[
                pl.BlockSpec((PATCH, features), lambda p, h, c: (p, 0)),
                tall,
                wide,
                wide,
            ],
            scratch_shapes=[
                pltpu.VMEM((LANES, PATCH), bf16),
                pltpu.VMEM((PATCH, LANES), f32),
                pltpu.VMEM((PATCH, LANES), f32),
            ],
        ),
        out_shape=[
            jax.ShapeDtypeStruct((row_count, features), bf16),
            jax.ShapeDtypeStruct((LANES, row_count), bf16),
            jax.ShapeDtypeStruct((row_count, LANES), bf16),
            jax.ShapeDtypeStruct((row_count, LANES), bf16),
        ],
        compiler_params=params(52),
        cost_estimate=cost(2048 * elements, 2 * elements),
        name="attention_backward",
    )(column, weights, inverse, values, query_t, key_t, attended, *grads, out_weight)


def weight_grad_body(d_query_ref, d_key_ref, d_value_ref, attended_ref, hidden_ref, d_out_ref, out_ref):
    hidden = hidden_ref[...]
    out_ref[:, :LANES] = dot(d_query_ref[...], hidden).T.astype(bf16)
    out_ref[:, LANES : 2 * LANES] = dot(d_key_ref[...].T, hidden).T.astype(bf16)
    out_ref[:, 2 * LANES : 3 * LANES] = dot(d_value_ref[...].T, hidden).T.astype(bf16)
    out_ref[:, 3 * LANES :] = dot(attended_ref[...], d_out_ref[...]).T.astype(bf16)


def weight_grads(d_query_t, d_keys, d_values, attended, hidden, d_out):
    row_count, features = hidden.shape
    return pl.pallas_call(
        weight_grad_body,
        out_shape=jax.ShapeDtypeStruct((features, 4 * LANES), bf16),
        compiler_params=params(48),
        cost_estimate=cost(8 * row_count * features * LANES, 8 * row_count * features),
        name="weight_grads",
    )(d_query_t, d_keys, d_values, attended, hidden, d_out)


def partial_body(column_ref, d_query_ref, d_key_ref, d_value_ref, weight_ref, hidden_ref, mine_ref, other_ref, sums_ref):
    me = column_ref[0]
    d_projected = jnp.concatenate([d_query_ref[...].T, d_key_ref[...], d_value_ref[...]], axis=1)
    part = dot_rows(d_projected, weight_ref[...]).astype(bf16)
    crossed = part.astype(f32) * hidden_ref[...].astype(f32)
    high = crossed.astype(bf16)
    low = (crossed - high.astype(f32)).astype(bf16)
    ones = jnp.ones((8, part.shape[1]), bf16)
    sums_ref[0:1, :] = dot_rows(ones, part)[0:1]
    sums_ref[1:2, :] = (dot_rows(ones, high) + dot_rows(ones, low))[0:1]
    odd = me % 2
    for j in range(4):
        block = part[:, j * LANES : (j + 1) * LANES]

        @pl.when(odd == j % 2)
        def _():
            mine_ref[:, (j // 2) * LANES : (j // 2 + 1) * LANES] = block

        @pl.when(odd != j % 2)
        def _():
            other_ref[:, (j // 2) * LANES : (j // 2 + 1) * LANES] = block


def hidden_part(d_query_t, d_keys, d_values, weight, hidden, column):
    row_count, features = hidden.shape
    step_rows = 512
    wide = pl.BlockSpec((step_rows, LANES), lambda i, c: (i, 0))
    half = pl.BlockSpec((step_rows, 2 * LANES), lambda i, c: (i, 0))
    halves = jax.ShapeDtypeStruct((row_count, 2 * LANES), bf16)
    return pl.pallas_call(
        partial_body,
        grid_spec=pltpu.PrefetchScalarGridSpec(
            num_scalar_prefetch=1,
            grid=(row_count // step_rows,),
            in_specs=[
                pl.BlockSpec((LANES, step_rows), lambda i, c: (0, i)),
                wide,
                wide,
                pl.BlockSpec(weight.shape, lambda i, c: (0, 0)),
                pl.BlockSpec((step_rows, features), lambda i, c: (i, 0)),
            ],
            out_specs=[half, half, pl.BlockSpec((2, step_rows), lambda i, c: (0, i))],
        ),
        out_shape=[halves, halves, jax.ShapeDtypeStruct((2, row_count), f32)],
        compiler_params=params(32),
        cost_estimate=cost(8 * row_count * features * LANES, 8 * row_count * features),
        name="hidden_part",
    )(column, d_query_t, d_keys, d_values, weight, hidden)


def local(
    scan_points,
    send_order,
    arrive_order,
    qkv_weight,
    out_weight,
    voxel_grads,
    voxel_shard,
    voxel_point,
):
    shards = lax.axis_size("seq")
    members = lax.axis_size("mp")
    local_rows, features = scan_points.shape
    voxels = voxel_grads.shape[0]
    capacity = 2 * voxels // shards
    me = lax.axis_index("mp")
    column = me.astype(i32).reshape(1)
    zero = jnp.zeros((1,), i32)
    weight = qkv_weight.reshape(features, 3 * LANES)

    def swap(rows, mask):
        return lax.ppermute(rows, "mp", [(i, i ^ mask) for i in range(members)])

    def exchange(rows):
        return lax.all_to_all(rows, "seq", split_axis=0, concat_axis=0, tiled=True)

    def all_columns(rows):
        across = swap(rows, 2)
        return (rows, across, swap(rows, 1), swap(across, 1))

    arrived = exchange(permute_rows(scan_points, send_order, column))
    buckets = bucket_rows(voxel_grads, voxel_shard, voxel_point, column, shards, capacity)
    got = exchange(buckets.reshape(shards * (capacity + INDEX_ROWS), LANES))
    got = got.reshape(shards, capacity + INDEX_ROWS, LANES)
    points = all_columns(permute_rows(arrived, arrive_order, zero))
    hidden, normed, inv_scale, keys, values, query_t, key_t, value_t = project(points, weight, column)
    weights, attended, inverse = attention_forward(keys, query_t, value_t)
    grads = all_columns(segment_rows(got, local_rows))
    d_out, d_query_t, d_keys, d_values = attention_backward(
        weights, inverse, values, query_t, key_t, attended, grads, out_weight, column
    )
    mine, other, sums = hidden_part(d_query_t, d_keys, d_values, weight, hidden, column)
    weight_parts = weight_grads(d_query_t, d_keys, d_values, attended, hidden, d_out)
    summed = jnp.sum(
        exchange(weight_parts).reshape(shards, features // shards, 4 * LANES).astype(f32), axis=0
    )
    grad_qkv = summed[:, : 3 * LANES].reshape(features // shards, 3, LANES)
    grad_out = summed[:, 3 * LANES :]

    pair = mine.astype(f32) + swap(other, 1).astype(f32)
    sums = sums + swap(sums, 1)
    top = me // 2 == 1
    low_half, high_half = pair[:, :LANES], pair[:, LANES:]
    kept = jnp.where(top, high_half, low_half)
    sent = jnp.where(top, low_half, high_half).astype(bf16)
    d_hidden = kept + swap(sent, 2).astype(f32)
    sums = (sums + swap(sums, 2)) / float(features)
    d_points = grads[0].astype(f32) + inv_scale * (
        d_hidden - sums[0][:, None] - normed * sums[1][:, None]
    )
    return (d_points, grad_qkv, grad_out)


def solution(mesh):
    in_specs = (
        P("seq", None),
        P("seq"),
        P("seq"),
        P(None, None, "mp"),
        P(None, "mp"),
        P("seq", None),
        P("seq", None),
        P("seq"),
    )
    out_specs = (P("seq", "mp"), P("seq", None, "mp"), P("seq", "mp"))
    return jax.shard_map(local, mesh=mesh, in_specs=in_specs, out_specs=out_specs, check_vma=False)
```

```python
import functools

import jax
import jax.numpy as jnp
from jax import lax
from jax.experimental import pallas as pl
from jax.experimental.pallas import tpu as pltpu
from jax.sharding import PartitionSpec as P

HD = 16
PATCH = 1024
LANES = 128
INDEX_ROWS = 16
INDEX_BASE = 64
BLOCK_MASKS = (0, 2, 1, 3)
SAFE_SCORE = 60.0

score_scale = 0.25
epsilon = 1e-05
log2_e = 1.4426950408889634

f32 = jnp.float32
bf16 = jnp.bfloat16
i32 = jnp.int32

ROWS_BY_ROWS = (((1,), (1,)), ((), ()))


def params(mib):
    return pltpu.CompilerParams(vmem_limit_bytes=mib << 20)


def cost(flops, bytes_accessed, transcendentals=0):
    return pl.CostEstimate(
        flops=int(flops), bytes_accessed=int(bytes_accessed), transcendentals=int(transcendentals)
    )


def dot(a, b):
    return jnp.dot(a, b, preferred_element_type=f32)


def dot_rows(a, b):
    return lax.dot_general(a, b, ROWS_BY_ROWS, preferred_element_type=f32)


def ones_where(mask):
    return jnp.where(mask, 1.0, 0.0).astype(bf16)


def permute_body(column_ref, order_ref, block_ref, out_ref):
    step = pl.program_id(0)
    source_rows = block_ref.shape[0]
    chunks = out_ref.shape[0] // LANES
    lane = lax.broadcasted_iota(i32, (LANES, LANES), 1)
    block = block_ref[...]
    for j in range(chunks):
        wanted = order_ref[pl.ds(step * chunks + j, 1), :].astype(f32)
        wanted = jnp.broadcast_to(wanted, (LANES, LANES)).T.astype(i32)
        onehot = jnp.concatenate(
            [ones_where(wanted == lane + k * LANES) for k in range(source_rows // LANES)], axis=1
        )
        out_ref[j * LANES : (j + 1) * LANES, :] = dot(onehot, block).astype(bf16)


def permute_rows(rows, order, column):
    row_count = order.shape[0]
    step_rows = min(512, row_count)
    return pl.pallas_call(
        permute_body,
        grid_spec=pltpu.PrefetchScalarGridSpec(
            num_scalar_prefetch=1,
            grid=(row_count // step_rows,),
            in_specs=[
                pl.BlockSpec((row_count // LANES, LANES), lambda i, c: (0, 0)),
                pl.BlockSpec((rows.shape[0], LANES), lambda i, c: (0, c[0])),
            ],
            out_specs=pl.BlockSpec((step_rows, LANES), lambda i, c: (i, 0)),
        ),
        out_shape=jax.ShapeDtypeStruct((row_count, LANES), bf16),
        compiler_params=params(32),
        cost_estimate=cost(2 * row_count * row_count * LANES * 4, 3 * row_count * LANES * 2),
        name="permute_rows",
    )(column, order.reshape(row_count // LANES, LANES), rows)


def bucket_body(shards, capacity, column_ref, shard_ref, point_ref, grads_ref, out_ref, place_ref):
    step = pl.program_id(0)
    row_count = grads_ref.shape[0]
    groups = row_count // LANES

    @pl.when(step == 0)
    def _():
        targets = shard_ref[...]
        masks = [ones_where(targets == t) for t in range(shards)]
        stacked = jnp.concatenate(masks, axis=0)
        above = ones_where(
            lax.broadcasted_iota(i32, (LANES, LANES), 0)
            < lax.broadcasted_iota(i32, (LANES, LANES), 1)
        )
        earlier = ones_where(
            lax.broadcasted_iota(i32, (groups, groups), 1)
            < lax.broadcasted_iota(i32, (groups, groups), 0)
        )
        in_row = dot(stacked, above)
        places = jnp.zeros((groups, LANES), f32)
        for t in range(shards):
            rows_before = jnp.sum(dot(earlier, masks[t]), axis=1, keepdims=True)
            place = in_row[t * groups : (t + 1) * groups] + rows_before + float(t * capacity)
            places = jnp.where(targets == t, place, places)
        place_ref[...] = places.astype(i32)

    slot = lax.broadcasted_iota(i32, (capacity, LANES), 0) + step * capacity
    onehot = jnp.concatenate(
        [ones_where(place_ref[j : j + 1, :] == slot) for j in range(groups)], axis=1
    )
    out_ref[0, :capacity, :] = dot(onehot, grads_ref[...]).astype(bf16)
    points = jnp.concatenate([point_ref[j : j + 1, :] for j in range(groups)], axis=1)
    high = points // INDEX_BASE
    low = points - high * INDEX_BASE
    digits = jnp.concatenate(
        [high.astype(f32), low.astype(f32), jnp.zeros((INDEX_ROWS - 2, row_count), f32)], axis=0
    )
    sent = dot_rows(digits.astype(bf16), onehot)
    chunks = capacity // LANES
    rows = [sent[d : d + 1, j * LANES : (j + 1) * LANES] for d in range(2) for j in range(chunks)]
    rows.append(jnp.zeros((INDEX_ROWS - 2 * chunks, LANES), f32))
    out_ref[0, capacity:, :] = jnp.concatenate(rows, axis=0).astype(bf16)


def bucket_rows(grads, targets, points, column, shards, capacity):
    row_count = grads.shape[0]
    groups = row_count // LANES
    return pl.pallas_call(
        functools.partial(bucket_body, shards, capacity),
        grid_spec=pltpu.PrefetchScalarGridSpec(
            num_scalar_prefetch=1,
            grid=(shards,),
            in_specs=[
                pl.BlockSpec((groups, LANES), lambda i, c: (0, 0)),
                pl.BlockSpec((groups, LANES), lambda i, c: (0, 0)),
                pl.BlockSpec((row_count, LANES), lambda i, c: (0, c[0])),
            ],
            out_specs=pl.BlockSpec((1, capacity + INDEX_ROWS, LANES), lambda i, c: (i, 0, 0)),
            scratch_shapes=[pltpu.VMEM((groups, LANES), i32)],
        ),
        out_shape=jax.ShapeDtypeStruct((shards, capacity + INDEX_ROWS, LANES), bf16),
        compiler_params=params(32),
        cost_estimate=cost(
            8 * shards * capacity * row_count * LANES, 3 * shards * capacity * LANES * 2
        ),
        name="bucket_rows",
    )(column, targets.reshape(groups, LANES), points.reshape(groups, LANES), grads)


def segment_body(got_ref, out_ref, total_ref):
    step = pl.program_id(0)
    capacity = got_ref.shape[1] - INDEX_ROWS
    chunks = capacity // LANES
    row_count = total_ref.shape[0]
    digits = got_ref[0, capacity:, :].astype(f32)
    index = (digits[:chunks] * float(INDEX_BASE) + digits[chunks : 2 * chunks]).astype(i32)
    row = lax.broadcasted_iota(i32, (row_count, LANES), 0)
    onehot = jnp.concatenate([ones_where(index[j : j + 1] == row) for j in range(chunks)], axis=1)
    part = dot(onehot, got_ref[0, :capacity, :])

    @pl.when(step == 0)
    def _():
        total_ref[...] = part

    @pl.when(step > 0)
    def _():
        total_ref[...] += part

    @pl.when(step == pl.num_programs(0) - 1)
    def _():
        out_ref[...] = total_ref[...].T.astype(bf16)


def segment_rows(got, row_count):
    shards, message, _ = got.shape
    return pl.pallas_call(
        segment_body,
        grid=(shards,),
        in_specs=[pl.BlockSpec((1, message, LANES), lambda i: (i, 0, 0))],
        out_specs=pl.BlockSpec((LANES, row_count), lambda i: (0, 0)),
        out_shape=jax.ShapeDtypeStruct((LANES, row_count), bf16),
        scratch_shapes=[pltpu.VMEM((row_count, LANES), f32)],
        compiler_params=params(32),
        cost_estimate=cost(
            8 * shards * message * row_count * LANES, 3 * shards * message * LANES * 2
        ),
        name="segment_rows",
    )(got)


def project_body(
    column_ref,
    x0_ref,
    x1_ref,
    x2_ref,
    x3_ref,
    weight_ref,
    hidden_ref,
    normed_ref,
    inv_ref,
    key_ref,
    base2_t_ref,
    query_t_ref,
    key_t_ref,
    value_t_ref,
):
    me = column_ref[0]
    blocks = [r[...].astype(f32) for r in (x0_ref, x1_ref, x2_ref, x3_ref)]
    features = float(LANES * len(blocks))
    mean = jnp.sum(blocks[0] + blocks[1] + (blocks[2] + blocks[3]), axis=1, keepdims=True) / features
    centered = [b - mean for b in blocks]
    squares = [c * c for c in centered]
    var = jnp.sum(squares[0] + squares[1] + (squares[2] + squares[3]), axis=1, keepdims=True) / features
    inv = lax.rsqrt(var + epsilon)
    normed_ref[...] = centered[0] * inv
    inv_ref[...] = jnp.broadcast_to(inv, inv_ref.shape)
    for block, mask in zip(centered, BLOCK_MASKS):
        at = pl.multiple_of((me ^ mask) * LANES, LANES)
        hidden_ref[:, pl.ds(at, LANES)] = (block * inv).astype(bf16)
    projected = dot(hidden_ref[...], weight_ref[...]).astype(bf16)
    key_ref[...] = projected[:, LANES : 2 * LANES]
    query = projected[:, :LANES].astype(f32).T * score_scale
    query_t_ref[...] = query.astype(bf16)
    base2_t_ref[...] = (query * log2_e).astype(bf16)
    key_t_ref[...] = projected[:, LANES : 2 * LANES].astype(f32).T.astype(bf16)
    value_t_ref[...] = projected[:, 2 * LANES :].astype(f32).T.astype(bf16)


def project(blocks, weight, column):
    row_count = blocks[0].shape[0]
    step_rows = 512
    features = weight.shape[0]
    width = pl.BlockSpec((step_rows, LANES), lambda i, c: (i, 0))
    tall = pl.BlockSpec((LANES, step_rows), lambda i, c: (0, i))
    normal = lambda t: jax.ShapeDtypeStruct((row_count, LANES), t)
    turned = jax.ShapeDtypeStruct((LANES, row_count), bf16)
    return pl.pallas_call(
        project_body,
        grid_spec=pltpu.PrefetchScalarGridSpec(
            num_scalar_prefetch=1,
            grid=(row_count // step_rows,),
            in_specs=[width] * 4 + [pl.BlockSpec(weight.shape, lambda i, c: (0, 0))],
            out_specs=[pl.BlockSpec((step_rows, features), lambda i, c: (i, 0))]
            + [width] * 3
            + [tall] * 4,
        ),
        out_shape=[jax.ShapeDtypeStruct((row_count, features), bf16)]
        + [normal(f32), normal(f32), normal(bf16)]
        + [turned] * 4,
        compiler_params=params(32),
        cost_estimate=cost(4 * row_count * features * 3 * LANES, row_count * LANES * 40),
        name="project",
    )(column, *blocks, weight)


def forward_body(
    key_ref,
    base2_t_ref,
    key_t_ref,
    value_t_ref,
    exp_ref,
    attended_ref,
    inverse_ref,
    covariance_ref,
    safe_ref,
):
    head = pl.program_id(0)
    at = pl.multiple_of(head * HD, HD)

    @pl.when(head == 0)
    def _():
        def largest(ref):
            squares = jnp.square(ref[...].astype(f32)).reshape(LANES // HD, HD, PATCH)
            return jnp.max(jnp.sum(squares, axis=1), axis=1, keepdims=True)

        bound = jnp.max(largest(base2_t_ref) * largest(key_t_ref))
        safe_ref[0] = (bound <= SAFE_SCORE * SAFE_SCORE).astype(i32)

    def attend(shifted):
        in_head = lax.broadcasted_iota(i32, (LANES, 1), 0) // HD == head
        query = jnp.where(in_head, base2_t_ref[...], jnp.zeros((), bf16))
        scores = dot(key_ref[...], query)
        if shifted:
            scores = scores - jnp.max(scores, axis=0, keepdims=True)
        weights = jnp.exp2(scores).astype(bf16)
        exp_ref[0] = weights
        keys = key_t_ref[pl.ds(at, HD), :].astype(f32)
        values = value_t_ref[pl.ds(at, HD), :].astype(f32)
        middle = jnp.mean(values, axis=1, keepdims=True)
        centered = values - middle
        features = [centered[j : j + 1] * keys for j in range(HD)]
        features += [keys, values, jnp.ones((HD, PATCH), f32)]
        sums = dot(jnp.concatenate([f.astype(bf16) for f in features], axis=0), weights)
        inverse = 1.0 / sums[(HD + 2) * HD : (HD + 2) * HD + 1]
        inverse_ref[0] = inverse
        mean_key = sums[HD * HD : (HD + 1) * HD] * inverse
        mean_value = sums[(HD + 1) * HD : (HD + 2) * HD] * inverse
        attended_ref[pl.ds(at, HD), :] = mean_value.astype(bf16)
        offset = mean_value - middle
        for j in range(HD):
            crossed = sums[j * HD : (j + 1) * HD] * inverse - offset[j : j + 1] * mean_key
            covariance_ref[0, j * HD : (j + 1) * HD, :] = crossed.astype(bf16)

    @pl.when(safe_ref[0] == 1)
    def _():
        attend(False)

    @pl.when(safe_ref[0] == 0)
    def _():
        attend(True)


def attention_forward(keys, base2_t, key_t, value_t):
    heads = LANES // HD
    tall = pl.BlockSpec((LANES, PATCH), lambda h: (0, 0))
    per_head = lambda h: (h, 0, 0)
    elements = heads * PATCH * PATCH
    return pl.pallas_call(
        forward_body,
        grid=(heads,),
        in_specs=[pl.BlockSpec((PATCH, LANES), lambda h: (0, 0)), tall, tall, tall],
        out_specs=[
            pl.BlockSpec((1, PATCH, PATCH), per_head),
            tall,
            pl.BlockSpec((1, 1, PATCH), per_head),
            pl.BlockSpec((1, HD * HD, PATCH), per_head),
        ],
        out_shape=[
            jax.ShapeDtypeStruct((heads, PATCH, PATCH), bf16),
            jax.ShapeDtypeStruct((LANES, PATCH), bf16),
            jax.ShapeDtypeStruct((heads, 1, PATCH), f32),
            jax.ShapeDtypeStruct((heads, HD * HD, PATCH), bf16),
        ],
        scratch_shapes=[pltpu.SMEM((1,), i32)],
        compiler_params=params(48),
        cost_estimate=cost(1600 * elements, 2 * elements, elements),
        name="attention_forward",
    )(keys, base2_t, key_t, value_t)


def backward_body(
    column_ref,
    exp_ref,
    inverse_ref,
    covariance_ref,
    query_t_ref,
    value_t_ref,
    attended_ref,
    g0_ref,
    g1_ref,
    g2_ref,
    g3_ref,
    weight_t_ref,
    d_out_ref,
    d_query_ref,
    d_key_ref,
    d_value_ref,
    d_attended_ref,
):
    head = pl.program_id(0)
    at = pl.multiple_of(head * HD, HD)

    @pl.when(head == 0)
    def _():
        me = column_ref[0]
        for block, mask in zip((g0_ref, g1_ref, g2_ref, g3_ref), BLOCK_MASKS):
            start = pl.multiple_of((me ^ mask) * LANES, LANES)
            d_out_ref[pl.ds(start, LANES), :] = block[...]
        d_attended_ref[...] = dot(weight_t_ref[...], d_out_ref[...]).astype(bf16)

    grads = d_attended_ref[pl.ds(at, HD), :].astype(f32)
    query = query_t_ref[pl.ds(at, HD), :].astype(f32)
    values = value_t_ref[pl.ds(at, HD), :].astype(f32)
    inverse = inverse_ref[0]
    middle = jnp.mean(values, axis=1, keepdims=True)
    centered = values - middle
    offset = attended_ref[pl.ds(at, HD), :].astype(f32) - middle
    scaled = grads * inverse
    delta = jnp.sum(scaled * offset, axis=0, keepdims=True)
    features = [scaled[j : j + 1] * query for j in range(HD)] + [delta * query, scaled]
    sums = dot_rows(jnp.concatenate([f.astype(bf16) for f in features], axis=0), exp_ref[0])
    d_value_ref[pl.ds(at, HD), :] = sums[(HD + 1) * HD :].astype(bf16)
    d_key = centered[0:1] * sums[:HD]
    d_query = grads[0:1] * covariance_ref[0, :HD, :].astype(f32)
    for j in range(1, HD):
        rows = slice(j * HD, (j + 1) * HD)
        d_key += centered[j : j + 1] * sums[rows]
        d_query += grads[j : j + 1] * covariance_ref[0, rows, :].astype(f32)
    d_key_ref[pl.ds(at, HD), :] = (d_key - sums[HD * HD : (HD + 1) * HD]).astype(bf16)
    d_query_ref[pl.ds(at, HD), :] = (d_query * score_scale).astype(bf16)


def attention_backward(patch, weights, inverse, covariance, query_t, value_t, attended, grads, weight_t, column):
    features = weight_t.shape[1]
    heads = LANES // HD
    tall = pl.BlockSpec((LANES, PATCH), lambda h, c: (0, 0))
    part = pl.BlockSpec((LANES, PATCH), lambda h, c: (0, patch))
    per_head = lambda h, c: (h, 0, 0)
    elements = heads * PATCH * PATCH
    turned = jax.ShapeDtypeStruct((LANES, PATCH), bf16)
    return pl.pallas_call(
        backward_body,
        grid_spec=pltpu.PrefetchScalarGridSpec(
            num_scalar_prefetch=1,
            grid=(heads,),
            in_specs=[
                pl.BlockSpec((1, PATCH, PATCH), per_head),
                pl.BlockSpec((1, 1, PATCH), per_head),
                pl.BlockSpec((1, HD * HD, PATCH), per_head),
                tall,
                tall,
                tall,
                part,
                part,
                part,
                part,
                pl.BlockSpec(weight_t.shape, lambda h, c: (0, 0)),
            ],
            out_specs=[pl.BlockSpec((features, PATCH), lambda h, c: (0, 0)), tall, tall, tall],
            scratch_shapes=[pltpu.VMEM((LANES, PATCH), bf16)],
        ),
        out_shape=[jax.ShapeDtypeStruct((features, PATCH), bf16), turned, turned, turned],
        compiler_params=params(48),
        cost_estimate=cost(1100 * elements, 2 * elements),
        name="attention_backward",
    )(column, weights, inverse, covariance, query_t, value_t, attended, *grads, weight_t)


def whole(shape, dtype):
    return jax.ShapeDtypeStruct(shape, dtype)


def weight_grad_body(*refs):
    *ins, out_ref = refs
    patches = [ins[:6], ins[6:]]
    for t in range(3):
        total = dot(patches[0][t][...], patches[0][4][...]) + dot(patches[1][t][...], patches[1][4][...])
        out_ref[:, t * LANES : (t + 1) * LANES] = total.T.astype(bf16)
    total = dot_rows(patches[0][3][...], patches[0][5][...]) + dot_rows(
        patches[1][3][...], patches[1][5][...]
    )
    out_ref[:, 3 * LANES :] = total.T.astype(bf16)


def weight_grads(patches):
    features = patches[0][4].shape[1]
    work = 2 * PATCH * features * LANES
    return pl.pallas_call(
        weight_grad_body,
        out_shape=whole((features, 4 * LANES), bf16),
        compiler_params=params(48),
        cost_estimate=cost(8 * work, 12 * PATCH * features),
        name="weight_grads",
    )(*patches[0], *patches[1])


def split_sums(sums):
    high = sums.astype(bf16)
    low = (sums - high.astype(f32)).astype(bf16)
    pad = jnp.zeros((INDEX_ROWS - 2 * sums.shape[0], sums.shape[1]), f32)
    return jnp.concatenate([high.astype(f32), low.astype(f32), pad], axis=0).astype(bf16)


def join_sums(rows):
    rows = rows.astype(f32)
    return rows[0:2] + rows[2:4]


def partial_body(
    column_ref,
    d_query_ref,
    d_key_ref,
    d_value_ref,
    query_ref,
    key_ref,
    value_ref,
    weight_ref,
    mine_ref,
    other_ref,
    sums_ref,
):
    me = column_ref[0]
    d_projected = jnp.concatenate([d_query_ref[...], d_key_ref[...], d_value_ref[...]], axis=0)
    plain = jnp.zeros((1, PATCH), f32)
    for j, mask in enumerate(BLOCK_MASKS):
        start = pl.multiple_of((me ^ mask) * LANES, LANES)
        block = dot(weight_ref[pl.ds(start, LANES), :], d_projected).astype(bf16)
        plain += jnp.sum(block.astype(f32), axis=0, keepdims=True)
        to = mine_ref if j < 2 else other_ref
        to[(j % 2) * LANES : (j % 2 + 1) * LANES, :] = block
    crossed = (
        d_query_ref[...].astype(f32) * (query_ref[...].astype(f32) / score_scale)
        + d_key_ref[...].astype(f32) * key_ref[...].astype(f32)
        + d_value_ref[...].astype(f32) * value_ref[...].astype(f32)
    )
    sums = jnp.concatenate([plain, jnp.sum(crossed, axis=0, keepdims=True)], axis=0)
    sums_ref[...] = sums
    other_ref[2 * LANES :, :] = split_sums(sums)


def hidden_part(d_query, d_key, d_value, query, key, value, weight, column):
    features = weight.shape[0]
    return pl.pallas_call(
        partial_body,
        in_specs=[pl.BlockSpec(memory_space=pltpu.SMEM)] + [pl.BlockSpec(memory_space=pltpu.VMEM)] * 7,
        out_shape=[
            whole((2 * LANES, PATCH), bf16),
            whole((2 * LANES + INDEX_ROWS, PATCH), bf16),
            whole((2, PATCH), f32),
        ],
        compiler_params=params(32),
        cost_estimate=cost(6 * PATCH * features * LANES, 4 * PATCH * features),
        name="hidden_part",
    )(column, d_query, d_key, d_value, query, key, value, weight)


def pair_body(mine_ref, sums_ref, got_ref, kept_ref, sums_out_ref, sent_ref):
    pair = mine_ref[...].astype(f32) + got_ref[: 2 * LANES, :].astype(f32)
    sums = sums_ref[...] + join_sums(got_ref[2 * LANES :, :])
    kept_ref[...] = pair[:LANES]
    sums_out_ref[...] = sums
    sent_ref[:LANES, :] = pair[LANES:].astype(bf16)
    sent_ref[LANES:, :] = split_sums(sums)


def pair_sum(mine, sums, got):
    return pl.pallas_call(
        pair_body,
        out_shape=[
            whole((LANES, PATCH), f32),
            whole((2, PATCH), f32),
            whole((LANES + INDEX_ROWS, PATCH), bf16),
        ],
        compiler_params=params(32),
        cost_estimate=cost(4 * LANES * PATCH, 16 * LANES * PATCH),
        name="pair_sum",
    )(mine, sums, got)


def points_body(kept_ref, sums_ref, got_ref, d_out_ref, normed_ref, inv_ref, *rest):
    out_ref = rest[-1]
    features = 4.0 * LANES
    means = (sums_ref[...] + join_sums(got_ref[LANES:, :])) / features
    d_hidden = kept_ref[...] + got_ref[:LANES, :].astype(f32) - means[0:1]
    cross = jnp.broadcast_to(means[1:2], (LANES, PATCH)).T
    inner = d_hidden.T - normed_ref[...] * cross
    out_ref[...] = d_out_ref[...].astype(f32).T + inv_ref[...] * inner


def points_grad(patch, patches, kept, sums, got, d_out, normed, inv_scale, before):
    full = lambda a: pl.BlockSpec(a.shape, lambda i: (0, 0))
    in_specs = [full(kept), full(sums), full(got), pl.BlockSpec((LANES, PATCH), lambda i: (0, patch))]
    in_specs += [full(normed), full(inv_scale)]
    operands = [kept, sums, got, d_out, normed, inv_scale]
    if before is not None:
        in_specs.append(pl.BlockSpec(memory_space=pl.ANY))
        operands.append(before)
    return pl.pallas_call(
        points_body,
        grid=(1,),
        in_specs=in_specs,
        out_specs=pl.BlockSpec((PATCH, LANES), lambda i: (patch, 0)),
        out_shape=whole((patches * PATCH, LANES), f32),
        input_output_aliases={} if before is None else {len(operands) - 1: 0},
        compiler_params=params(32),
        cost_estimate=cost(8 * LANES * PATCH, 24 * LANES * PATCH),
        name="points_grad",
    )(*operands)


def local(
    scan_points,
    send_order,
    arrive_order,
    qkv_weight,
    out_weight,
    voxel_grads,
    voxel_shard,
    voxel_point,
):
    shards = lax.axis_size("seq")
    members = lax.axis_size("mp")
    local_rows, features = scan_points.shape
    voxels = voxel_grads.shape[0]
    capacity = 2 * voxels // shards
    patches = local_rows // PATCH
    column = lax.axis_index("mp").astype(i32).reshape(1)
    zero = jnp.zeros((1,), i32)
    weight = qkv_weight.reshape(features, 3 * LANES)
    weight_t = out_weight.T

    def swap(rows, mask):
        return lax.ppermute(rows, "mp", [(i, i ^ mask) for i in range(members)])

    def exchange(rows):
        return lax.all_to_all(rows, "seq", split_axis=0, concat_axis=0, tiled=True)

    def all_columns(rows):
        across = swap(rows, 2)
        return (rows, across, swap(rows, 1), swap(across, 1))

    arrived = exchange(permute_rows(scan_points, send_order, column))
    buckets = bucket_rows(voxel_grads, voxel_shard, voxel_point, column, shards, capacity)
    got = exchange(buckets.reshape(shards * (capacity + INDEX_ROWS), LANES))
    projected, forwards = [], []
    for p in range(patches):
        own = permute_rows(arrived, arrive_order[p * PATCH : (p + 1) * PATCH], zero)
        projected.append(project(all_columns(own), weight, column))
    forwards.append(attention_forward(projected[0][3], projected[0][4], *projected[0][6:]))
    got, forwards[0] = lax.optimization_barrier((got, forwards[0]))
    summed_rows = segment_rows(got.reshape(shards, capacity + INDEX_ROWS, LANES), local_rows)
    projected[1], summed_rows = lax.optimization_barrier((projected[1], summed_rows))
    grads = all_columns(summed_rows)
    forwards.append(attention_forward(projected[1][3], projected[1][4], *projected[1][6:]))

    d_points = None
    grad_parts = []
    for p in range(patches):
        hidden, normed, inv_scale, _, _, query_t, key_t, value_t = projected[p]
        weights, attended, inverse, covariance = forwards[p]
        d_out, d_query, d_key, d_value = attention_backward(
            p, weights, inverse, covariance, query_t, value_t, attended, grads, weight_t, column
        )
        grad_parts.append((d_query, d_key, d_value, attended, hidden, d_out))
        mine, other, sums = hidden_part(d_query, d_key, d_value, query_t, key_t, value_t, weight, column)
        kept, sums, sent = pair_sum(mine, sums, swap(other, 1))
        d_points = points_grad(
            p, patches, kept, sums, swap(sent, 2), grads[0], normed, inv_scale, d_points
        )
    parts = exchange(weight_grads(grad_parts)).reshape(shards, features // shards, 4 * LANES)
    summed = jnp.sum(parts.astype(f32), axis=0)
    grad_qkv = summed[:, : 3 * LANES].reshape(features // shards, 3, LANES)
    grad_out = summed[:, 3 * LANES :]
    return (d_points, grad_qkv, grad_out)


def solution(mesh):
    in_specs = (
        P("seq", None),
        P("seq"),
        P("seq"),
        P(None, None, "mp"),
        P(None, "mp"),
        P("seq", None),
        P("seq", None),
        P("seq"),
    )
    out_specs = (P("seq", "mp"), P("seq", None, "mp"), P("seq", "mp"))
    return jax.shard_map(local, mesh=mesh, in_specs=in_specs, out_specs=out_specs, check_vma=False)
```

```python
import functools

import jax
import jax.numpy as jnp
from jax import lax
from jax.experimental import pallas as pl
from jax.experimental.pallas import tpu as pltpu
from jax.sharding import PartitionSpec as P

HD = 16
PATCH = 1024
LANES = 128
INDEX_ROWS = 16
INDEX_BASE = 64
BLOCK_MASKS = (0, 2, 1, 3)
SAFE_SCORE = 60.0

score_scale = 0.25
epsilon = 1e-05
log2_e = 1.4426950408889634

f32 = jnp.float32
bf16 = jnp.bfloat16
i32 = jnp.int32

ROWS_BY_ROWS = (((1,), (1,)), ((), ()))


def params(mib):
    return pltpu.CompilerParams(vmem_limit_bytes=mib << 20)


def cost(flops, bytes_accessed, transcendentals=0):
    return pl.CostEstimate(
        flops=int(flops), bytes_accessed=int(bytes_accessed), transcendentals=int(transcendentals)
    )


def dot(a, b):
    return jnp.dot(a, b, preferred_element_type=f32)


def dot_rows(a, b):
    return lax.dot_general(a, b, ROWS_BY_ROWS, preferred_element_type=f32)


def ones_where(mask):
    return jnp.where(mask, 1.0, 0.0).astype(bf16)


def permute_body(column_ref, order_ref, block_ref, out_ref):
    step = pl.program_id(0)
    source_rows = block_ref.shape[0]
    chunks = out_ref.shape[0] // LANES
    lane = lax.broadcasted_iota(i32, (LANES, LANES), 1)
    block = block_ref[...]
    for j in range(chunks):
        wanted = order_ref[pl.ds(step * chunks + j, 1), :].astype(f32)
        wanted = jnp.broadcast_to(wanted, (LANES, LANES)).T.astype(i32)
        onehot = jnp.concatenate(
            [ones_where(wanted == lane + k * LANES) for k in range(source_rows // LANES)], axis=1
        )
        out_ref[j * LANES : (j + 1) * LANES, :] = dot(onehot, block).astype(bf16)


def permute_rows(rows, order, column, out, mib):
    row_count = order.shape[0]
    step_rows = min(512, row_count)
    return pl.pallas_call(
        permute_body,
        grid_spec=pltpu.PrefetchScalarGridSpec(
            num_scalar_prefetch=1,
            grid=(row_count // step_rows,),
            in_specs=[
                pl.BlockSpec((row_count // LANES, LANES), lambda i, c: (0, 0)),
                pl.BlockSpec((rows.shape[0], LANES), lambda i, c: (0, c[0])),
            ],
            out_specs=pl.BlockSpec((step_rows, LANES), lambda i, c: (i, 0)),
        ),
        out_shape=out((row_count, LANES), bf16),
        compiler_params=params(mib),
        cost_estimate=cost(2 * row_count * row_count * LANES * 4, 3 * row_count * LANES * 2),
        name="permute_rows",
    )(column, order.reshape(row_count // LANES, LANES), rows)


def bucket_body(shards, capacity, column_ref, shard_ref, point_ref, grads_ref, out_ref, place_ref):
    step = pl.program_id(0)
    row_count = grads_ref.shape[0]
    groups = row_count // LANES

    @pl.when(step == 0)
    def _():
        targets = shard_ref[...]
        masks = [ones_where(targets == t) for t in range(shards)]
        stacked = jnp.concatenate(masks, axis=0)
        above = ones_where(
            lax.broadcasted_iota(i32, (LANES, LANES), 0)
            < lax.broadcasted_iota(i32, (LANES, LANES), 1)
        )
        earlier = ones_where(
            lax.broadcasted_iota(i32, (groups, groups), 1)
            < lax.broadcasted_iota(i32, (groups, groups), 0)
        )
        in_row = dot(stacked, above)
        places = jnp.zeros((groups, LANES), f32)
        for t in range(shards):
            rows_before = jnp.sum(dot(earlier, masks[t]), axis=1, keepdims=True)
            place = in_row[t * groups : (t + 1) * groups] + rows_before + float(t * capacity)
            places = jnp.where(targets == t, place, places)
        place_ref[...] = places.astype(i32)

    slot = lax.broadcasted_iota(i32, (capacity, LANES), 0) + step * capacity
    onehot = jnp.concatenate(
        [ones_where(place_ref[j : j + 1, :] == slot) for j in range(groups)], axis=1
    )
    out_ref[0, :capacity, :] = dot(onehot, grads_ref[...]).astype(bf16)
    points = jnp.concatenate([point_ref[j : j + 1, :] for j in range(groups)], axis=1)
    high = points // INDEX_BASE
    low = points - high * INDEX_BASE
    digits = jnp.concatenate(
        [high.astype(f32), low.astype(f32), jnp.zeros((INDEX_ROWS - 2, row_count), f32)], axis=0
    )
    sent = dot_rows(digits.astype(bf16), onehot)
    chunks = capacity // LANES
    rows = [sent[d : d + 1, j * LANES : (j + 1) * LANES] for d in range(2) for j in range(chunks)]
    rows.append(jnp.zeros((INDEX_ROWS - 2 * chunks, LANES), f32))
    out_ref[0, capacity:, :] = jnp.concatenate(rows, axis=0).astype(bf16)


def bucket_rows(grads, targets, points, column, shards, capacity):
    row_count = grads.shape[0]
    groups = row_count // LANES
    return pl.pallas_call(
        functools.partial(bucket_body, shards, capacity),
        grid_spec=pltpu.PrefetchScalarGridSpec(
            num_scalar_prefetch=1,
            grid=(shards,),
            in_specs=[
                pl.BlockSpec((groups, LANES), lambda i, c: (0, 0)),
                pl.BlockSpec((groups, LANES), lambda i, c: (0, 0)),
                pl.BlockSpec((row_count, LANES), lambda i, c: (0, c[0])),
            ],
            out_specs=pl.BlockSpec((1, capacity + INDEX_ROWS, LANES), lambda i, c: (i, 0, 0)),
            scratch_shapes=[pltpu.VMEM((groups, LANES), i32)],
        ),
        out_shape=jax.ShapeDtypeStruct((shards, capacity + INDEX_ROWS, LANES), bf16),
        compiler_params=params(60),
        cost_estimate=cost(
            8 * shards * capacity * row_count * LANES, 3 * shards * capacity * LANES * 2
        ),
        name="bucket_rows",
    )(column, targets.reshape(groups, LANES), points.reshape(groups, LANES), grads)


def segment_body(got_ref, out_ref, total_ref):
    step = pl.program_id(0)
    capacity = got_ref.shape[1] - INDEX_ROWS
    chunks = capacity // LANES
    row_count = total_ref.shape[0]
    digits = got_ref[0, capacity:, :].astype(f32)
    index = (digits[:chunks] * float(INDEX_BASE) + digits[chunks : 2 * chunks]).astype(i32)
    row = lax.broadcasted_iota(i32, (row_count, LANES), 0)
    onehot = jnp.concatenate([ones_where(index[j : j + 1] == row) for j in range(chunks)], axis=1)
    part = dot(onehot, got_ref[0, :capacity, :])

    @pl.when(step == 0)
    def _():
        total_ref[...] = part

    @pl.when(step > 0)
    def _():
        total_ref[...] += part

    @pl.when(step == pl.num_programs(0) - 1)
    def _():
        out_ref[...] = total_ref[...].T.astype(bf16)


def segment_rows(got, row_count):
    shards, message, _ = got.shape
    return pl.pallas_call(
        segment_body,
        grid=(shards,),
        in_specs=[pl.BlockSpec((1, message, LANES), lambda i: (i, 0, 0))],
        out_specs=pl.BlockSpec((LANES, row_count), lambda i: (0, 0)),
        out_shape=pltpu.VMEM((LANES, row_count), bf16),
        scratch_shapes=[pltpu.VMEM((row_count, LANES), f32)],
        compiler_params=params(16),
        cost_estimate=cost(
            8 * shards * message * row_count * LANES, 3 * shards * message * LANES * 2
        ),
        name="segment_rows",
    )(got)


def project_body(
    column_ref,
    x0_ref,
    x1_ref,
    x2_ref,
    x3_ref,
    weight_ref,
    hidden_ref,
    normed_ref,
    inv_ref,
    key_ref,
    base2_t_ref,
    query_t_ref,
    key_t_ref,
    value_t_ref,
):
    me = column_ref[0]
    blocks = [r[...].astype(f32) for r in (x0_ref, x1_ref, x2_ref, x3_ref)]
    features = float(LANES * len(blocks))
    mean = jnp.sum(blocks[0] + blocks[1] + (blocks[2] + blocks[3]), axis=1, keepdims=True) / features
    centered = [b - mean for b in blocks]
    squares = [c * c for c in centered]
    var = jnp.sum(squares[0] + squares[1] + (squares[2] + squares[3]), axis=1, keepdims=True) / features
    inv = lax.rsqrt(var + epsilon)
    normed_ref[...] = centered[0] * inv
    inv_ref[...] = jnp.broadcast_to(inv, inv_ref.shape)
    for block, mask in zip(centered, BLOCK_MASKS):
        at = pl.multiple_of((me ^ mask) * LANES, LANES)
        hidden_ref[:, pl.ds(at, LANES)] = (block * inv).astype(bf16)
    projected = dot(hidden_ref[...], weight_ref[...]).astype(bf16)
    key_ref[...] = projected[:, LANES : 2 * LANES]
    query = projected[:, :LANES].astype(f32).T * score_scale
    query_t_ref[...] = query.astype(bf16)
    base2_t_ref[...] = (query * log2_e).astype(bf16)
    key_t_ref[...] = projected[:, LANES : 2 * LANES].astype(f32).T.astype(bf16)
    value_t_ref[...] = projected[:, 2 * LANES :].astype(f32).T.astype(bf16)


def project(blocks, weight, column):
    row_count = blocks[0].shape[0]
    step_rows = 512
    features = weight.shape[0]
    width = pl.BlockSpec((step_rows, LANES), lambda i, c: (i, 0))
    tall = pl.BlockSpec((LANES, step_rows), lambda i, c: (0, i))
    normal = lambda t: pltpu.VMEM((row_count, LANES), t)
    turned = pltpu.VMEM((LANES, row_count), bf16)
    return pl.pallas_call(
        project_body,
        grid_spec=pltpu.PrefetchScalarGridSpec(
            num_scalar_prefetch=1,
            grid=(row_count // step_rows,),
            in_specs=[width] * 4 + [pl.BlockSpec(weight.shape, lambda i, c: (0, 0))],
            out_specs=[pl.BlockSpec((step_rows, features), lambda i, c: (i, 0))]
            + [width] * 3
            + [tall] * 4,
        ),
        out_shape=[pltpu.VMEM((row_count, features), bf16)]
        + [pltpu.HBM((row_count, LANES), f32)] * 2
        + [normal(bf16)]
        + [turned] * 4,
        compiler_params=params(12),
        cost_estimate=cost(4 * row_count * features * 3 * LANES, row_count * LANES * 40),
        name="project",
    )(column, *blocks, weight)


def forward_body(
    key_ref,
    base2_t_ref,
    key_t_ref,
    value_t_ref,
    exp_ref,
    attended_ref,
    inverse_ref,
    covariance_ref,
    safe_ref,
):
    head = pl.program_id(0)
    at = pl.multiple_of(head * HD, HD)

    @pl.when(head == 0)
    def _():
        def largest(ref):
            squares = jnp.square(ref[...].astype(f32)).reshape(LANES // HD, HD, PATCH)
            return jnp.max(jnp.sum(squares, axis=1), axis=1, keepdims=True)

        bound = jnp.max(largest(base2_t_ref) * largest(key_t_ref))
        safe_ref[0] = (bound <= SAFE_SCORE * SAFE_SCORE).astype(i32)

    def attend(shifted):
        in_head = lax.broadcasted_iota(i32, (LANES, 1), 0) // HD == head
        query = jnp.where(in_head, base2_t_ref[...], jnp.zeros((), bf16))
        scores = dot(key_ref[...], query)
        if shifted:
            scores = scores - jnp.max(scores, axis=0, keepdims=True)
        weights = jnp.exp2(scores).astype(bf16)
        exp_ref[0] = weights
        keys = key_t_ref[pl.ds(at, HD), :].astype(f32)
        values = value_t_ref[pl.ds(at, HD), :].astype(f32)
        middle = jnp.mean(values, axis=1, keepdims=True)
        centered = values - middle
        features = [centered[j : j + 1] * keys for j in range(HD)]
        features += [keys, values, jnp.ones((HD, PATCH), f32)]
        sums = dot(jnp.concatenate([f.astype(bf16) for f in features], axis=0), weights)
        inverse = 1.0 / sums[(HD + 2) * HD : (HD + 2) * HD + 1]
        inverse_ref[0] = inverse
        mean_key = sums[HD * HD : (HD + 1) * HD] * inverse
        mean_value = sums[(HD + 1) * HD : (HD + 2) * HD] * inverse
        attended_ref[pl.ds(at, HD), :] = mean_value.astype(bf16)
        offset = mean_value - middle
        for j in range(HD):
            crossed = sums[j * HD : (j + 1) * HD] * inverse - offset[j : j + 1] * mean_key
            covariance_ref[0, j * HD : (j + 1) * HD, :] = crossed.astype(bf16)

    @pl.when(safe_ref[0] == 1)
    def _():
        attend(False)

    @pl.when(safe_ref[0] == 0)
    def _():
        attend(True)


def attention_forward(keys, base2_t, key_t, value_t):
    heads = LANES // HD
    tall = pl.BlockSpec((LANES, PATCH), lambda h: (0, 0))
    per_head = lambda h: (h, 0, 0)
    elements = heads * PATCH * PATCH
    return pl.pallas_call(
        forward_body,
        grid=(heads,),
        in_specs=[pl.BlockSpec((PATCH, LANES), lambda h: (0, 0)), tall, tall, tall],
        out_specs=[
            pl.BlockSpec((1, PATCH, PATCH), per_head),
            tall,
            pl.BlockSpec((1, 1, PATCH), per_head),
            pl.BlockSpec((1, HD * HD, PATCH), per_head),
        ],
        out_shape=[
            pltpu.HBM((heads, PATCH, PATCH), bf16),
            pltpu.VMEM((LANES, PATCH), bf16),
            pltpu.VMEM((heads, 1, PATCH), f32),
            pltpu.HBM((heads, HD * HD, PATCH), bf16),
        ],
        scratch_shapes=[pltpu.SMEM((1,), i32)],
        compiler_params=params(28),
        cost_estimate=cost(1600 * elements, 2 * elements, elements),
        name="attention_forward",
    )(keys, base2_t, key_t, value_t)


def backward_body(
    column_ref,
    exp_ref,
    inverse_ref,
    covariance_ref,
    query_t_ref,
    value_t_ref,
    attended_ref,
    g0_ref,
    g1_ref,
    g2_ref,
    g3_ref,
    weight_t_ref,
    d_out_ref,
    d_query_ref,
    d_key_ref,
    d_value_ref,
    d_attended_ref,
    exp_all_ref,
    covariance_all_ref,
    exp_sems,
    covariance_sems,
):
    head = pl.program_id(0)
    at = pl.multiple_of(head * HD, HD)

    def copies(h):
        return (
            pltpu.make_async_copy(exp_ref.at[h], exp_all_ref.at[h], exp_sems.at[h]),
            pltpu.make_async_copy(
                covariance_ref.at[h], covariance_all_ref.at[h], covariance_sems.at[h]
            ),
        )

    @pl.when(head == 0)
    def _():
        for h in range(LANES // HD):
            for copy in copies(h):
                copy.start()
        me = column_ref[0]
        for block, mask in zip((g0_ref, g1_ref, g2_ref, g3_ref), BLOCK_MASKS):
            start = pl.multiple_of((me ^ mask) * LANES, LANES)
            d_out_ref[pl.ds(start, LANES), :] = block[...]
        d_attended_ref[...] = dot(weight_t_ref[...], d_out_ref[...]).astype(bf16)

    grads = d_attended_ref[pl.ds(at, HD), :].astype(f32)
    query = query_t_ref[pl.ds(at, HD), :].astype(f32)
    values = value_t_ref[pl.ds(at, HD), :].astype(f32)
    inverse = inverse_ref[0]
    middle = jnp.mean(values, axis=1, keepdims=True)
    centered = values - middle
    offset = attended_ref[pl.ds(at, HD), :].astype(f32) - middle
    scaled = grads * inverse
    delta = jnp.sum(scaled * offset, axis=0, keepdims=True)
    features = [scaled[j : j + 1] * query for j in range(HD)] + [delta * query, scaled]
    for copy in copies(head):
        copy.wait()
    sums = dot_rows(jnp.concatenate([f.astype(bf16) for f in features], axis=0), exp_all_ref[head])
    d_value_ref[pl.ds(at, HD), :] = sums[(HD + 1) * HD :].astype(bf16)
    d_key = centered[0:1] * sums[:HD]
    d_query = grads[0:1] * covariance_all_ref[head, :HD, :].astype(f32)
    for j in range(1, HD):
        rows = slice(j * HD, (j + 1) * HD)
        d_key += centered[j : j + 1] * sums[rows]
        d_query += grads[j : j + 1] * covariance_all_ref[head, rows, :].astype(f32)
    d_key_ref[pl.ds(at, HD), :] = (d_key - sums[HD * HD : (HD + 1) * HD]).astype(bf16)
    d_query_ref[pl.ds(at, HD), :] = (d_query * score_scale).astype(bf16)


def attention_backward(patch, weights, inverse, covariance, query_t, value_t, attended, grads, weight_t, column):
    features = weight_t.shape[1]
    heads = LANES // HD
    tall = pl.BlockSpec((LANES, PATCH), lambda h, c: (0, 0))
    part = pl.BlockSpec((LANES, PATCH), lambda h, c: (0, patch))
    per_head = lambda h, c: (h, 0, 0)
    elements = heads * PATCH * PATCH
    turned = pltpu.VMEM((LANES, PATCH), bf16)
    return pl.pallas_call(
        backward_body,
        grid_spec=pltpu.PrefetchScalarGridSpec(
            num_scalar_prefetch=1,
            grid=(heads,),
            in_specs=[
                pl.BlockSpec(memory_space=pltpu.HBM),
                pl.BlockSpec((1, 1, PATCH), per_head),
                pl.BlockSpec(memory_space=pltpu.HBM),
                tall,
                tall,
                tall,
                part,
                part,
                part,
                part,
                pl.BlockSpec(weight_t.shape, lambda h, c: (0, 0)),
            ],
            out_specs=[pl.BlockSpec((features, PATCH), lambda h, c: (0, 0)), tall, tall, tall],
            scratch_shapes=[
                pltpu.VMEM((LANES, PATCH), bf16),
                pltpu.VMEM((heads, PATCH, PATCH), bf16),
                pltpu.VMEM((heads, HD * HD, PATCH), bf16),
                pltpu.SemaphoreType.DMA((heads,)),
                pltpu.SemaphoreType.DMA((heads,)),
            ],
        ),
        out_shape=[pltpu.VMEM((features, PATCH), bf16), turned, turned, turned],
        compiler_params=params(30),
        cost_estimate=cost(1100 * elements, 2 * elements),
        name="attention_backward",
    )(column, weights, inverse, covariance, query_t, value_t, attended, *grads, weight_t)


def whole(shape, dtype):
    return jax.ShapeDtypeStruct(shape, dtype)


def weight_grad_body(*refs):
    *ins, out_ref = refs
    patches = [ins[:6], ins[6:]]
    for t in range(3):
        total = dot(patches[0][t][...], patches[0][4][...]) + dot(patches[1][t][...], patches[1][4][...])
        out_ref[:, t * LANES : (t + 1) * LANES] = total.T.astype(bf16)
    total = dot_rows(patches[0][3][...], patches[0][5][...]) + dot_rows(
        patches[1][3][...], patches[1][5][...]
    )
    out_ref[:, 3 * LANES :] = total.T.astype(bf16)


def weight_grads(patches):
    features = patches[0][4].shape[1]
    work = 2 * PATCH * features * LANES
    return pl.pallas_call(
        weight_grad_body,
        out_shape=whole((features, 4 * LANES), bf16),
        compiler_params=params(12),
        cost_estimate=cost(8 * work, 12 * PATCH * features),
        name="weight_grads",
    )(*patches[0], *patches[1])


def split_sums(sums):
    high = sums.astype(bf16)
    low = (sums - high.astype(f32)).astype(bf16)
    pad = jnp.zeros((INDEX_ROWS - 2 * sums.shape[0], sums.shape[1]), f32)
    return jnp.concatenate([high.astype(f32), low.astype(f32), pad], axis=0).astype(bf16)


def join_sums(rows):
    rows = rows.astype(f32)
    return rows[0:2] + rows[2:4]


def partial_body(
    column_ref,
    d_query_ref,
    d_key_ref,
    d_value_ref,
    query_ref,
    key_ref,
    value_ref,
    weight_ref,
    mine_ref,
    other_ref,
    sums_ref,
):
    me = column_ref[0]
    d_projected = jnp.concatenate([d_query_ref[...], d_key_ref[...], d_value_ref[...]], axis=0)
    plain = jnp.zeros((1, PATCH), f32)
    for j, mask in enumerate(BLOCK_MASKS):
        start = pl.multiple_of((me ^ mask) * LANES, LANES)
        block = dot(weight_ref[pl.ds(start, LANES), :], d_projected).astype(bf16)
        plain += jnp.sum(block.astype(f32), axis=0, keepdims=True)
        to = mine_ref if j < 2 else other_ref
        to[(j % 2) * LANES : (j % 2 + 1) * LANES, :] = block
    crossed = (
        d_query_ref[...].astype(f32) * (query_ref[...].astype(f32) / score_scale)
        + d_key_ref[...].astype(f32) * key_ref[...].astype(f32)
        + d_value_ref[...].astype(f32) * value_ref[...].astype(f32)
    )
    sums = jnp.concatenate([plain, jnp.sum(crossed, axis=0, keepdims=True)], axis=0)
    sums_ref[...] = sums
    other_ref[2 * LANES :, :] = split_sums(sums)


def hidden_part(d_query, d_key, d_value, query, key, value, weight, column):
    features = weight.shape[0]
    return pl.pallas_call(
        partial_body,
        in_specs=[pl.BlockSpec(memory_space=pltpu.SMEM)] + [pl.BlockSpec(memory_space=pltpu.VMEM)] * 7,
        out_shape=[
            pltpu.VMEM((2 * LANES, PATCH), bf16),
            pltpu.VMEM((2 * LANES + INDEX_ROWS, PATCH), bf16),
            pltpu.VMEM((2, PATCH), f32),
        ],
        compiler_params=params(12),
        cost_estimate=cost(6 * PATCH * features * LANES, 4 * PATCH * features),
        name="hidden_part",
    )(column, d_query, d_key, d_value, query, key, value, weight)


def pair_body(mine_ref, sums_ref, got_ref, kept_ref, sums_out_ref, sent_ref):
    pair = mine_ref[...].astype(f32) + got_ref[: 2 * LANES, :].astype(f32)
    sums = sums_ref[...] + join_sums(got_ref[2 * LANES :, :])
    kept_ref[...] = pair[:LANES]
    sums_out_ref[...] = sums
    sent_ref[:LANES, :] = pair[LANES:].astype(bf16)
    sent_ref[LANES:, :] = split_sums(sums)


def pair_sum(mine, sums, got):
    return pl.pallas_call(
        pair_body,
        out_shape=[
            pltpu.VMEM((LANES, PATCH), f32),
            pltpu.VMEM((2, PATCH), f32),
            pltpu.VMEM((LANES + INDEX_ROWS, PATCH), bf16),
        ],
        compiler_params=params(6),
        cost_estimate=cost(4 * LANES * PATCH, 16 * LANES * PATCH),
        name="pair_sum",
    )(mine, sums, got)


def points_body(kept_ref, sums_ref, got_ref, d_out_ref, normed_ref, inv_ref, *rest):
    out_ref = rest[-1]
    features = 4.0 * LANES
    means = (sums_ref[...] + join_sums(got_ref[LANES:, :])) / features
    d_hidden = kept_ref[...] + got_ref[:LANES, :].astype(f32) - means[0:1]
    cross = jnp.broadcast_to(means[1:2], (LANES, PATCH)).T
    inner = d_hidden.T - normed_ref[...] * cross
    out_ref[...] = d_out_ref[...].astype(f32).T + inv_ref[...] * inner


def points_grad(patch, patches, kept, sums, got, d_out, normed, inv_scale, before):
    full = lambda a: pl.BlockSpec(a.shape, lambda i: (0, 0))
    in_specs = [full(kept), full(sums), full(got), pl.BlockSpec((LANES, PATCH), lambda i: (0, patch))]
    in_specs += [full(normed), full(inv_scale)]
    operands = [kept, sums, got, d_out, normed, inv_scale]
    if before is not None:
        in_specs.append(pl.BlockSpec(memory_space=pl.ANY))
        operands.append(before)
    return pl.pallas_call(
        points_body,
        grid=(1,),
        in_specs=in_specs,
        out_specs=pl.BlockSpec((PATCH, LANES), lambda i: (patch, 0)),
        out_shape=whole((patches * PATCH, LANES), f32),
        input_output_aliases={} if before is None else {len(operands) - 1: 0},
        compiler_params=params(8),
        cost_estimate=cost(8 * LANES * PATCH, 24 * LANES * PATCH),
        name="points_grad",
    )(*operands)


def local(
    scan_points,
    send_order,
    arrive_order,
    qkv_weight,
    out_weight,
    voxel_grads,
    voxel_shard,
    voxel_point,
):
    shards = lax.axis_size("seq")
    members = lax.axis_size("mp")
    local_rows, features = scan_points.shape
    voxels = voxel_grads.shape[0]
    capacity = 2 * voxels // shards
    patches = local_rows // PATCH
    column = lax.axis_index("mp").astype(i32).reshape(1)
    zero = jnp.zeros((1,), i32)
    weight = qkv_weight.reshape(features, 3 * LANES)
    weight_t = out_weight.T

    def swap(rows, mask):
        return lax.ppermute(rows, "mp", [(i, i ^ mask) for i in range(members)])

    def exchange(rows):
        return lax.all_to_all(rows, "seq", split_axis=0, concat_axis=0, tiled=True)

    def after(value, first):
        return lax.optimization_barrier((value, first))

    def in_hbm(value):
        return pltpu.with_memory_space_constraint(value, pltpu.HBM)

    arrived = exchange(permute_rows(scan_points, send_order, column, whole, 60))
    buckets = bucket_rows(voxel_grads, voxel_shard, voxel_point, column, shards, capacity)
    got = exchange(buckets.reshape(shards * (capacity + INDEX_ROWS), LANES))
    (weight, weight_t), arrived = after((weight, weight_t), arrived)
    owns = [
        permute_rows(arrived, arrive_order[p * PATCH : (p + 1) * PATCH], zero, pltpu.VMEM, 8)
        for p in range(patches)
    ]
    across = [swap(own, 2) for own in owns]

    def forward(p):
        columns = (owns[p], across[p], swap(owns[p], 1), swap(across[p], 1))
        projected = project(columns, weight, column)
        return projected, attention_forward(projected[3], projected[4], *projected[6:])

    projected0, forward0 = forward(0)
    (got, across[1]), forward0 = after((got, across[1]), forward0)
    summed_rows = segment_rows(got.reshape(shards, capacity + INDEX_ROWS, LANES), local_rows)
    summed_across = swap(summed_rows, 2)
    across[1], summed_rows = after(across[1], summed_rows)
    projected1, forward1 = forward(1)
    summed_across, forward1 = after(summed_across, forward1)
    grads = (summed_rows, summed_across, swap(summed_rows, 1), swap(summed_across, 1))
    forwards = [(projected0, forward0), (projected1, forward1)]

    kept, sums, received, grad_parts = [], [], [], []
    for p in range(patches):
        (hidden, _, _, _, _, query_t, key_t, value_t), (weights, attended, inverse, covariance) = forwards[p]
        if p > 0:
            weights, sent = after(weights, sent)
            received.append(swap(sent, 2))
        d_out, d_query, d_key, d_value = attention_backward(
            p, weights, inverse, covariance, query_t, value_t, attended, grads, weight_t, column
        )
        if p > 0:
            received[p - 1], d_query = after(received[p - 1], d_query)
        grad_parts.append((d_query, d_key, d_value, attended, hidden, d_out))
        mine, other, own_sums = hidden_part(d_query, d_key, d_value, query_t, key_t, value_t, weight, column)
        if p == patches - 1:
            grad_parts, other = after(grad_parts, other)
        keep, pair_sums, sent = pair_sum(mine, own_sums, swap(other, 1))
        kept.append(keep)
        sums.append(pair_sums)
    received.append(swap(sent, 2))
    d_points = None
    for p in range(patches):
        normed, inv_scale = map(in_hbm, forwards[p][0][1:3])
        d_points = points_grad(
            p, patches, kept[p], sums[p], received[p], grads[0], normed, inv_scale, d_points
        )
    parts = exchange(weight_grads(grad_parts)).reshape(shards, features // shards, 4 * LANES)
    summed = jnp.sum(parts.astype(f32), axis=0)
    grad_qkv = summed[:, : 3 * LANES].reshape(features // shards, 3, LANES)
    grad_out = summed[:, 3 * LANES :]
    return (d_points, grad_qkv, grad_out)


def solution(mesh):
    in_specs = (
        P("seq", None),
        P("seq"),
        P("seq"),
        P(None, None, "mp"),
        P(None, "mp"),
        P("seq", None),
        P("seq", None),
        P("seq"),
    )
    out_specs = (P("seq", "mp"), P("seq", None, "mp"), P("seq", "mp"))
    return jax.shard_map(local, mesh=mesh, in_specs=in_specs, out_specs=out_specs, check_vma=False)
```

```python
import functools

import jax
import jax.numpy as jnp
from jax import lax
from jax.experimental import pallas as pl
from jax.experimental.pallas import tpu as pltpu
from jax.sharding import PartitionSpec as P

HD = 16
PATCH = 1024
LANES = 128
INDEX_ROWS = 16
INDEX_BASE = 64
BLOCK_MASKS = (0, 2, 1, 3)
SAFE_SCORE = 60.0

score_scale = 0.25
epsilon = 1e-05
log2_e = 1.4426950408889634

f32 = jnp.float32
bf16 = jnp.bfloat16
i32 = jnp.int32

ROWS_BY_ROWS = (((1,), (1,)), ((), ()))


def params(mib):
    return pltpu.CompilerParams(vmem_limit_bytes=mib << 20)


def cost(flops, bytes_accessed, transcendentals=0):
    return pl.CostEstimate(
        flops=int(flops), bytes_accessed=int(bytes_accessed), transcendentals=int(transcendentals)
    )


def dot(a, b):
    return jnp.dot(a, b, preferred_element_type=f32)


def dot_rows(a, b):
    return lax.dot_general(a, b, ROWS_BY_ROWS, preferred_element_type=f32)


def ones_where(mask):
    return jnp.where(mask, 1.0, 0.0).astype(bf16)


def permute_body(column_ref, order_ref, block_ref, out_ref):
    step = pl.program_id(0)
    half = block_ref.shape[0] // 2
    chunks = out_ref.shape[0] // LANES
    lane = lax.broadcasted_iota(i32, (LANES, LANES), 1)
    sides = jnp.concatenate([block_ref[:half, :], block_ref[half:, :]], axis=1)
    onehots, lows = [], []
    for j in range(chunks):
        wanted = order_ref[pl.ds(step * chunks + j, 1), :].astype(f32)
        wanted = jnp.broadcast_to(wanted, (LANES, LANES)).T.astype(i32)
        low = wanted < half
        local_row = jnp.where(low, wanted, wanted - half)
        onehots.append(
            jnp.concatenate(
                [ones_where(local_row == lane + k * LANES) for k in range(half // LANES)], axis=1
            )
        )
        lows.append(low)
    both = dot(jnp.concatenate(onehots, axis=0), sides)
    for j in range(chunks):
        rows = slice(j * LANES, (j + 1) * LANES)
        out_ref[rows, :] = jnp.where(lows[j], both[rows, :LANES], both[rows, LANES:]).astype(bf16)


def permute_rows(rows, order, column, part, parts, out, mib):
    row_count = order.shape[0] // parts
    groups = row_count // LANES
    step_rows = min(512, row_count)
    return pl.pallas_call(
        permute_body,
        grid_spec=pltpu.PrefetchScalarGridSpec(
            num_scalar_prefetch=1,
            grid=(row_count // step_rows,),
            in_specs=[
                pl.BlockSpec((groups, LANES), lambda i, c: (part, 0)),
                pl.BlockSpec((rows.shape[0], LANES), lambda i, c: (0, c[0])),
            ],
            out_specs=pl.BlockSpec((step_rows, LANES), lambda i, c: (i, 0)),
        ),
        out_shape=out((row_count, LANES), bf16),
        compiler_params=params(mib),
        cost_estimate=cost(2 * row_count * row_count * LANES * 4, 3 * row_count * LANES * 2),
        name="permute_rows",
    )(column, order.reshape(parts * groups, LANES), rows)


def bucket_body(shards, capacity, column_ref, shard_ref, point_ref, grads_ref, out_ref, place_ref):
    step = pl.program_id(0)
    row_count = grads_ref.shape[0]
    groups = row_count // LANES

    @pl.when(step == 0)
    def _():
        targets = shard_ref[...]
        masks = [ones_where(targets == t) for t in range(shards)]
        stacked = jnp.concatenate(masks, axis=0)
        above = ones_where(
            lax.broadcasted_iota(i32, (LANES, LANES), 0)
            < lax.broadcasted_iota(i32, (LANES, LANES), 1)
        )
        earlier = ones_where(
            lax.broadcasted_iota(i32, (groups, groups), 1)
            < lax.broadcasted_iota(i32, (groups, groups), 0)
        )
        in_row = dot(stacked, above)
        places = jnp.zeros((groups, LANES), f32)
        for t in range(shards):
            rows_before = jnp.sum(dot(earlier, masks[t]), axis=1, keepdims=True)
            place = in_row[t * groups : (t + 1) * groups] + rows_before + float(t * capacity)
            places = jnp.where(targets == t, place, places)
        place_ref[...] = places.astype(i32)

    slot = lax.broadcasted_iota(i32, (capacity, LANES), 0) + step * capacity
    onehot = jnp.concatenate(
        [ones_where(place_ref[j : j + 1, :] == slot) for j in range(groups)], axis=1
    )
    out_ref[0, :capacity, :] = dot(onehot, grads_ref[...]).astype(bf16)
    points = jnp.concatenate([point_ref[j : j + 1, :] for j in range(groups)], axis=1)
    high = points // INDEX_BASE
    low = points - high * INDEX_BASE
    digits = jnp.concatenate(
        [high.astype(f32), low.astype(f32), jnp.zeros((INDEX_ROWS - 2, row_count), f32)], axis=0
    )
    sent = dot_rows(digits.astype(bf16), onehot)
    chunks = capacity // LANES
    rows = [sent[d : d + 1, j * LANES : (j + 1) * LANES] for d in range(2) for j in range(chunks)]
    rows.append(jnp.zeros((INDEX_ROWS - 2 * chunks, LANES), f32))
    out_ref[0, capacity:, :] = jnp.concatenate(rows, axis=0).astype(bf16)


def bucket_rows(grads, targets, points, column, shards, capacity):
    row_count = grads.shape[0]
    groups = row_count // LANES
    return pl.pallas_call(
        functools.partial(bucket_body, shards, capacity),
        grid_spec=pltpu.PrefetchScalarGridSpec(
            num_scalar_prefetch=1,
            grid=(shards,),
            in_specs=[
                pl.BlockSpec((groups, LANES), lambda i, c: (0, 0)),
                pl.BlockSpec((groups, LANES), lambda i, c: (0, 0)),
                pl.BlockSpec((row_count, LANES), lambda i, c: (0, c[0])),
            ],
            out_specs=pl.BlockSpec((1, capacity + INDEX_ROWS, LANES), lambda i, c: (i, 0, 0)),
            scratch_shapes=[pltpu.VMEM((groups, LANES), i32)],
        ),
        out_shape=jax.ShapeDtypeStruct((shards, capacity + INDEX_ROWS, LANES), bf16),
        compiler_params=params(60),
        cost_estimate=cost(
            8 * shards * capacity * row_count * LANES, 3 * shards * capacity * LANES * 2
        ),
        name="bucket_rows",
    )(column, targets.reshape(groups, LANES), points.reshape(groups, LANES), grads)


def segment_body(got_ref, out_ref, total_ref):
    step = pl.program_id(0)
    capacity = got_ref.shape[1] - INDEX_ROWS
    chunks = capacity // LANES
    half = total_ref.shape[0]
    digits = got_ref[0, capacity:, :].astype(f32)
    index = digits[:chunks] * float(INDEX_BASE) + digits[chunks : 2 * chunks]
    position = index.astype(i32)
    local_row = jnp.where(position < half, position, position - half)
    row = lax.broadcasted_iota(i32, (half, LANES), 0)
    onehot = jnp.concatenate([ones_where(local_row[j : j + 1] == row) for j in range(chunks)], axis=1)
    sides = []
    for j in range(chunks):
        low = jnp.broadcast_to(index[j : j + 1], (LANES, LANES)).T < float(half)
        rows = got_ref[0, j * LANES : (j + 1) * LANES, :].astype(f32)
        sides.append(
            jnp.concatenate([jnp.where(low, rows, 0.0), jnp.where(low, 0.0, rows)], axis=1).astype(bf16)
        )
    part = dot(onehot, jnp.concatenate(sides, axis=0))

    @pl.when(step == 0)
    def _():
        total_ref[...] = part

    @pl.when(step > 0)
    def _():
        total_ref[...] += part

    @pl.when(step == pl.num_programs(0) - 1)
    def _():
        out_ref[:, :half] = total_ref[:, :LANES].T.astype(bf16)
        out_ref[:, half:] = total_ref[:, LANES:].T.astype(bf16)


def segment_rows(got, row_count):
    shards, message, _ = got.shape
    return pl.pallas_call(
        segment_body,
        grid=(shards,),
        in_specs=[pl.BlockSpec((1, message, LANES), lambda i: (i, 0, 0))],
        out_specs=pl.BlockSpec((LANES, row_count), lambda i: (0, 0)),
        out_shape=pltpu.VMEM((LANES, row_count), bf16),
        scratch_shapes=[pltpu.VMEM((row_count // 2, 2 * LANES), f32)],
        compiler_params=params(16),
        cost_estimate=cost(
            8 * shards * message * row_count * LANES, 3 * shards * message * LANES * 2
        ),
        name="segment_rows",
    )(got)


def project_body(
    column_ref,
    x0_ref,
    x1_ref,
    x2_ref,
    x3_ref,
    weight_ref,
    hidden_ref,
    normed_ref,
    inv_ref,
    key_ref,
    base2_t_ref,
    query_t_ref,
    key_t_ref,
    value_t_ref,
):
    me = column_ref[0]
    blocks = [r[...].astype(f32) for r in (x0_ref, x1_ref, x2_ref, x3_ref)]
    features = float(LANES * len(blocks))
    mean = jnp.sum(blocks[0] + blocks[1] + (blocks[2] + blocks[3]), axis=1, keepdims=True) / features
    centered = [b - mean for b in blocks]
    squares = [c * c for c in centered]
    var = jnp.sum(squares[0] + squares[1] + (squares[2] + squares[3]), axis=1, keepdims=True) / features
    inv = lax.rsqrt(var + epsilon)
    normed_ref[...] = (centered[0] * inv).T
    inv_ref[...] = jnp.broadcast_to(inv, centered[0].shape).T[:8]
    for block, mask in zip(centered, BLOCK_MASKS):
        at = pl.multiple_of((me ^ mask) * LANES, LANES)
        hidden_ref[:, pl.ds(at, LANES)] = (block * inv).astype(bf16)
    weight = jnp.concatenate([weight_ref[t] for t in range(3)], axis=1)
    projected = dot(hidden_ref[...], weight).astype(bf16)
    key_ref[...] = projected[:, LANES : 2 * LANES]
    query = projected[:, :LANES].astype(f32).T * score_scale
    query_t_ref[...] = query.astype(bf16)
    base2_t_ref[...] = (query * log2_e).astype(bf16)
    key_t_ref[...] = projected[:, LANES : 2 * LANES].astype(f32).T.astype(bf16)
    value_t_ref[...] = projected[:, 2 * LANES :].astype(f32).T.astype(bf16)


def project(blocks, weight, column):
    row_count = blocks[0].shape[0]
    step_rows = 512
    features = weight.shape[1]
    width = pl.BlockSpec((step_rows, LANES), lambda i, c: (i, 0))
    tall = pl.BlockSpec((LANES, step_rows), lambda i, c: (0, i))
    normal = lambda t: pltpu.VMEM((row_count, LANES), t)
    turned = pltpu.VMEM((LANES, row_count), bf16)
    return pl.pallas_call(
        project_body,
        grid_spec=pltpu.PrefetchScalarGridSpec(
            num_scalar_prefetch=1,
            grid=(row_count // step_rows,),
            in_specs=[width] * 4 + [pl.BlockSpec(weight.shape, lambda i, c: (0, 0, 0))],
            out_specs=[
                pl.BlockSpec((step_rows, features), lambda i, c: (i, 0)),
                tall,
                pl.BlockSpec((8, step_rows), lambda i, c: (0, i)),
                width,
            ]
            + [tall] * 4,
        ),
        out_shape=[pltpu.VMEM((row_count, features), bf16)]
        + [pltpu.HBM((LANES, row_count), f32), pltpu.HBM((8, row_count), f32)]
        + [normal(bf16)]
        + [turned] * 4,
        compiler_params=params(12),
        cost_estimate=cost(4 * row_count * features * 3 * LANES, row_count * LANES * 40),
        name="project",
    )(column, *blocks, weight)


def forward_body(
    key_ref,
    base2_t_ref,
    key_t_ref,
    value_t_ref,
    exp_ref,
    attended_ref,
    inverse_ref,
    covariance_ref,
    safe_ref,
):
    head = pl.program_id(0)
    at = pl.multiple_of(head * HD, HD)

    @pl.when(head == 0)
    def _():
        def largest(ref):
            squares = jnp.square(ref[...].astype(f32)).reshape(LANES // HD, HD, PATCH)
            return jnp.max(jnp.sum(squares, axis=1), axis=1, keepdims=True)

        bound = jnp.max(largest(base2_t_ref) * largest(key_t_ref))
        safe_ref[0] = (bound <= SAFE_SCORE * SAFE_SCORE).astype(i32)

    def attend(shifted):
        in_head = lax.broadcasted_iota(i32, (LANES, 1), 0) // HD == head
        query = jnp.where(in_head, base2_t_ref[...], jnp.zeros((), bf16))
        scores = dot(key_ref[...], query)
        if shifted:
            scores = scores - jnp.max(scores, axis=0, keepdims=True)
        weights = jnp.exp2(scores).astype(bf16)
        exp_ref[0] = weights
        keys = key_t_ref[pl.ds(at, HD), :].astype(f32)
        values = value_t_ref[pl.ds(at, HD), :].astype(f32)
        middle = jnp.mean(values, axis=1, keepdims=True)
        centered = values - middle
        features = [centered[j : j + 1] * keys for j in range(HD)]
        features += [keys, values, jnp.ones((HD, PATCH), f32)]
        sums = dot(jnp.concatenate([f.astype(bf16) for f in features], axis=0), weights)
        inverse = 1.0 / sums[(HD + 2) * HD : (HD + 2) * HD + 1]
        inverse_ref[0] = inverse
        mean_key = sums[HD * HD : (HD + 1) * HD] * inverse
        mean_value = sums[(HD + 1) * HD : (HD + 2) * HD] * inverse
        attended_ref[pl.ds(at, HD), :] = mean_value.astype(bf16)
        offset = mean_value - middle
        for j in range(HD):
            crossed = sums[j * HD : (j + 1) * HD] * inverse - offset[j : j + 1] * mean_key
            covariance_ref[0, j * HD : (j + 1) * HD, :] = crossed.astype(bf16)

    @pl.when(safe_ref[0] == 1)
    def _():
        attend(False)

    @pl.when(safe_ref[0] == 0)
    def _():
        attend(True)


def attention_forward(keys, base2_t, key_t, value_t):
    heads = LANES // HD
    tall = pl.BlockSpec((LANES, PATCH), lambda h: (0, 0))
    per_head = lambda h: (h, 0, 0)
    elements = heads * PATCH * PATCH
    return pl.pallas_call(
        forward_body,
        grid=(heads,),
        in_specs=[pl.BlockSpec((PATCH, LANES), lambda h: (0, 0)), tall, tall, tall],
        out_specs=[
            pl.BlockSpec((1, PATCH, PATCH), per_head),
            tall,
            pl.BlockSpec((1, 1, PATCH), per_head),
            pl.BlockSpec((1, HD * HD, PATCH), per_head),
        ],
        out_shape=[
            pltpu.HBM((heads, PATCH, PATCH), bf16),
            pltpu.VMEM((LANES, PATCH), bf16),
            pltpu.VMEM((heads, 1, PATCH), f32),
            pltpu.HBM((heads, HD * HD, PATCH), bf16),
        ],
        scratch_shapes=[pltpu.SMEM((1,), i32)],
        compiler_params=params(28),
        cost_estimate=cost(1600 * elements, 2 * elements, elements),
        name="attention_forward",
    )(keys, base2_t, key_t, value_t)


def backward_body(
    column_ref,
    exp_ref,
    inverse_ref,
    covariance_ref,
    query_t_ref,
    value_t_ref,
    attended_ref,
    g0_ref,
    g1_ref,
    g2_ref,
    g3_ref,
    weight_ref,
    d_out_ref,
    d_query_ref,
    d_key_ref,
    d_value_ref,
    d_attended_ref,
    exp_all_ref,
    covariance_all_ref,
    exp_sems,
    covariance_sems,
):
    head = pl.program_id(0)
    at = pl.multiple_of(head * HD, HD)

    def copies(h):
        return (
            pltpu.make_async_copy(exp_ref.at[h], exp_all_ref.at[h], exp_sems.at[h]),
            pltpu.make_async_copy(
                covariance_ref.at[h], covariance_all_ref.at[h], covariance_sems.at[h]
            ),
        )

    @pl.when(head == 0)
    def _():
        for h in range(LANES // HD):
            for copy in copies(h):
                copy.start()
        me = column_ref[0]
        for block, mask in zip((g0_ref, g1_ref, g2_ref, g3_ref), BLOCK_MASKS):
            start = pl.multiple_of((me ^ mask) * LANES, LANES)
            d_out_ref[pl.ds(start, LANES), :] = block[...]
        d_attended_ref[...] = dot(weight_ref[...].T, d_out_ref[...]).astype(bf16)

    grads = d_attended_ref[pl.ds(at, HD), :].astype(f32)
    query = query_t_ref[pl.ds(at, HD), :].astype(f32)
    values = value_t_ref[pl.ds(at, HD), :].astype(f32)
    inverse = inverse_ref[0]
    middle = jnp.mean(values, axis=1, keepdims=True)
    centered = values - middle
    offset = attended_ref[pl.ds(at, HD), :].astype(f32) - middle
    scaled = grads * inverse
    delta = jnp.sum(scaled * offset, axis=0, keepdims=True)
    features = [scaled[j : j + 1] * query for j in range(HD)] + [delta * query, scaled]
    for copy in copies(head):
        copy.wait()
    sums = dot_rows(jnp.concatenate([f.astype(bf16) for f in features], axis=0), exp_all_ref[head])
    d_value_ref[pl.ds(at, HD), :] = sums[(HD + 1) * HD :].astype(bf16)
    d_key = centered[0:1] * sums[:HD]
    d_query = grads[0:1] * covariance_all_ref[head, :HD, :].astype(f32)
    for j in range(1, HD):
        rows = slice(j * HD, (j + 1) * HD)
        d_key += centered[j : j + 1] * sums[rows]
        d_query += grads[j : j + 1] * covariance_all_ref[head, rows, :].astype(f32)
    d_key_ref[pl.ds(at, HD), :] = (d_key - sums[HD * HD : (HD + 1) * HD]).astype(bf16)
    d_query_ref[pl.ds(at, HD), :] = (d_query * score_scale).astype(bf16)


def attention_backward(patch, weights, inverse, covariance, query_t, value_t, attended, grads, weight, column):
    features = weight.shape[0]
    heads = LANES // HD
    tall = pl.BlockSpec((LANES, PATCH), lambda h, c: (0, 0))
    part = pl.BlockSpec((LANES, PATCH), lambda h, c: (0, patch))
    per_head = lambda h, c: (h, 0, 0)
    elements = heads * PATCH * PATCH
    turned = pltpu.VMEM((LANES, PATCH), bf16)
    return pl.pallas_call(
        backward_body,
        grid_spec=pltpu.PrefetchScalarGridSpec(
            num_scalar_prefetch=1,
            grid=(heads,),
            in_specs=[
                pl.BlockSpec(memory_space=pltpu.HBM),
                pl.BlockSpec((1, 1, PATCH), per_head),
                pl.BlockSpec(memory_space=pltpu.HBM),
                tall,
                tall,
                tall,
                part,
                part,
                part,
                part,
                pl.BlockSpec(weight.shape, lambda h, c: (0, 0)),
            ],
            out_specs=[pl.BlockSpec((features, PATCH), lambda h, c: (0, 0)), tall, tall, tall],
            scratch_shapes=[
                pltpu.VMEM((LANES, PATCH), bf16),
                pltpu.VMEM((heads, PATCH, PATCH), bf16),
                pltpu.VMEM((heads, HD * HD, PATCH), bf16),
                pltpu.SemaphoreType.DMA((heads,)),
                pltpu.SemaphoreType.DMA((heads,)),
            ],
        ),
        out_shape=[pltpu.VMEM((features, PATCH), bf16), turned, turned, turned],
        compiler_params=params(30),
        cost_estimate=cost(1100 * elements, 2 * elements),
        name="attention_backward",
    )(column, weights, inverse, covariance, query_t, value_t, attended, *grads, weight)


def whole(shape, dtype):
    return jax.ShapeDtypeStruct(shape, dtype)


def weight_grad_body(*refs):
    *ins, out_ref = refs
    patches = [ins[:6], ins[6:]]
    for t in range(3):
        total = dot(patches[0][t][...], patches[0][4][...]) + dot(patches[1][t][...], patches[1][4][...])
        out_ref[:, t * LANES : (t + 1) * LANES] = total.T.astype(bf16)
    total = dot_rows(patches[0][3][...], patches[0][5][...]) + dot_rows(
        patches[1][3][...], patches[1][5][...]
    )
    out_ref[:, 3 * LANES :] = total.T.astype(bf16)


def weight_grads(patches):
    features = patches[0][4].shape[1]
    work = 2 * PATCH * features * LANES
    return pl.pallas_call(
        weight_grad_body,
        out_shape=whole((features, 4 * LANES), bf16),
        compiler_params=params(12),
        cost_estimate=cost(8 * work, 12 * PATCH * features),
        name="weight_grads",
    )(*patches[0], *patches[1])


def split_sums(sums):
    high = sums.astype(bf16)
    low = (sums - high.astype(f32)).astype(bf16)
    pad = jnp.zeros((INDEX_ROWS - 2 * sums.shape[0], sums.shape[1]), f32)
    return jnp.concatenate([high.astype(f32), low.astype(f32), pad], axis=0).astype(bf16)


def join_sums(rows):
    rows = rows.astype(f32)
    return rows[0:2] + rows[2:4]


def partial_body(
    column_ref,
    d_query_ref,
    d_key_ref,
    d_value_ref,
    query_ref,
    key_ref,
    value_ref,
    weight_ref,
    mine_ref,
    other_ref,
    sums_ref,
):
    me = column_ref[0]
    d_projected = jnp.concatenate([d_query_ref[...], d_key_ref[...], d_value_ref[...]], axis=0)
    plain = jnp.zeros((1, PATCH), f32)
    for j, mask in enumerate(BLOCK_MASKS):
        start = pl.multiple_of((me ^ mask) * LANES, LANES)
        rows = [weight_ref[t, pl.ds(start, LANES), :] for t in range(3)]
        block = dot(jnp.concatenate(rows, axis=1), d_projected).astype(bf16)
        plain += jnp.sum(block.astype(f32), axis=0, keepdims=True)
        to = mine_ref if j < 2 else other_ref
        to[(j % 2) * LANES : (j % 2 + 1) * LANES, :] = block
    crossed = (
        d_query_ref[...].astype(f32) * (query_ref[...].astype(f32) / score_scale)
        + d_key_ref[...].astype(f32) * key_ref[...].astype(f32)
        + d_value_ref[...].astype(f32) * value_ref[...].astype(f32)
    )
    sums = jnp.concatenate([plain, jnp.sum(crossed, axis=0, keepdims=True)], axis=0)
    sums_ref[...] = sums
    other_ref[2 * LANES :, :] = split_sums(sums)


def hidden_part(d_query, d_key, d_value, query, key, value, weight, column):
    features = weight.shape[1]
    return pl.pallas_call(
        partial_body,
        in_specs=[pl.BlockSpec(memory_space=pltpu.SMEM)] + [pl.BlockSpec(memory_space=pltpu.VMEM)] * 7,
        out_shape=[
            pltpu.VMEM((2 * LANES, PATCH), bf16),
            pltpu.VMEM((2 * LANES + INDEX_ROWS, PATCH), bf16),
            pltpu.VMEM((2, PATCH), f32),
        ],
        compiler_params=params(12),
        cost_estimate=cost(6 * PATCH * features * LANES, 4 * PATCH * features),
        name="hidden_part",
    )(column, d_query, d_key, d_value, query, key, value, weight)


def pair_body(mine_ref, sums_ref, got_ref, kept_ref, sums_out_ref, sent_ref):
    pair = mine_ref[...].astype(f32) + got_ref[: 2 * LANES, :].astype(f32)
    sums = sums_ref[...] + join_sums(got_ref[2 * LANES :, :])
    kept_ref[...] = pair[:LANES]
    sums_out_ref[...] = sums
    sent_ref[:LANES, :] = pair[LANES:].astype(bf16)
    sent_ref[LANES:, :] = split_sums(sums)


def pair_sum(mine, sums, got):
    return pl.pallas_call(
        pair_body,
        out_shape=[
            pltpu.VMEM((LANES, PATCH), f32),
            pltpu.VMEM((2, PATCH), f32),
            pltpu.VMEM((LANES + INDEX_ROWS, PATCH), bf16),
        ],
        compiler_params=params(6),
        cost_estimate=cost(4 * LANES * PATCH, 16 * LANES * PATCH),
        name="pair_sum",
    )(mine, sums, got)


def points_body(kept_ref, sums_ref, got_ref, d_out_ref, normed_ref, inv_ref, *rest):
    out_ref = rest[-1]
    features = 4.0 * LANES
    means = (sums_ref[...] + join_sums(got_ref[LANES:, :])) / features
    d_hidden = kept_ref[...] + got_ref[:LANES, :].astype(f32) - means[0:1]
    inner = d_hidden - normed_ref[...] * means[1:2]
    out_ref[...] = (d_out_ref[...].astype(f32) + inv_ref[0:1] * inner).T


def points_grad(patch, patches, kept, sums, got, d_out, normed, inv_scale, before):
    full = lambda a: pl.BlockSpec(a.shape, lambda i: (0, 0))
    in_specs = [full(kept), full(sums), full(got), pl.BlockSpec((LANES, PATCH), lambda i: (0, patch))]
    in_specs += [full(normed), full(inv_scale)]
    operands = [kept, sums, got, d_out, normed, inv_scale]
    if before is not None:
        in_specs.append(pl.BlockSpec(memory_space=pl.ANY))
        operands.append(before)
    return pl.pallas_call(
        points_body,
        grid=(1,),
        in_specs=in_specs,
        out_specs=pl.BlockSpec((PATCH, LANES), lambda i: (patch, 0)),
        out_shape=whole((patches * PATCH, LANES), f32),
        input_output_aliases={} if before is None else {len(operands) - 1: 0},
        compiler_params=params(8),
        cost_estimate=cost(8 * LANES * PATCH, 24 * LANES * PATCH),
        name="points_grad",
    )(*operands)


def grad_sum_body(parts_ref, qkv_ref, out_ref):
    total = parts_ref[0].astype(f32)
    for j in range(1, parts_ref.shape[0]):
        total += parts_ref[j].astype(f32)
    for t in range(3):
        qkv_ref[t] = total[:, t * LANES : (t + 1) * LANES]
    out_ref[...] = total[:, 3 * LANES :]


def grad_sum(parts):
    shards, rows, width = parts.shape
    return pl.pallas_call(
        grad_sum_body,
        out_shape=[whole((3, rows, LANES), f32), whole((rows, LANES), f32)],
        compiler_params=params(8),
        cost_estimate=cost(shards * rows * width, 4 * shards * rows * width),
        name="grad_sum",
    )(parts)


def local(
    scan_points,
    send_order,
    arrive_order,
    qkv_weight,
    out_weight,
    voxel_grads,
    voxel_shard,
    voxel_point,
):
    shards = lax.axis_size("seq")
    members = lax.axis_size("mp")
    local_rows, features = scan_points.shape
    voxels = voxel_grads.shape[0]
    capacity = 2 * voxels // shards
    patches = local_rows // PATCH
    column = lax.axis_index("mp").astype(i32).reshape(1)
    zero = jnp.zeros((1,), i32)
    weight = qkv_weight.transpose(1, 0, 2)

    def swap(rows, mask):
        return lax.ppermute(rows, "mp", [(i, i ^ mask) for i in range(members)])

    def exchange(rows):
        return lax.all_to_all(rows, "seq", split_axis=0, concat_axis=0, tiled=True)

    def after(value, first):
        return lax.optimization_barrier((value, first))

    def in_hbm(value):
        return pltpu.with_memory_space_constraint(value, pltpu.HBM)

    arrived = exchange(permute_rows(scan_points, send_order, column, 0, 1, whole, 60))
    buckets = bucket_rows(voxel_grads, voxel_shard, voxel_point, column, shards, capacity)
    got = exchange(buckets.reshape(shards * (capacity + INDEX_ROWS), LANES))
    owns = [
        permute_rows(arrived, arrive_order, zero, p, patches, pltpu.VMEM, 8)
        for p in range(patches)
    ]
    across = [swap(own, 2) for own in owns]
    across[0], owns[1] = after(across[0], owns[1])

    def forward(p):
        columns = (owns[p], across[p], swap(owns[p], 1), swap(across[p], 1))
        projected = project(columns, weight, column)
        return projected, attention_forward(projected[3], projected[4], *projected[6:])

    projected0, forward0 = forward(0)
    (got, across[1]), forward0 = after((got, across[1]), forward0)
    summed_rows = segment_rows(got.reshape(shards, capacity + INDEX_ROWS, LANES), local_rows)
    summed_across = swap(summed_rows, 2)
    across[1], summed_rows = after(across[1], summed_rows)
    projected1, forward1 = forward(1)
    summed_across, forward1 = after(summed_across, forward1)
    grads = (summed_rows, summed_across, swap(summed_rows, 1), swap(summed_across, 1))
    forwards = [(projected0, forward0), (projected1, forward1)]

    kept, sums, received, grad_parts = [], [], [], []
    for p in range(patches):
        (hidden, _, _, _, _, query_t, key_t, value_t), (weights, attended, inverse, covariance) = forwards[p]
        if p > 0:
            weights, sent = after(weights, sent)
            received.append(swap(sent, 2))
        d_out, d_query, d_key, d_value = attention_backward(
            p, weights, inverse, covariance, query_t, value_t, attended, grads, out_weight, column
        )
        if p > 0:
            received[p - 1], d_query = after(received[p - 1], d_query)
        grad_parts.append((d_query, d_key, d_value, attended, hidden, d_out))
        if p == patches - 1:
            weight_parts = weight_grads(grad_parts)
            (d_query, d_key, d_value, query_t, key_t, value_t), weight_parts = after(
                (d_query, d_key, d_value, query_t, key_t, value_t), weight_parts
            )
            d_query, d_key, d_value, query_t, key_t, value_t = map(
                in_hbm, (d_query, d_key, d_value, query_t, key_t, value_t)
            )
        mine, other, own_sums = hidden_part(d_query, d_key, d_value, query_t, key_t, value_t, weight, column)
        partner = swap(other, 1)
        keep, pair_sums, sent = pair_sum(mine, own_sums, partner)
        kept.append(keep)
        sums.append(pair_sums)
    received.append(swap(sent, 2))
    d_points = None
    for p in range(patches):
        normed, inv_scale = map(in_hbm, forwards[p][0][1:3])
        d_points = points_grad(
            p, patches, kept[p], sums[p], received[p], grads[0], normed, inv_scale, d_points
        )
    parts = exchange(weight_parts).reshape(shards, features // shards, 4 * LANES)
    grad_qkv, grad_out = grad_sum(parts)
    return (d_points, grad_qkv.transpose(1, 0, 2), grad_out)


def solution(mesh):
    in_specs = (
        P("seq", None),
        P("seq"),
        P("seq"),
        P(None, None, "mp"),
        P(None, "mp"),
        P("seq", None),
        P("seq", None),
        P("seq"),
    )
    out_specs = (P("seq", "mp"), P("seq", None, "mp"), P("seq", "mp"))
    return jax.shard_map(local, mesh=mesh, in_specs=in_specs, out_specs=out_specs, check_vma=False)
```

```python
import functools

import jax
import jax.numpy as jnp
from jax import lax
from jax.experimental import pallas as pl
from jax.experimental.pallas import tpu as pltpu
from jax.sharding import PartitionSpec as P

HD = 16
PATCH = 1024
LANES = 128
INDEX_ROWS = 16
INDEX_BASE = 64
BLOCK_MASKS = (0, 2, 1, 3)
SAFE_SCORE = 60.0
SEGMENT_SHARDS = 4
BUCKET_SHARDS = 2

score_scale = 0.25
epsilon = 1e-05
log2_e = 1.4426950408889634

f32 = jnp.float32
bf16 = jnp.bfloat16
i32 = jnp.int32

ROWS_BY_ROWS = (((1,), (1,)), ((), ()))


def params(mib):
    return pltpu.CompilerParams(vmem_limit_bytes=mib << 20)


def cost(flops, bytes_accessed, transcendentals=0):
    return pl.CostEstimate(
        flops=int(flops), bytes_accessed=int(bytes_accessed), transcendentals=int(transcendentals)
    )


def dot(a, b):
    return jnp.dot(a, b, preferred_element_type=f32)


def dot_rows(a, b):
    return lax.dot_general(a, b, ROWS_BY_ROWS, preferred_element_type=f32)


def ones_where(mask):
    return jnp.where(mask, 1.0, 0.0).astype(bf16)


def permute_body(column_ref, order_ref, block_ref, out_ref):
    step = pl.program_id(0)
    half = block_ref.shape[0] // 2
    chunks = out_ref.shape[0] // LANES
    lane = lax.broadcasted_iota(i32, (LANES, LANES), 1)
    sides = jnp.concatenate([block_ref[:half, :], block_ref[half:, :]], axis=1)
    onehots, lows = [], []
    for j in range(chunks):
        wanted = order_ref[pl.ds(step * chunks + j, 1), :].astype(f32)
        wanted = jnp.broadcast_to(wanted, (LANES, LANES)).T.astype(i32)
        low = wanted < half
        local_row = jnp.where(low, wanted, wanted - half)
        onehots.append(
            jnp.concatenate(
                [ones_where(local_row == lane + k * LANES) for k in range(half // LANES)], axis=1
            )
        )
        lows.append(low)
    both = dot(jnp.concatenate(onehots, axis=0), sides)
    for j in range(chunks):
        rows = slice(j * LANES, (j + 1) * LANES)
        out_ref[rows, :] = jnp.where(lows[j], both[rows, :LANES], both[rows, LANES:]).astype(bf16)


def permute_rows(rows, order, column, part, parts, out, mib):
    row_count = order.shape[0] // parts
    groups = row_count // LANES
    step_rows = min(1024, row_count)
    return pl.pallas_call(
        permute_body,
        grid_spec=pltpu.PrefetchScalarGridSpec(
            num_scalar_prefetch=1,
            grid=(row_count // step_rows,),
            in_specs=[
                pl.BlockSpec((groups, LANES), lambda i, c: (part, 0)),
                pl.BlockSpec((rows.shape[0], LANES), lambda i, c: (0, c[0])),
            ],
            out_specs=pl.BlockSpec((step_rows, LANES), lambda i, c: (i, 0)),
        ),
        out_shape=out((row_count, LANES), bf16),
        compiler_params=params(mib),
        cost_estimate=cost(2 * row_count * row_count * LANES * 4, 3 * row_count * LANES * 2),
        name="permute_rows",
    )(column, order.reshape(parts * groups, LANES), rows)


def bucket_body(shards, capacity, column_ref, shard_ref, point_ref, grads_ref, out_ref, place_ref):
    step = pl.program_id(0)
    row_count = grads_ref.shape[0]
    groups = row_count // LANES

    @pl.when(step == 0)
    def _():
        targets = shard_ref[...]
        masks = [ones_where(targets == t) for t in range(shards)]
        stacked = jnp.concatenate(masks, axis=0)
        above = ones_where(
            lax.broadcasted_iota(i32, (LANES, LANES), 0)
            < lax.broadcasted_iota(i32, (LANES, LANES), 1)
        )
        earlier = ones_where(
            lax.broadcasted_iota(i32, (groups, groups), 1)
            < lax.broadcasted_iota(i32, (groups, groups), 0)
        )
        in_row = dot(stacked, above)
        places = jnp.zeros((groups, LANES), f32)
        for t in range(shards):
            rows_before = jnp.sum(dot(earlier, masks[t]), axis=1, keepdims=True)
            place = in_row[t * groups : (t + 1) * groups] + rows_before + float(t * capacity)
            places = jnp.where(targets == t, place, places)
        place_ref[...] = places.astype(i32)

    points = jnp.concatenate([point_ref[j : j + 1, :] for j in range(groups)], axis=1)
    high = points // INDEX_BASE
    low = points - high * INDEX_BASE
    digits = jnp.concatenate(
        [high.astype(f32), low.astype(f32), jnp.zeros((INDEX_ROWS - 2, row_count), f32)], axis=0
    )
    group = out_ref.shape[0]
    chunks = capacity // LANES
    slot = lax.broadcasted_iota(i32, (group * capacity, LANES), 0) + step * (group * capacity)
    onehot = jnp.concatenate(
        [ones_where(place_ref[j : j + 1, :] == slot) for j in range(groups)], axis=1
    )
    filled = dot(onehot, grads_ref[...]).astype(bf16)
    sent = dot_rows(digits.astype(bf16), onehot)
    for shard in range(group):
        start = shard * capacity
        out_ref[shard, :capacity, :] = filled[start : start + capacity]
        rows = [
            sent[d : d + 1, start + j * LANES : start + (j + 1) * LANES]
            for d in range(2)
            for j in range(chunks)
        ]
        rows.append(jnp.zeros((INDEX_ROWS - 2 * chunks, LANES), f32))
        out_ref[shard, capacity:, :] = jnp.concatenate(rows, axis=0).astype(bf16)


def bucket_rows(grads, targets, points, column, shards, capacity):
    row_count = grads.shape[0]
    groups = row_count // LANES
    group = BUCKET_SHARDS if shards % BUCKET_SHARDS == 0 else 1
    return pl.pallas_call(
        functools.partial(bucket_body, shards, capacity),
        grid_spec=pltpu.PrefetchScalarGridSpec(
            num_scalar_prefetch=1,
            grid=(shards // group,),
            in_specs=[
                pl.BlockSpec((groups, LANES), lambda i, c: (0, 0)),
                pl.BlockSpec((groups, LANES), lambda i, c: (0, 0)),
                pl.BlockSpec((row_count, LANES), lambda i, c: (0, c[0])),
            ],
            out_specs=pl.BlockSpec((group, capacity + INDEX_ROWS, LANES), lambda i, c: (i, 0, 0)),
            scratch_shapes=[pltpu.VMEM((groups, LANES), i32)],
        ),
        out_shape=jax.ShapeDtypeStruct((shards, capacity + INDEX_ROWS, LANES), bf16),
        compiler_params=params(60),
        cost_estimate=cost(
            8 * shards * capacity * row_count * LANES, 3 * shards * capacity * LANES * 2
        ),
        name="bucket_rows",
    )(column, targets.reshape(groups, LANES), points.reshape(groups, LANES), grads)


def segment_body(got_ref, out_ref, total_ref):
    step = pl.program_id(0)
    capacity = got_ref.shape[1] - INDEX_ROWS
    chunks = capacity // LANES
    half = total_ref.shape[0]
    row = lax.broadcasted_iota(i32, (half, LANES), 0)
    onehots, sides = [], []
    for shard in range(got_ref.shape[0]):
        digits = got_ref[shard, capacity:, :].astype(f32)
        index = digits[:chunks] * float(INDEX_BASE) + digits[chunks : 2 * chunks]
        position = index.astype(i32)
        local_row = jnp.where(position < half, position, position - half)
        for j in range(chunks):
            onehots.append(ones_where(local_row[j : j + 1] == row))
            low = jnp.broadcast_to(index[j : j + 1], (LANES, LANES)).T < float(half)
            rows = got_ref[shard, j * LANES : (j + 1) * LANES, :].astype(f32)
            both = [jnp.where(low, rows, 0.0), jnp.where(low, 0.0, rows)]
            sides.append(jnp.concatenate(both, axis=1).astype(bf16))
    part = dot(jnp.concatenate(onehots, axis=1), jnp.concatenate(sides, axis=0))

    @pl.when(step == 0)
    def _():
        total_ref[...] = part

    @pl.when(step > 0)
    def _():
        total_ref[...] += part

    @pl.when(step == pl.num_programs(0) - 1)
    def _():
        out_ref[:, :half] = total_ref[:, :LANES].T.astype(bf16)
        out_ref[:, half:] = total_ref[:, LANES:].T.astype(bf16)


def segment_rows(got, row_count):
    shards, message, _ = got.shape
    group = SEGMENT_SHARDS if shards % SEGMENT_SHARDS == 0 else 1
    return pl.pallas_call(
        segment_body,
        grid=(shards // group,),
        in_specs=[pl.BlockSpec((group, message, LANES), lambda i: (i, 0, 0))],
        out_specs=pl.BlockSpec((LANES, row_count), lambda i: (0, 0)),
        out_shape=pltpu.VMEM((LANES, row_count), bf16),
        scratch_shapes=[pltpu.VMEM((row_count // 2, 2 * LANES), f32)],
        compiler_params=params(24),
        cost_estimate=cost(
            8 * shards * message * row_count * LANES, 3 * shards * message * LANES * 2
        ),
        name="segment_rows",
    )(got)


def project_body(
    column_ref,
    x0_ref,
    x1_ref,
    x2_ref,
    x3_ref,
    weight_ref,
    hidden_ref,
    normed_ref,
    inv_ref,
    key_ref,
    base2_t_ref,
    query_t_ref,
    key_t_ref,
    value_t_ref,
):
    me = column_ref[0]
    blocks = [r[...].astype(f32) for r in (x0_ref, x1_ref, x2_ref, x3_ref)]
    features = float(LANES * len(blocks))
    mean = jnp.sum(blocks[0] + blocks[1] + (blocks[2] + blocks[3]), axis=1, keepdims=True) / features
    centered = [b - mean for b in blocks]
    squares = [c * c for c in centered]
    var = jnp.sum(squares[0] + squares[1] + (squares[2] + squares[3]), axis=1, keepdims=True) / features
    inv = lax.rsqrt(var + epsilon)
    normed_ref[...] = (centered[0] * inv).T
    inv_ref[...] = jnp.broadcast_to(inv, centered[0].shape).T[:8]
    for block, mask in zip(centered, BLOCK_MASKS):
        at = pl.multiple_of((me ^ mask) * LANES, LANES)
        hidden_ref[:, pl.ds(at, LANES)] = (block * inv).astype(bf16)
    weight = jnp.concatenate([weight_ref[t] for t in range(3)], axis=1)
    projected = dot(hidden_ref[...], weight).astype(bf16)
    key_ref[...] = projected[:, LANES : 2 * LANES]
    query = projected[:, :LANES].astype(f32).T * score_scale
    query_t_ref[...] = query.astype(bf16)
    base2_t_ref[...] = (query * log2_e).astype(bf16)
    key_t_ref[...] = projected[:, LANES : 2 * LANES].astype(f32).T.astype(bf16)
    value_t_ref[...] = projected[:, 2 * LANES :].astype(f32).T.astype(bf16)


def project(blocks, weight, column, space):
    row_count = blocks[0].shape[0]
    step_rows = 512
    features = weight.shape[1]
    width = pl.BlockSpec((step_rows, LANES), lambda i, c: (i, 0))
    tall = pl.BlockSpec((LANES, step_rows), lambda i, c: (0, i))
    normal = lambda t: pltpu.VMEM((row_count, LANES), t)
    turned = pltpu.VMEM((LANES, row_count), bf16)
    return pl.pallas_call(
        project_body,
        grid_spec=pltpu.PrefetchScalarGridSpec(
            num_scalar_prefetch=1,
            grid=(row_count // step_rows,),
            in_specs=[width] * 4 + [pl.BlockSpec(weight.shape, lambda i, c: (0, 0, 0))],
            out_specs=[
                pl.BlockSpec((step_rows, features), lambda i, c: (i, 0)),
                tall,
                pl.BlockSpec((8, step_rows), lambda i, c: (0, i)),
                width,
            ]
            + [tall] * 4,
        ),
        out_shape=[space((row_count, features), bf16)]
        + [pltpu.HBM((LANES, row_count), f32), pltpu.HBM((8, row_count), f32)]
        + [normal(bf16)]
        + [turned] * 4,
        compiler_params=params(12),
        cost_estimate=cost(4 * row_count * features * 3 * LANES, row_count * LANES * 40),
        name="project",
    )(column, *blocks, weight)


def forward_body(
    key_ref,
    base2_t_ref,
    key_t_ref,
    value_t_ref,
    exp_ref,
    attended_ref,
    inverse_ref,
    covariance_ref,
    safe_ref,
):
    head = pl.program_id(0)
    at = pl.multiple_of(head * HD, HD)

    @pl.when(head == 0)
    def _():
        def largest(ref):
            squares = jnp.square(ref[...].astype(f32)).reshape(LANES // HD, HD, PATCH)
            return jnp.max(jnp.sum(squares, axis=1), axis=1, keepdims=True)

        bound = jnp.max(largest(base2_t_ref) * largest(key_t_ref))
        safe_ref[0] = (bound <= SAFE_SCORE * SAFE_SCORE).astype(i32)

    def attend(shifted):
        in_head = lax.broadcasted_iota(i32, (LANES, 1), 0) // HD == head
        query = jnp.where(in_head, base2_t_ref[...], jnp.zeros((), bf16))
        scores = dot(key_ref[...], query)
        if shifted:
            scores = scores - jnp.max(scores, axis=0, keepdims=True)
        weights = jnp.exp2(scores).astype(bf16)
        exp_ref[0] = weights
        keys = key_t_ref[pl.ds(at, HD), :].astype(f32)
        values = value_t_ref[pl.ds(at, HD), :].astype(f32)
        middle = jnp.mean(values, axis=1, keepdims=True)
        centered = values - middle
        features = [centered[j : j + 1] * keys for j in range(HD)]
        features += [keys, values, jnp.ones((HD, PATCH), f32)]
        sums = dot(jnp.concatenate([f.astype(bf16) for f in features], axis=0), weights)
        inverse = 1.0 / sums[(HD + 2) * HD : (HD + 2) * HD + 1]
        inverse_ref[0] = inverse
        mean_key = sums[HD * HD : (HD + 1) * HD] * inverse
        mean_value = sums[(HD + 1) * HD : (HD + 2) * HD] * inverse
        attended_ref[pl.ds(at, HD), :] = mean_value.astype(bf16)
        offset = mean_value - middle
        for j in range(HD):
            crossed = sums[j * HD : (j + 1) * HD] * inverse - offset[j : j + 1] * mean_key
            covariance_ref[0, j * HD : (j + 1) * HD, :] = crossed.astype(bf16)

    @pl.when(safe_ref[0] == 1)
    def _():
        attend(False)

    @pl.when(safe_ref[0] == 0)
    def _():
        attend(True)


def attention_forward(keys, base2_t, key_t, value_t, space):
    heads = LANES // HD
    tall = pl.BlockSpec((LANES, PATCH), lambda h: (0, 0))
    per_head = lambda h: (h, 0, 0)
    elements = heads * PATCH * PATCH
    return pl.pallas_call(
        forward_body,
        grid=(heads,),
        in_specs=[pl.BlockSpec((PATCH, LANES), lambda h: (0, 0)), tall, tall, tall],
        out_specs=[
            pl.BlockSpec((1, PATCH, PATCH), per_head),
            tall,
            pl.BlockSpec((1, 1, PATCH), per_head),
            pl.BlockSpec((1, HD * HD, PATCH), per_head),
        ],
        out_shape=[
            space((heads, PATCH, PATCH), bf16),
            space((LANES, PATCH), bf16),
            pltpu.VMEM((heads, 1, PATCH), f32),
            space((heads, HD * HD, PATCH), bf16),
        ],
        scratch_shapes=[pltpu.SMEM((1,), i32)],
        compiler_params=params(16),
        cost_estimate=cost(1600 * elements, 2 * elements, elements),
        name="attention_forward",
    )(keys, base2_t, key_t, value_t)


def backward_body(
    column_ref,
    exp_ref,
    inverse_ref,
    covariance_ref,
    query_t_ref,
    value_t_ref,
    attended_ref,
    g0_ref,
    g1_ref,
    g2_ref,
    g3_ref,
    weight_ref,
    d_out_ref,
    d_query_ref,
    d_key_ref,
    d_value_ref,
    d_attended_ref,
    *early,
):
    head = pl.program_id(0)
    at = pl.multiple_of(head * HD, HD)

    def copies(h):
        exp_all_ref, covariance_all_ref, exp_sems, covariance_sems = early
        return (
            pltpu.make_async_copy(exp_ref.at[h], exp_all_ref.at[h], exp_sems.at[h]),
            pltpu.make_async_copy(
                covariance_ref.at[h], covariance_all_ref.at[h], covariance_sems.at[h]
            ),
        )

    @pl.when(head == 0)
    def _():
        for h in range(LANES // HD if early else 0):
            for copy in copies(h):
                copy.start()
        me = column_ref[0]
        for block, mask in zip((g0_ref, g1_ref, g2_ref, g3_ref), BLOCK_MASKS):
            start = pl.multiple_of((me ^ mask) * LANES, LANES)
            d_out_ref[pl.ds(start, LANES), :] = block[...]
        d_attended_ref[...] = dot(weight_ref[...].T, d_out_ref[...]).astype(bf16)

    grads = d_attended_ref[pl.ds(at, HD), :].astype(f32)
    query = query_t_ref[pl.ds(at, HD), :].astype(f32)
    values = value_t_ref[pl.ds(at, HD), :].astype(f32)
    inverse = inverse_ref[0]
    middle = jnp.mean(values, axis=1, keepdims=True)
    centered = values - middle
    offset = attended_ref[pl.ds(at, HD), :].astype(f32) - middle
    scaled = grads * inverse
    delta = jnp.sum(scaled * offset, axis=0, keepdims=True)
    features = [scaled[j : j + 1] * query for j in range(HD)] + [delta * query, scaled]
    if early:
        for copy in copies(head):
            copy.wait()
        weights, covariance = early[0].at[head], early[1].at[head]
    else:
        weights, covariance = exp_ref.at[0], covariance_ref.at[0]
    sums = dot_rows(jnp.concatenate([f.astype(bf16) for f in features], axis=0), weights[...])
    d_value_ref[pl.ds(at, HD), :] = sums[(HD + 1) * HD :].astype(bf16)
    d_key = centered[0:1] * sums[:HD]
    d_query = grads[0:1] * covariance[:HD, :].astype(f32)
    for j in range(1, HD):
        rows = slice(j * HD, (j + 1) * HD)
        d_key += centered[j : j + 1] * sums[rows]
        d_query += grads[j : j + 1] * covariance[rows, :].astype(f32)
    d_key_ref[pl.ds(at, HD), :] = (d_key - sums[HD * HD : (HD + 1) * HD]).astype(bf16)
    d_query_ref[pl.ds(at, HD), :] = (d_query * score_scale).astype(bf16)


def attention_backward(patch, resident, weights, inverse, covariance, query_t, value_t, attended, grads, weight, column):
    features = weight.shape[0]
    heads = LANES // HD
    in_hbm = pl.BlockSpec(memory_space=pltpu.HBM)
    early = [
        pltpu.VMEM((heads, PATCH, PATCH), bf16),
        pltpu.VMEM((heads, HD * HD, PATCH), bf16),
        pltpu.SemaphoreType.DMA((heads,)),
        pltpu.SemaphoreType.DMA((heads,)),
    ]
    tall = pl.BlockSpec((LANES, PATCH), lambda h, c: (0, 0))
    part = pl.BlockSpec((LANES, PATCH), lambda h, c: (0, patch))
    per_head = lambda h, c: (h, 0, 0)
    elements = heads * PATCH * PATCH
    turned = pltpu.VMEM((LANES, PATCH), bf16)
    return pl.pallas_call(
        backward_body,
        grid_spec=pltpu.PrefetchScalarGridSpec(
            num_scalar_prefetch=1,
            grid=(heads,),
            in_specs=[
                pl.BlockSpec((1, PATCH, PATCH), per_head) if resident else in_hbm,
                pl.BlockSpec((1, 1, PATCH), per_head),
                pl.BlockSpec((1, HD * HD, PATCH), per_head) if resident else in_hbm,
                tall,
                tall,
                tall,
                part,
                part,
                part,
                part,
                pl.BlockSpec(weight.shape, lambda h, c: (0, 0)),
            ],
            out_specs=[pl.BlockSpec((features, PATCH), lambda h, c: (0, 0)), tall, tall, tall],
            scratch_shapes=[pltpu.VMEM((LANES, PATCH), bf16)] + ([] if resident else early),
        ),
        out_shape=[pltpu.VMEM((features, PATCH), bf16), turned, turned, turned],
        compiler_params=params(14 if resident else 30),
        cost_estimate=cost(1100 * elements, 2 * elements),
        name="attention_backward",
    )(column, weights, inverse, covariance, query_t, value_t, attended, *grads, weight)


def whole(shape, dtype):
    return jax.ShapeDtypeStruct(shape, dtype)


def weight_grad_body(*refs):
    d_query_ref, d_key_ref, d_value_ref, attended_ref, hidden_ref, d_out_ref, *before, out_ref = refs
    hidden = hidden_ref[...]
    parts = [dot(ref[...], hidden) for ref in (d_query_ref, d_key_ref, d_value_ref)]
    parts.append(dot_rows(attended_ref[...], d_out_ref[...]))
    for t, part in enumerate(parts):
        columns = slice(t * LANES, (t + 1) * LANES)
        if before:
            out_ref[:, columns] = (before[0][columns, :] + part).T.astype(bf16)
        else:
            out_ref[columns, :] = part


def weight_grads(*operands):
    features = operands[4].shape[1]
    work = 2 * PATCH * features * LANES
    last = len(operands) > 6
    return pl.pallas_call(
        weight_grad_body,
        out_shape=whole((features, 4 * LANES), bf16) if last else pltpu.VMEM((4 * LANES, features), f32),
        compiler_params=params(12),
        cost_estimate=cost(4 * work, 12 * PATCH * features),
        name="weight_grads",
    )(*operands)


def split_sums(sums):
    high = sums.astype(bf16)
    low = (sums - high.astype(f32)).astype(bf16)
    pad = jnp.zeros((INDEX_ROWS - 2 * sums.shape[0], sums.shape[1]), f32)
    return jnp.concatenate([high.astype(f32), low.astype(f32), pad], axis=0).astype(bf16)


def join_sums(rows):
    rows = rows.astype(f32)
    return rows[0:2] + rows[2:4]


def partial_body(
    column_ref,
    d_query_ref,
    d_key_ref,
    d_value_ref,
    query_ref,
    key_ref,
    value_ref,
    weight_ref,
    mine_ref,
    other_ref,
    sums_ref,
):
    me = column_ref[0]
    d_projected = jnp.concatenate([d_query_ref[...], d_key_ref[...], d_value_ref[...]], axis=0)
    plain = jnp.zeros((1, PATCH), f32)
    for j, mask in enumerate(BLOCK_MASKS):
        start = pl.multiple_of((me ^ mask) * LANES, LANES)
        rows = [weight_ref[t, pl.ds(start, LANES), :] for t in range(3)]
        block = dot(jnp.concatenate(rows, axis=1), d_projected).astype(bf16)
        plain += jnp.sum(block.astype(f32), axis=0, keepdims=True)
        to = mine_ref if j < 2 else other_ref
        to[(j % 2) * LANES : (j % 2 + 1) * LANES, :] = block
    crossed = (
        d_query_ref[...].astype(f32) * (query_ref[...].astype(f32) / score_scale)
        + d_key_ref[...].astype(f32) * key_ref[...].astype(f32)
        + d_value_ref[...].astype(f32) * value_ref[...].astype(f32)
    )
    sums = jnp.concatenate([plain, jnp.sum(crossed, axis=0, keepdims=True)], axis=0)
    sums_ref[...] = sums
    other_ref[2 * LANES :, :] = split_sums(sums)


def hidden_part(d_query, d_key, d_value, query, key, value, weight, column):
    features = weight.shape[1]
    return pl.pallas_call(
        partial_body,
        in_specs=[pl.BlockSpec(memory_space=pltpu.SMEM)] + [pl.BlockSpec(memory_space=pltpu.VMEM)] * 7,
        out_shape=[
            pltpu.VMEM((2 * LANES, PATCH), bf16),
            pltpu.VMEM((2 * LANES + INDEX_ROWS, PATCH), bf16),
            pltpu.VMEM((2, PATCH), f32),
        ],
        compiler_params=params(12),
        cost_estimate=cost(6 * PATCH * features * LANES, 4 * PATCH * features),
        name="hidden_part",
    )(column, d_query, d_key, d_value, query, key, value, weight)


def pair_body(mine_ref, sums_ref, got_ref, kept_ref, sums_out_ref, sent_ref):
    pair = mine_ref[...].astype(f32) + got_ref[: 2 * LANES, :].astype(f32)
    sums = sums_ref[...] + join_sums(got_ref[2 * LANES :, :])
    kept_ref[...] = pair[:LANES]
    sums_out_ref[...] = sums
    sent_ref[:LANES, :] = pair[LANES:].astype(bf16)
    sent_ref[LANES:, :] = split_sums(sums)


def pair_sum(mine, sums, got):
    return pl.pallas_call(
        pair_body,
        out_shape=[
            pltpu.VMEM((LANES, PATCH), f32),
            pltpu.VMEM((2, PATCH), f32),
            pltpu.VMEM((LANES + INDEX_ROWS, PATCH), bf16),
        ],
        compiler_params=params(6),
        cost_estimate=cost(4 * LANES * PATCH, 16 * LANES * PATCH),
        name="pair_sum",
    )(mine, sums, got)


def points_body(kept_ref, sums_ref, got_ref, d_out_ref, normed_ref, inv_ref, *rest):
    out_ref = rest[-1]
    features = 4.0 * LANES
    means = (sums_ref[...] + join_sums(got_ref[LANES:, :])) / features
    d_hidden = kept_ref[...] + got_ref[:LANES, :].astype(f32) - means[0:1]
    inner = d_hidden - normed_ref[...] * means[1:2]
    out_ref[...] = (d_out_ref[...].astype(f32) + inv_ref[0:1] * inner).T


def points_grad(patch, patches, kept, sums, got, d_out, normed, inv_scale, before):
    full = lambda a: pl.BlockSpec(a.shape, lambda i: (0, 0))
    in_specs = [full(kept), full(sums), full(got), pl.BlockSpec((LANES, PATCH), lambda i: (0, patch))]
    in_specs += [full(normed), full(inv_scale)]
    operands = [kept, sums, got, d_out, normed, inv_scale]
    if before is not None:
        in_specs.append(pl.BlockSpec(memory_space=pl.ANY))
        operands.append(before)
    return pl.pallas_call(
        points_body,
        grid=(1,),
        in_specs=in_specs,
        out_specs=pl.BlockSpec((PATCH, LANES), lambda i: (patch, 0)),
        out_shape=whole((patches * PATCH, LANES), f32),
        input_output_aliases={} if before is None else {len(operands) - 1: 0},
        compiler_params=params(8),
        cost_estimate=cost(8 * LANES * PATCH, 24 * LANES * PATCH),
        name="points_grad",
    )(*operands)


def grad_sum_body(parts_ref, qkv_ref, out_ref):
    total = parts_ref[0].astype(f32)
    for j in range(1, parts_ref.shape[0]):
        total += parts_ref[j].astype(f32)
    for t in range(3):
        qkv_ref[t] = total[:, t * LANES : (t + 1) * LANES]
    out_ref[...] = total[:, 3 * LANES :]


def grad_sum(parts):
    shards, rows, width = parts.shape
    return pl.pallas_call(
        grad_sum_body,
        out_shape=[whole((3, rows, LANES), f32), whole((rows, LANES), f32)],
        compiler_params=params(8),
        cost_estimate=cost(shards * rows * width, 4 * shards * rows * width),
        name="grad_sum",
    )(parts)


def local(
    scan_points,
    send_order,
    arrive_order,
    qkv_weight,
    out_weight,
    voxel_grads,
    voxel_shard,
    voxel_point,
):
    shards = lax.axis_size("seq")
    members = lax.axis_size("mp")
    local_rows, features = scan_points.shape
    voxels = voxel_grads.shape[0]
    capacity = 2 * voxels // shards
    patches = local_rows // PATCH
    column = lax.axis_index("mp").astype(i32).reshape(1)
    zero = jnp.zeros((1,), i32)
    weight = qkv_weight.transpose(1, 0, 2)

    def swap(rows, mask):
        return lax.ppermute(rows, "mp", [(i, i ^ mask) for i in range(members)])

    def exchange(rows):
        return lax.all_to_all(rows, "seq", split_axis=0, concat_axis=0, tiled=True)

    def after(value, first):
        return lax.optimization_barrier((value, first))

    def in_hbm(value):
        return pltpu.with_memory_space_constraint(value, pltpu.HBM)

    arrived = exchange(permute_rows(scan_points, send_order, column, 0, 1, whole, 60))
    buckets = bucket_rows(voxel_grads, voxel_shard, voxel_point, column, shards, capacity)
    got = exchange(buckets.reshape(shards * (capacity + INDEX_ROWS), LANES))
    owns = [
        permute_rows(arrived, arrive_order, zero, p, patches, pltpu.VMEM, 12)
        for p in range(patches)
    ]
    across = [swap(own, 2) for own in owns]
    across[0], owns[1] = after(across[0], owns[1])

    def forward(p):
        columns = (owns[p], across[p], swap(owns[p], 1), swap(across[p], 1))
        space = pltpu.VMEM if p == patches - 1 else pltpu.HBM
        projected = project(columns, weight, column, space)
        return projected, attention_forward(projected[3], projected[4], *projected[6:], space)

    projected0, forward0 = forward(0)
    (got, across[1]), forward0 = after((got, across[1]), forward0)
    summed_rows = segment_rows(got.reshape(shards, capacity + INDEX_ROWS, LANES), local_rows)
    summed_across = swap(summed_rows, 2)
    across[1], summed_rows = after(across[1], summed_rows)
    projected1, forward1 = forward(1)
    summed_across, forward1 = after(summed_across, forward1)
    grads = (summed_rows, summed_across, swap(summed_rows, 1), swap(summed_across, 1))
    forwards = [(projected0, forward0), (projected1, forward1)]

    kept, sums, received = {}, {}, {}
    for p in reversed(range(patches)):
        (hidden, _, _, _, _, query_t, key_t, value_t), (weights, attended, inverse, covariance) = forwards[p]
        if p == 0:
            weights, sent = after(weights, sent)
            received[1] = swap(sent, 2)
            weights, covariance = in_hbm(weights), in_hbm(covariance)
        d_out, d_query, d_key, d_value = attention_backward(
            p, p == patches - 1, weights, inverse, covariance, query_t, value_t, attended, grads,
            out_weight, column,
        )
        if p == 0:
            received[1], d_query = after(received[1], d_query)
        grad_operands = (d_query, d_key, d_value, attended, hidden, d_out)
        if p == 0:
            weight_parts = weight_grads(*grad_operands, first_parts)
            operands = (d_query, d_key, d_value, query_t, key_t, value_t)
            operands, weight_parts = after(operands, weight_parts)
            d_query, d_key, d_value, query_t, key_t, value_t = map(in_hbm, operands)
        mine, other, own_sums = hidden_part(d_query, d_key, d_value, query_t, key_t, value_t, weight, column)
        partner = swap(other, 1)
        if p > 0:
            first_parts = weight_grads(*grad_operands)
            partner, first_parts = after(partner, first_parts)
        kept[p], sums[p], sent = pair_sum(mine, own_sums, partner)
    received[0] = swap(sent, 2)
    d_points = None
    for p in reversed(range(patches)):
        normed, inv_scale = forwards[p][0][1:3]
        if p > 0:
            normed, inv_scale = in_hbm(normed), in_hbm(inv_scale)
        d_points = points_grad(
            p, patches, kept[p], sums[p], received[p], grads[0], normed, inv_scale, d_points
        )
    parts = exchange(weight_parts).reshape(shards, features // shards, 4 * LANES)
    grad_qkv, grad_out = grad_sum(parts)
    return (d_points, grad_qkv.transpose(1, 0, 2), grad_out)


def solution(mesh):
    in_specs = (
        P("seq", None),
        P("seq"),
        P("seq"),
        P(None, None, "mp"),
        P(None, "mp"),
        P("seq", None),
        P("seq", None),
        P("seq"),
    )
    out_specs = (P("seq", "mp"), P("seq", None, "mp"), P("seq", "mp"))
    return jax.shard_map(local, mesh=mesh, in_specs=in_specs, out_specs=out_specs, check_vma=False)
```

```python
import functools

import jax
import jax.numpy as jnp
from jax import lax
from jax.experimental import pallas as pl
from jax.experimental.pallas import tpu as pltpu
from jax.sharding import PartitionSpec as P

HD = 16
PATCH = 1024
LANES = 128
INDEX_ROWS = 16
INDEX_BASE = 64
BLOCK_MASKS = (0, 2, 1, 3)
SAFE_SCORE = 60.0
STAGED_HEADS = 1
SEGMENT_SHARDS = 8
BUCKET_SHARDS = 2

score_scale = 0.25
epsilon = 1e-05
log2_e = 1.4426950408889634

f32 = jnp.float32
bf16 = jnp.bfloat16
i32 = jnp.int32

ROWS_BY_ROWS = (((1,), (1,)), ((), ()))


def params(mib):
    return pltpu.CompilerParams(vmem_limit_bytes=mib << 20)


def cost(flops, bytes_accessed, transcendentals=0):
    return pl.CostEstimate(
        flops=int(flops), bytes_accessed=int(bytes_accessed), transcendentals=int(transcendentals)
    )


def dot(a, b):
    return jnp.dot(a, b, preferred_element_type=f32)


def dot_rows(a, b):
    return lax.dot_general(a, b, ROWS_BY_ROWS, preferred_element_type=f32)


def ones_where(mask):
    return jnp.where(mask, 1.0, 0.0).astype(bf16)


def permute_body(column_ref, order_ref, block_ref, out_ref):
    step = pl.program_id(0)
    half = block_ref.shape[0] // 2
    chunks = out_ref.shape[0] // LANES
    lane = lax.broadcasted_iota(i32, (LANES, LANES), 1)
    sides = jnp.concatenate([block_ref[:half, :], block_ref[half:, :]], axis=1)
    onehots, lows = [], []
    for j in range(chunks):
        wanted = order_ref[pl.ds(step * chunks + j, 1), :].astype(f32)
        wanted = jnp.broadcast_to(wanted, (LANES, LANES)).T.astype(i32)
        low = wanted < half
        local_row = jnp.where(low, wanted, wanted - half)
        onehots.append(
            jnp.concatenate(
                [ones_where(local_row == lane + k * LANES) for k in range(half // LANES)], axis=1
            )
        )
        lows.append(low)
    both = dot(jnp.concatenate(onehots, axis=0), sides)
    for j in range(chunks):
        rows = slice(j * LANES, (j + 1) * LANES)
        out_ref[rows, :] = jnp.where(lows[j], both[rows, :LANES], both[rows, LANES:]).astype(bf16)


def permute_rows(rows, order, column, part, parts, out, mib):
    row_count = order.shape[0] // parts
    groups = row_count // LANES
    step_rows = min(1024, row_count)
    return pl.pallas_call(
        permute_body,
        grid_spec=pltpu.PrefetchScalarGridSpec(
            num_scalar_prefetch=1,
            grid=(row_count // step_rows,),
            in_specs=[
                pl.BlockSpec((groups, LANES), lambda i, c: (part, 0)),
                pl.BlockSpec((rows.shape[0], LANES), lambda i, c: (0, c[0])),
            ],
            out_specs=pl.BlockSpec((step_rows, LANES), lambda i, c: (i, 0)),
        ),
        out_shape=out((row_count, LANES), bf16),
        compiler_params=params(mib),
        cost_estimate=cost(2 * row_count * row_count * LANES * 4, 3 * row_count * LANES * 2),
        name="permute_rows",
    )(column, order.reshape(parts * groups, LANES), rows)


def bucket_body(shards, capacity, column_ref, shard_ref, point_ref, grads_ref, out_ref, place_ref):
    step = pl.program_id(0)
    row_count = grads_ref.shape[0]
    groups = row_count // LANES

    @pl.when(step == 0)
    def _():
        targets = shard_ref[...]
        masks = [ones_where(targets == t) for t in range(shards)]
        stacked = jnp.concatenate(masks, axis=0)
        above = ones_where(
            lax.broadcasted_iota(i32, (LANES, LANES), 0)
            < lax.broadcasted_iota(i32, (LANES, LANES), 1)
        )
        earlier = ones_where(
            lax.broadcasted_iota(i32, (groups, groups), 1)
            < lax.broadcasted_iota(i32, (groups, groups), 0)
        )
        in_row = dot(stacked, above)
        places = jnp.zeros((groups, LANES), f32)
        for t in range(shards):
            rows_before = jnp.sum(dot(earlier, masks[t]), axis=1, keepdims=True)
            place = in_row[t * groups : (t + 1) * groups] + rows_before + float(t * capacity)
            places = jnp.where(targets == t, place, places)
        place_ref[...] = places.astype(i32)

    points = jnp.concatenate([point_ref[j : j + 1, :] for j in range(groups)], axis=1)
    high = points // INDEX_BASE
    low = points - high * INDEX_BASE
    digits = jnp.concatenate(
        [high.astype(f32), low.astype(f32), jnp.zeros((INDEX_ROWS - 2, row_count), f32)], axis=0
    )
    group = out_ref.shape[0]
    chunks = capacity // LANES
    slot = lax.broadcasted_iota(i32, (group * capacity, LANES), 0) + step * (group * capacity)
    onehot = jnp.concatenate(
        [ones_where(place_ref[j : j + 1, :] == slot) for j in range(groups)], axis=1
    )
    filled = dot(onehot, grads_ref[...]).astype(bf16)
    sent = dot_rows(digits.astype(bf16), onehot)
    for shard in range(group):
        start = shard * capacity
        out_ref[shard, :capacity, :] = filled[start : start + capacity]
        rows = [
            sent[d : d + 1, start + j * LANES : start + (j + 1) * LANES]
            for d in range(2)
            for j in range(chunks)
        ]
        rows.append(jnp.zeros((INDEX_ROWS - 2 * chunks, LANES), f32))
        out_ref[shard, capacity:, :] = jnp.concatenate(rows, axis=0).astype(bf16)


def bucket_rows(grads, targets, points, column, shards, capacity):
    row_count = grads.shape[0]
    groups = row_count // LANES
    group = BUCKET_SHARDS if shards % BUCKET_SHARDS == 0 else 1
    return pl.pallas_call(
        functools.partial(bucket_body, shards, capacity),
        grid_spec=pltpu.PrefetchScalarGridSpec(
            num_scalar_prefetch=1,
            grid=(shards // group,),
            in_specs=[
                pl.BlockSpec((groups, LANES), lambda i, c: (0, 0)),
                pl.BlockSpec((groups, LANES), lambda i, c: (0, 0)),
                pl.BlockSpec((row_count, LANES), lambda i, c: (0, c[0])),
            ],
            out_specs=pl.BlockSpec((group, capacity + INDEX_ROWS, LANES), lambda i, c: (i, 0, 0)),
            scratch_shapes=[pltpu.VMEM((groups, LANES), i32)],
        ),
        out_shape=jax.ShapeDtypeStruct((shards, capacity + INDEX_ROWS, LANES), bf16),
        compiler_params=params(60),
        cost_estimate=cost(
            8 * shards * capacity * row_count * LANES, 3 * shards * capacity * LANES * 2
        ),
        name="bucket_rows",
    )(column, targets.reshape(groups, LANES), points.reshape(groups, LANES), grads)


def segment_body(got_ref, out_ref, total_ref):
    step = pl.program_id(0)
    capacity = got_ref.shape[1] - INDEX_ROWS
    chunks = capacity // LANES
    half = total_ref.shape[0]
    row = lax.broadcasted_iota(i32, (half, LANES), 0)
    onehots, sides = [], []
    for shard in range(got_ref.shape[0]):
        digits = got_ref[shard, capacity:, :].astype(f32)
        index = digits[:chunks] * float(INDEX_BASE) + digits[chunks : 2 * chunks]
        position = index.astype(i32)
        local_row = jnp.where(position < half, position, position - half)
        for j in range(chunks):
            onehots.append(ones_where(local_row[j : j + 1] == row))
            low = jnp.broadcast_to(index[j : j + 1], (LANES, LANES)).T < float(half)
            rows = got_ref[shard, j * LANES : (j + 1) * LANES, :].astype(f32)
            both = [jnp.where(low, rows, 0.0), jnp.where(low, 0.0, rows)]
            sides.append(jnp.concatenate(both, axis=1).astype(bf16))
    part = dot(jnp.concatenate(onehots, axis=1), jnp.concatenate(sides, axis=0))

    @pl.when(step == 0)
    def _():
        total_ref[...] = part

    @pl.when(step > 0)
    def _():
        total_ref[...] += part

    @pl.when(step == pl.num_programs(0) - 1)
    def _():
        out_ref[:, :half] = total_ref[:, :LANES].T.astype(bf16)
        out_ref[:, half:] = total_ref[:, LANES:].T.astype(bf16)


def segment_rows(got, row_count):
    shards, message, _ = got.shape
    group = SEGMENT_SHARDS if shards % SEGMENT_SHARDS == 0 else 1
    return pl.pallas_call(
        segment_body,
        grid=(shards // group,),
        in_specs=[pl.BlockSpec((group, message, LANES), lambda i: (i, 0, 0))],
        out_specs=pl.BlockSpec((LANES, row_count), lambda i: (0, 0)),
        out_shape=pltpu.VMEM((LANES, row_count), bf16),
        scratch_shapes=[pltpu.VMEM((row_count // 2, 2 * LANES), f32)],
        compiler_params=params(40),
        cost_estimate=cost(
            8 * shards * message * row_count * LANES, 3 * shards * message * LANES * 2
        ),
        name="segment_rows",
    )(got)


def project_body(
    column_ref,
    x0_ref,
    x1_ref,
    x2_ref,
    x3_ref,
    weight_ref,
    hidden_ref,
    normed_ref,
    inv_ref,
    key_ref,
    base2_t_ref,
    query_t_ref,
    key_t_ref,
    value_t_ref,
):
    me = column_ref[0]
    blocks = [r[...].astype(f32) for r in (x0_ref, x1_ref, x2_ref, x3_ref)]
    features = float(LANES * len(blocks))
    mean = jnp.sum(blocks[0] + blocks[1] + (blocks[2] + blocks[3]), axis=1, keepdims=True) / features
    centered = [b - mean for b in blocks]
    squares = [c * c for c in centered]
    var = jnp.sum(squares[0] + squares[1] + (squares[2] + squares[3]), axis=1, keepdims=True) / features
    inv = lax.rsqrt(var + epsilon)
    normed_ref[...] = (centered[0] * inv).T
    inv_ref[...] = jnp.broadcast_to(inv, centered[0].shape).T[:8]
    for block, mask in zip(centered, BLOCK_MASKS):
        at = pl.multiple_of((me ^ mask) * LANES, LANES)
        hidden_ref[:, pl.ds(at, LANES)] = (block * inv).astype(bf16)
    weight = jnp.concatenate([weight_ref[t] for t in range(3)], axis=1)
    projected = dot(hidden_ref[...], weight).astype(bf16)
    key_ref[...] = projected[:, LANES : 2 * LANES]
    query = projected[:, :LANES].astype(f32).T * score_scale
    query_t_ref[...] = query.astype(bf16)
    base2_t_ref[...] = (query * log2_e).astype(bf16)
    key_t_ref[...] = projected[:, LANES : 2 * LANES].astype(f32).T.astype(bf16)
    value_t_ref[...] = projected[:, 2 * LANES :].astype(f32).T.astype(bf16)


def project(blocks, weight, column, space):
    row_count = blocks[0].shape[0]
    step_rows = row_count
    features = weight.shape[1]
    width = pl.BlockSpec((step_rows, LANES), lambda i, c: (i, 0))
    tall = pl.BlockSpec((LANES, step_rows), lambda i, c: (0, i))
    normal = lambda t: pltpu.VMEM((row_count, LANES), t)
    turned = pltpu.VMEM((LANES, row_count), bf16)
    return pl.pallas_call(
        project_body,
        grid_spec=pltpu.PrefetchScalarGridSpec(
            num_scalar_prefetch=1,
            grid=(row_count // step_rows,),
            in_specs=[width] * 4 + [pl.BlockSpec(weight.shape, lambda i, c: (0, 0, 0))],
            out_specs=[
                pl.BlockSpec((step_rows, features), lambda i, c: (i, 0)),
                tall,
                pl.BlockSpec((8, step_rows), lambda i, c: (0, i)),
                width,
            ]
            + [tall] * 4,
        ),
        out_shape=[space((row_count, features), bf16)]
        + [pltpu.HBM((LANES, row_count), f32), pltpu.HBM((8, row_count), f32)]
        + [normal(bf16)]
        + [turned] * 4,
        compiler_params=params(12),
        cost_estimate=cost(4 * row_count * features * 3 * LANES, row_count * LANES * 40),
        name="project",
    )(column, *blocks, weight)


def forward_body(
    key_ref,
    base2_t_ref,
    key_t_ref,
    value_t_ref,
    exp_ref,
    attended_ref,
    inverse_ref,
    covariance_ref,
    safe_ref,
):
    head = pl.program_id(0)
    at = pl.multiple_of(head * HD, HD)

    @pl.when(head == 0)
    def _():
        def largest(ref):
            squares = jnp.square(ref[...].astype(f32)).reshape(LANES // HD, HD, PATCH)
            return jnp.max(jnp.sum(squares, axis=1), axis=1, keepdims=True)

        bound = jnp.max(largest(base2_t_ref) * largest(key_t_ref))
        safe_ref[0] = (bound <= SAFE_SCORE * SAFE_SCORE).astype(i32)

    def attend(shifted):
        in_head = lax.broadcasted_iota(i32, (LANES, 1), 0) // HD == head
        query = jnp.where(in_head, base2_t_ref[...], jnp.zeros((), bf16))
        scores = dot(key_ref[...], query)
        if shifted:
            scores = scores - jnp.max(scores, axis=0, keepdims=True)
        weights = jnp.exp2(scores).astype(bf16)
        exp_ref[0] = weights
        keys = key_t_ref[pl.ds(at, HD), :].astype(f32)
        values = value_t_ref[pl.ds(at, HD), :].astype(f32)
        middle = jnp.mean(values, axis=1, keepdims=True)
        centered = values - middle
        features = [centered[j : j + 1] * keys for j in range(HD)]
        features += [keys, values, jnp.ones((HD, PATCH), f32)]
        sums = dot(jnp.concatenate([f.astype(bf16) for f in features], axis=0), weights)
        inverse = 1.0 / sums[(HD + 2) * HD : (HD + 2) * HD + 1]
        inverse_ref[0] = inverse
        mean_key = sums[HD * HD : (HD + 1) * HD] * inverse
        mean_value = sums[(HD + 1) * HD : (HD + 2) * HD] * inverse
        attended_ref[pl.ds(at, HD), :] = mean_value.astype(bf16)
        offset = mean_value - middle
        for j in range(HD):
            crossed = sums[j * HD : (j + 1) * HD] * inverse - offset[j : j + 1] * mean_key
            covariance_ref[0, j * HD : (j + 1) * HD, :] = crossed.astype(bf16)

    @pl.when(safe_ref[0] == 1)
    def _():
        attend(False)

    @pl.when(safe_ref[0] == 0)
    def _():
        attend(True)


def attention_forward(keys, base2_t, key_t, value_t, space):
    heads = LANES // HD
    tall = pl.BlockSpec((LANES, PATCH), lambda h: (0, 0))
    per_head = lambda h: (h, 0, 0)
    elements = heads * PATCH * PATCH
    return pl.pallas_call(
        forward_body,
        grid=(heads,),
        in_specs=[pl.BlockSpec((PATCH, LANES), lambda h: (0, 0)), tall, tall, tall],
        out_specs=[
            pl.BlockSpec((1, PATCH, PATCH), per_head),
            tall,
            pl.BlockSpec((1, 1, PATCH), per_head),
            pl.BlockSpec((1, HD * HD, PATCH), per_head),
        ],
        out_shape=[
            space((heads, PATCH, PATCH), bf16),
            space((LANES, PATCH), bf16),
            pltpu.VMEM((heads, 1, PATCH), f32),
            space((heads, HD * HD, PATCH), bf16),
        ],
        scratch_shapes=[pltpu.SMEM((1,), i32)],
        compiler_params=params(16),
        cost_estimate=cost(1600 * elements, 2 * elements, elements),
        name="attention_forward",
    )(keys, base2_t, key_t, value_t)


def backward_body(first, *refs):
    (
        column_ref,
        exp_ref,
        inverse_ref,
        query_t_ref,
        value_t_ref,
        attended_ref,
        g0_ref,
        g1_ref,
        g2_ref,
        g3_ref,
        weight_ref,
        covariance_ref,
        *refs,
    ) = refs
    if first:
        later_exp_ref, *refs = refs
    else:
        rest_ref, *refs = refs
    d_out_ref, d_query_ref, d_key_ref, d_value_ref, *refs = refs
    if first:
        staged_ref, d_attended_ref, staged_sem = refs
        staged = pltpu.make_async_copy(
            later_exp_ref.at[pl.ds(0, STAGED_HEADS)], staged_ref, staged_sem
        )
    else:
        d_attended_ref, exp_all_ref, exp_sems, covariance_all_ref, covariance_sems = refs
    head = pl.program_id(0)
    at = pl.multiple_of(head * HD, HD)

    def exp_copy(h):
        return pltpu.make_async_copy(
            rest_ref.at[h + STAGED_HEADS], exp_all_ref.at[h], exp_sems.at[h]
        )

    def covariance_copy(h):
        return pltpu.make_async_copy(
            covariance_ref.at[h], covariance_all_ref.at[h], covariance_sems.at[h]
        )

    @pl.when(head == 0)
    def _():
        if first:
            staged.start()
        else:
            for h in range(LANES // HD):
                if h >= STAGED_HEADS:
                    exp_copy(h - STAGED_HEADS).start()
                covariance_copy(h).start()
        me = column_ref[0]
        for block, mask in zip((g0_ref, g1_ref, g2_ref, g3_ref), BLOCK_MASKS):
            start = pl.multiple_of((me ^ mask) * LANES, LANES)
            d_out_ref[pl.ds(start, LANES), :] = block[...]
        d_attended_ref[...] = dot(weight_ref[...].T, d_out_ref[...]).astype(bf16)

    def one_head(weights):
        grads = d_attended_ref[pl.ds(at, HD), :].astype(f32)
        query = query_t_ref[pl.ds(at, HD), :].astype(f32)
        values = value_t_ref[pl.ds(at, HD), :].astype(f32)
        inverse = inverse_ref[0]
        middle = jnp.mean(values, axis=1, keepdims=True)
        centered = values - middle
        offset = attended_ref[pl.ds(at, HD), :].astype(f32) - middle
        scaled = grads * inverse
        delta = jnp.sum(scaled * offset, axis=0, keepdims=True)
        features = [scaled[j : j + 1] * query for j in range(HD)] + [delta * query, scaled]
        sums = dot_rows(jnp.concatenate([f.astype(bf16) for f in features], axis=0), weights())
        d_value_ref[pl.ds(at, HD), :] = sums[(HD + 1) * HD :].astype(bf16)
        if first:
            covariance = covariance_ref.at[0]
        else:
            covariance_copy(head).wait()
            covariance = covariance_all_ref.at[head]
        d_key = centered[0:1] * sums[:HD]
        d_query = grads[0:1] * covariance[:HD, :].astype(f32)
        for j in range(1, HD):
            rows = slice(j * HD, (j + 1) * HD)
            d_key += centered[j : j + 1] * sums[rows]
            d_query += grads[j : j + 1] * covariance[rows, :].astype(f32)
        d_key_ref[pl.ds(at, HD), :] = (d_key - sums[HD * HD : (HD + 1) * HD]).astype(bf16)
        d_query_ref[pl.ds(at, HD), :] = (d_query * score_scale).astype(bf16)

    if first:
        one_head(lambda: exp_ref[0])

        @pl.when(head == pl.num_programs(0) - 1)
        def _():
            staged.wait()

    else:

        @pl.when(head < STAGED_HEADS)
        def _():
            one_head(lambda: exp_ref[0])

        @pl.when(head >= STAGED_HEADS)
        def _():
            exp_copy(head - STAGED_HEADS).wait()
            one_head(lambda: exp_all_ref[head - STAGED_HEADS])


def attention_backward(
    patch, first, weights, other, inverse, covariance, query_t, value_t, attended, grads, weight, column
):
    features = weight.shape[0]
    heads = LANES // HD
    tall = pl.BlockSpec((LANES, PATCH), lambda h, c: (0, 0))
    part = pl.BlockSpec((LANES, PATCH), lambda h, c: (0, patch))
    per_head = lambda h, c: (h, 0, 0)
    kept_head = lambda h, c: (jnp.minimum(h, weights.shape[0] - 1), 0, 0)
    hbm = pl.BlockSpec(memory_space=pltpu.HBM)
    elements = heads * PATCH * PATCH
    turned = pltpu.VMEM((LANES, PATCH), bf16)
    in_specs = [
        pl.BlockSpec((1, PATCH, PATCH), kept_head),
        pl.BlockSpec((1, 1, PATCH), per_head),
        tall,
        tall,
        tall,
        part,
        part,
        part,
        part,
        pl.BlockSpec(weight.shape, lambda h, c: (0, 0)),
        pl.BlockSpec((1, HD * HD, PATCH), per_head) if first else hbm,
        hbm,
    ]
    operands = [weights, inverse, query_t, value_t, attended, *grads, weight, covariance, other]
    out_specs = [pl.BlockSpec((features, PATCH), lambda h, c: (0, 0)), tall, tall, tall]
    out_shape = [pltpu.VMEM((features, PATCH), bf16), turned, turned, turned]
    scratch = [pltpu.VMEM((LANES, PATCH), bf16)]
    if first:
        out_specs.append(pl.BlockSpec(memory_space=pl.ANY))
        out_shape.append(pltpu.VMEM((STAGED_HEADS, PATCH, PATCH), bf16))
        scratch.append(pltpu.SemaphoreType.DMA(()))
    else:
        rest = heads - STAGED_HEADS
        scratch += [pltpu.VMEM((rest, PATCH, PATCH), bf16), pltpu.SemaphoreType.DMA((rest,))]
        scratch += [pltpu.VMEM((heads, HD * HD, PATCH), bf16), pltpu.SemaphoreType.DMA((heads,))]
    return pl.pallas_call(
        functools.partial(backward_body, first),
        grid_spec=pltpu.PrefetchScalarGridSpec(
            num_scalar_prefetch=1,
            grid=(heads,),
            in_specs=in_specs,
            out_specs=out_specs,
            scratch_shapes=scratch,
        ),
        out_shape=out_shape,
        compiler_params=params(9 if first else 27),
        cost_estimate=cost(1100 * elements, 2 * elements),
        name="attention_backward",
    )(column, *operands)


def whole(shape, dtype):
    return jax.ShapeDtypeStruct(shape, dtype)


def weight_grad_body(*refs):
    d_query_ref, d_key_ref, d_value_ref, attended_ref, hidden_ref, d_out_ref, *before, out_ref = refs
    d_projected = jnp.concatenate([d_query_ref[...], d_key_ref[...], d_value_ref[...]], axis=0)
    projections = dot(d_projected, hidden_ref[...])
    output = dot_rows(attended_ref[...], d_out_ref[...])
    if before:
        out_ref[:, : 3 * LANES] = (before[0][: 3 * LANES, :] + projections).T.astype(bf16)
        out_ref[:, 3 * LANES :] = (before[0][3 * LANES :, :] + output).T.astype(bf16)
    else:
        out_ref[: 3 * LANES, :] = projections
        out_ref[3 * LANES :, :] = output


def weight_grads(*operands):
    features = operands[4].shape[1]
    work = 2 * PATCH * features * LANES
    last = len(operands) > 6
    return pl.pallas_call(
        weight_grad_body,
        out_shape=whole((features, 4 * LANES), bf16) if last else pltpu.VMEM((4 * LANES, features), f32),
        compiler_params=params(12),
        cost_estimate=cost(4 * work, 12 * PATCH * features),
        name="weight_grads",
    )(*operands)


def split_sums(sums):
    high = sums.astype(bf16)
    low = (sums - high.astype(f32)).astype(bf16)
    pad = jnp.zeros((INDEX_ROWS - 2 * sums.shape[0], sums.shape[1]), f32)
    return jnp.concatenate([high.astype(f32), low.astype(f32), pad], axis=0).astype(bf16)


def join_sums(rows):
    rows = rows.astype(f32)
    return rows[0:2] + rows[2:4]


def partial_body(
    column_ref,
    d_query_ref,
    d_key_ref,
    d_value_ref,
    query_ref,
    key_ref,
    value_ref,
    weight_ref,
    mine_ref,
    other_ref,
    sums_ref,
):
    me = column_ref[0]
    d_projected = jnp.concatenate([d_query_ref[...], d_key_ref[...], d_value_ref[...]], axis=0)
    plain = jnp.zeros((1, PATCH), f32)
    for j, mask in enumerate(BLOCK_MASKS):
        start = pl.multiple_of((me ^ mask) * LANES, LANES)
        rows = [weight_ref[t, pl.ds(start, LANES), :] for t in range(3)]
        block = dot(jnp.concatenate(rows, axis=1), d_projected).astype(bf16)
        plain += jnp.sum(block.astype(f32), axis=0, keepdims=True)
        to = mine_ref if j < 2 else other_ref
        to[(j % 2) * LANES : (j % 2 + 1) * LANES, :] = block
    crossed = (
        d_query_ref[...].astype(f32) * (query_ref[...].astype(f32) / score_scale)
        + d_key_ref[...].astype(f32) * key_ref[...].astype(f32)
        + d_value_ref[...].astype(f32) * value_ref[...].astype(f32)
    )
    sums = jnp.concatenate([plain, jnp.sum(crossed, axis=0, keepdims=True)], axis=0)
    sums_ref[...] = sums
    other_ref[2 * LANES :, :] = split_sums(sums)


def hidden_part(d_query, d_key, d_value, query, key, value, weight, column):
    features = weight.shape[1]
    return pl.pallas_call(
        partial_body,
        in_specs=[pl.BlockSpec(memory_space=pltpu.SMEM)] + [pl.BlockSpec(memory_space=pltpu.VMEM)] * 7,
        out_shape=[
            pltpu.VMEM((2 * LANES, PATCH), bf16),
            pltpu.VMEM((2 * LANES + INDEX_ROWS, PATCH), bf16),
            pltpu.VMEM((2, PATCH), f32),
        ],
        compiler_params=params(12),
        cost_estimate=cost(6 * PATCH * features * LANES, 4 * PATCH * features),
        name="hidden_part",
    )(column, d_query, d_key, d_value, query, key, value, weight)


def pair_body(mine_ref, sums_ref, got_ref, kept_ref, sums_out_ref, sent_ref):
    pair = mine_ref[...].astype(f32) + got_ref[: 2 * LANES, :].astype(f32)
    sums = sums_ref[...] + join_sums(got_ref[2 * LANES :, :])
    kept_ref[...] = pair[:LANES]
    sums_out_ref[...] = sums
    sent_ref[:LANES, :] = pair[LANES:].astype(bf16)
    sent_ref[LANES:, :] = split_sums(sums)


def pair_sum(mine, sums, got):
    return pl.pallas_call(
        pair_body,
        out_shape=[
            pltpu.VMEM((LANES, PATCH), f32),
            pltpu.VMEM((2, PATCH), f32),
            pltpu.VMEM((LANES + INDEX_ROWS, PATCH), bf16),
        ],
        compiler_params=params(6),
        cost_estimate=cost(4 * LANES * PATCH, 16 * LANES * PATCH),
        name="pair_sum",
    )(mine, sums, got)


def points_body(kept_ref, sums_ref, got_ref, d_out_ref, normed_ref, inv_ref, *rest):
    out_ref = rest[-1]
    features = 4.0 * LANES
    means = (sums_ref[...] + join_sums(got_ref[LANES:, :])) / features
    d_hidden = kept_ref[...] + got_ref[:LANES, :].astype(f32) - means[0:1]
    inner = d_hidden - normed_ref[...] * means[1:2]
    out_ref[...] = (d_out_ref[...].astype(f32) + inv_ref[0:1] * inner).T


def points_grad(patch, patches, kept, sums, got, d_out, normed, inv_scale, before):
    full = lambda a: pl.BlockSpec(a.shape, lambda i: (0, 0))
    in_specs = [full(kept), full(sums), full(got), pl.BlockSpec((LANES, PATCH), lambda i: (0, patch))]
    in_specs += [full(normed), full(inv_scale)]
    operands = [kept, sums, got, d_out, normed, inv_scale]
    if before is not None:
        in_specs.append(pl.BlockSpec(memory_space=pl.ANY))
        operands.append(before)
    return pl.pallas_call(
        points_body,
        grid=(1,),
        in_specs=in_specs,
        out_specs=pl.BlockSpec((PATCH, LANES), lambda i: (patch, 0)),
        out_shape=whole((patches * PATCH, LANES), f32),
        input_output_aliases={} if before is None else {len(operands) - 1: 0},
        compiler_params=params(8),
        cost_estimate=cost(8 * LANES * PATCH, 24 * LANES * PATCH),
        name="points_grad",
    )(*operands)


def grad_sum_body(parts_ref, qkv_ref, out_ref):
    total = parts_ref[0].astype(f32)
    for j in range(1, parts_ref.shape[0]):
        total += parts_ref[j].astype(f32)
    for t in range(3):
        qkv_ref[t] = total[:, t * LANES : (t + 1) * LANES]
    out_ref[...] = total[:, 3 * LANES :]


def grad_sum(parts):
    shards, rows, width = parts.shape
    return pl.pallas_call(
        grad_sum_body,
        out_shape=[whole((3, rows, LANES), f32), whole((rows, LANES), f32)],
        compiler_params=params(8),
        cost_estimate=cost(shards * rows * width, 4 * shards * rows * width),
        name="grad_sum",
    )(parts)


def local(
    scan_points,
    send_order,
    arrive_order,
    qkv_weight,
    out_weight,
    voxel_grads,
    voxel_shard,
    voxel_point,
):
    shards = lax.axis_size("seq")
    members = lax.axis_size("mp")
    local_rows, features = scan_points.shape
    voxels = voxel_grads.shape[0]
    capacity = 2 * voxels // shards
    patches = local_rows // PATCH
    column = lax.axis_index("mp").astype(i32).reshape(1)
    zero = jnp.zeros((1,), i32)
    weight = qkv_weight.transpose(1, 0, 2)

    def swap(rows, mask):
        return lax.ppermute(rows, "mp", [(i, i ^ mask) for i in range(members)])

    def exchange(rows):
        return lax.all_to_all(rows, "seq", split_axis=0, concat_axis=0, tiled=True)

    def after(value, first):
        return lax.optimization_barrier((value, first))

    def in_hbm(value):
        return pltpu.with_memory_space_constraint(value, pltpu.HBM)

    arrived = exchange(permute_rows(scan_points, send_order, column, 0, 1, whole, 60))
    buckets = bucket_rows(voxel_grads, voxel_shard, voxel_point, column, shards, capacity)
    got = exchange(buckets.reshape(shards * (capacity + INDEX_ROWS), LANES))
    owns = [
        permute_rows(arrived, arrive_order, zero, p, patches, pltpu.VMEM, 12)
        for p in range(patches)
    ]
    across = [swap(own, 2) for own in owns]
    across[0], owns[1] = after(across[0], owns[1])

    def forward(p):
        columns = (owns[p], across[p], swap(owns[p], 1), swap(across[p], 1))
        space = pltpu.VMEM if p == patches - 1 else pltpu.HBM
        projected = project(columns, weight, column, space)
        return projected, attention_forward(projected[3], projected[4], *projected[6:], space)

    projected0, forward0 = forward(0)
    (got, across[1]), forward0 = after((got, across[1]), forward0)
    summed_rows = segment_rows(got.reshape(shards, capacity + INDEX_ROWS, LANES), local_rows)
    summed_across = swap(summed_rows, 2)
    across[1], summed_rows = after(across[1], summed_rows)
    projected1, forward1 = forward(1)
    summed_across, forward1 = after(summed_across, forward1)
    grads = (summed_rows, summed_across, swap(summed_rows, 1), swap(summed_across, 1))
    forwards = [(projected0, forward0), (projected1, forward1)]

    kept, sums, received = {}, {}, {}
    for p in reversed(range(patches)):
        (hidden, _, _, _, _, query_t, key_t, value_t), (weights, attended, inverse, covariance) = forwards[p]
        if p == 0:
            weights, sent = after(weights, sent)
            received[1] = swap(sent, 2)
            other_exp, covariance, weights = in_hbm(weights), in_hbm(covariance), staged[0]
        else:
            other_exp = in_hbm(forwards[0][1][0])
        d_out, d_query, d_key, d_value, *staged = attention_backward(
            p, p > 0, weights, other_exp, inverse, covariance, query_t, value_t, attended, grads, out_weight, column
        )
        if p == 0:
            received[1], d_query = after(received[1], d_query)
        grad_operands = (d_query, d_key, d_value, attended, hidden, d_out)
        if p == 0:
            weight_parts = weight_grads(*grad_operands, first_parts)
            operands = (d_query, d_key, d_value, query_t, key_t, value_t)
            operands, weight_parts = after(operands, weight_parts)
            d_query, d_key, d_value, query_t, key_t, value_t = map(in_hbm, operands)
        mine, other, own_sums = hidden_part(d_query, d_key, d_value, query_t, key_t, value_t, weight, column)
        partner = swap(other, 1)
        if p > 0:
            first_parts = weight_grads(*grad_operands)
            partner, first_parts = after(partner, first_parts)
        kept[p], sums[p], sent = pair_sum(mine, own_sums, partner)
    received[0] = swap(sent, 2)
    d_points = None
    for p in reversed(range(patches)):
        normed, inv_scale = forwards[p][0][1:3]
        if p > 0:
            normed, inv_scale = in_hbm(normed), in_hbm(inv_scale)
        d_points = points_grad(
            p, patches, kept[p], sums[p], received[p], grads[0], normed, inv_scale, d_points
        )
    parts = exchange(weight_parts).reshape(shards, features // shards, 4 * LANES)
    grad_qkv, grad_out = grad_sum(parts)
    return (d_points, grad_qkv.transpose(1, 0, 2), grad_out)


def solution(mesh):
    in_specs = (
        P("seq", None),
        P("seq"),
        P("seq"),
        P(None, None, "mp"),
        P(None, "mp"),
        P("seq", None),
        P("seq", None),
        P("seq"),
    )
    out_specs = (P("seq", "mp"), P("seq", None, "mp"), P("seq", "mp"))
    return jax.shard_map(local, mesh=mesh, in_specs=in_specs, out_specs=out_specs, check_vma=False)
```

```python
import functools

import jax
import jax.numpy as jnp
from jax import lax
from jax.experimental import pallas as pl
from jax.experimental.pallas import tpu as pltpu
from jax.sharding import PartitionSpec as P

HD = 16
PATCH = 1024
LANES = 128
INDEX_ROWS = 16
INDEX_BASE = 64
BLOCK_MASKS = (0, 2, 1, 3)
SAFE_SCORE = 60.0
STAGED_HEADS = 1
SEGMENT_SHARDS = 8
BUCKET_SHARDS = 2

score_scale = 0.25
epsilon = 1e-05
log2_e = 1.4426950408889634

f32 = jnp.float32
bf16 = jnp.bfloat16
i32 = jnp.int32

ROWS_BY_ROWS = (((1,), (1,)), ((), ()))


def params(mib):
    return pltpu.CompilerParams(vmem_limit_bytes=mib << 20)


def cost(flops, bytes_accessed, transcendentals=0):
    return pl.CostEstimate(
        flops=int(flops), bytes_accessed=int(bytes_accessed), transcendentals=int(transcendentals)
    )


def dot(a, b):
    return jnp.dot(a, b, preferred_element_type=f32)


def dot_rows(a, b):
    return lax.dot_general(a, b, ROWS_BY_ROWS, preferred_element_type=f32)


def ones_where(mask):
    return jnp.where(mask, 1.0, 0.0).astype(bf16)


def permute_body(column_ref, order_ref, block_ref, out_ref):
    step = pl.program_id(0)
    half = block_ref.shape[0] // 2
    chunks = out_ref.shape[0] // LANES
    lane = lax.broadcasted_iota(i32, (LANES, LANES), 1)
    sides = jnp.concatenate([block_ref[:half, :], block_ref[half:, :]], axis=1)
    onehots, lows = [], []
    for j in range(chunks):
        wanted = order_ref[pl.ds(step * chunks + j, 1), :].astype(f32)
        wanted = jnp.broadcast_to(wanted, (LANES, LANES)).T.astype(i32)
        low = wanted < half
        local_row = jnp.where(low, wanted, wanted - half)
        onehots.append(
            jnp.concatenate(
                [ones_where(local_row == lane + k * LANES) for k in range(half // LANES)], axis=1
            )
        )
        lows.append(low)
    both = dot(jnp.concatenate(onehots, axis=0), sides)
    for j in range(chunks):
        rows = slice(j * LANES, (j + 1) * LANES)
        out_ref[rows, :] = jnp.where(lows[j], both[rows, :LANES], both[rows, LANES:]).astype(bf16)


def permute_rows(rows, order, column, part, parts, out, mib):
    row_count = order.shape[0] // parts
    groups = row_count // LANES
    step_rows = min(1024, row_count)
    return pl.pallas_call(
        permute_body,
        grid_spec=pltpu.PrefetchScalarGridSpec(
            num_scalar_prefetch=1,
            grid=(row_count // step_rows,),
            in_specs=[
                pl.BlockSpec((groups, LANES), lambda i, c: (part, 0)),
                pl.BlockSpec((rows.shape[0], LANES), lambda i, c: (0, c[0])),
            ],
            out_specs=pl.BlockSpec((step_rows, LANES), lambda i, c: (i, 0)),
        ),
        out_shape=out((row_count, LANES), bf16),
        compiler_params=params(mib),
        cost_estimate=cost(2 * row_count * LANES, row_count),
        name="permute_rows",
    )(column, order.reshape(parts * groups, LANES), rows)


def bucket_body(shards, capacity, column_ref, shard_ref, point_ref, grads_ref, out_ref, place_ref):
    step = pl.program_id(0)
    row_count = grads_ref.shape[0]
    groups = row_count // LANES

    @pl.when(step == 0)
    def _():
        targets = shard_ref[...]
        masks = [ones_where(targets == t) for t in range(shards)]
        stacked = jnp.concatenate(masks, axis=0)
        above = ones_where(
            lax.broadcasted_iota(i32, (LANES, LANES), 0)
            < lax.broadcasted_iota(i32, (LANES, LANES), 1)
        )
        earlier = ones_where(
            lax.broadcasted_iota(i32, (groups, groups), 1)
            < lax.broadcasted_iota(i32, (groups, groups), 0)
        )
        in_row = dot(stacked, above)
        places = jnp.zeros((groups, LANES), f32)
        for t in range(shards):
            rows_before = jnp.sum(dot(earlier, masks[t]), axis=1, keepdims=True)
            place = in_row[t * groups : (t + 1) * groups] + rows_before + float(t * capacity)
            places = jnp.where(targets == t, place, places)
        place_ref[...] = places.astype(i32)

    points = jnp.concatenate([point_ref[j : j + 1, :] for j in range(groups)], axis=1)
    high = points // INDEX_BASE
    low = points - high * INDEX_BASE
    digits = jnp.concatenate(
        [high.astype(f32), low.astype(f32), jnp.zeros((INDEX_ROWS - 2, row_count), f32)], axis=0
    )
    group = out_ref.shape[0]
    chunks = capacity // LANES
    slot = lax.broadcasted_iota(i32, (group * capacity, LANES), 0) + step * (group * capacity)
    onehot = jnp.concatenate(
        [ones_where(place_ref[j : j + 1, :] == slot) for j in range(groups)], axis=1
    )
    filled = dot(onehot, grads_ref[...]).astype(bf16)
    sent = dot_rows(digits.astype(bf16), onehot)
    for shard in range(group):
        start = shard * capacity
        out_ref[shard, :capacity, :] = filled[start : start + capacity]
        rows = [
            sent[d : d + 1, start + j * LANES : start + (j + 1) * LANES]
            for d in range(2)
            for j in range(chunks)
        ]
        rows.append(jnp.zeros((INDEX_ROWS - 2 * chunks, LANES), f32))
        out_ref[shard, capacity:, :] = jnp.concatenate(rows, axis=0).astype(bf16)


def bucket_rows(grads, targets, points, column, shards, capacity):
    row_count = grads.shape[0]
    groups = row_count // LANES
    group = BUCKET_SHARDS if shards % BUCKET_SHARDS == 0 else 1
    return pl.pallas_call(
        functools.partial(bucket_body, shards, capacity),
        grid_spec=pltpu.PrefetchScalarGridSpec(
            num_scalar_prefetch=1,
            grid=(shards // group,),
            in_specs=[
                pl.BlockSpec((groups, LANES), lambda i, c: (0, 0)),
                pl.BlockSpec((groups, LANES), lambda i, c: (0, 0)),
                pl.BlockSpec((row_count, LANES), lambda i, c: (0, c[0])),
            ],
            out_specs=pl.BlockSpec((group, capacity + INDEX_ROWS, LANES), lambda i, c: (i, 0, 0)),
            scratch_shapes=[pltpu.VMEM((groups, LANES), i32)],
        ),
        out_shape=jax.ShapeDtypeStruct((shards, capacity + INDEX_ROWS, LANES), bf16),
        compiler_params=params(60),
        cost_estimate=cost(
            8 * shards * capacity * row_count * LANES, 3 * shards * capacity * LANES * 2
        ),
        name="bucket_rows",
    )(column, targets.reshape(groups, LANES), points.reshape(groups, LANES), grads)


def segment_body(got_ref, out_ref, total_ref):
    step = pl.program_id(0)
    capacity = got_ref.shape[1] - INDEX_ROWS
    chunks = capacity // LANES
    half = total_ref.shape[0]
    row = lax.broadcasted_iota(i32, (half, LANES), 0)
    onehots, sides = [], []
    for shard in range(got_ref.shape[0]):
        digits = got_ref[shard, capacity:, :].astype(f32)
        index = digits[:chunks] * float(INDEX_BASE) + digits[chunks : 2 * chunks]
        position = index.astype(i32)
        local_row = jnp.where(position < half, position, position - half)
        for j in range(chunks):
            onehots.append(ones_where(local_row[j : j + 1] == row))
            low = jnp.broadcast_to(index[j : j + 1], (LANES, LANES)).T < float(half)
            rows = got_ref[shard, j * LANES : (j + 1) * LANES, :].astype(f32)
            both = [jnp.where(low, rows, 0.0), jnp.where(low, 0.0, rows)]
            sides.append(jnp.concatenate(both, axis=1).astype(bf16))
    part = dot(jnp.concatenate(onehots, axis=1), jnp.concatenate(sides, axis=0))

    @pl.when(step == 0)
    def _():
        total_ref[...] = part

    @pl.when(step > 0)
    def _():
        total_ref[...] += part

    @pl.when(step == pl.num_programs(0) - 1)
    def _():
        out_ref[:, :half] = total_ref[:, :LANES].T.astype(bf16)
        out_ref[:, half:] = total_ref[:, LANES:].T.astype(bf16)


def segment_rows(got, row_count):
    shards, message, _ = got.shape
    group = SEGMENT_SHARDS if shards % SEGMENT_SHARDS == 0 else 1
    return pl.pallas_call(
        segment_body,
        grid=(shards // group,),
        in_specs=[pl.BlockSpec((group, message, LANES), lambda i: (i, 0, 0))],
        out_specs=pl.BlockSpec((LANES, row_count), lambda i: (0, 0)),
        out_shape=pltpu.VMEM((LANES, row_count), bf16),
        scratch_shapes=[pltpu.VMEM((row_count // 2, 2 * LANES), f32)],
        compiler_params=params(40),
        cost_estimate=cost(
            8 * shards * message * row_count * LANES, 3 * shards * message * LANES * 2
        ),
        name="segment_rows",
    )(got)


def project_body(
    column_ref,
    x0_ref,
    x1_ref,
    x2_ref,
    x3_ref,
    weight_ref,
    hidden_ref,
    normed_ref,
    inv_ref,
    key_ref,
    base2_t_ref,
    query_t_ref,
    key_t_ref,
    value_t_ref,
):
    me = column_ref[0]
    blocks = [r[...].astype(f32) for r in (x0_ref, x1_ref, x2_ref, x3_ref)]
    features = float(LANES * len(blocks))
    mean = jnp.sum(blocks[0] + blocks[1] + (blocks[2] + blocks[3]), axis=1, keepdims=True) / features
    centered = [b - mean for b in blocks]
    squares = [c * c for c in centered]
    var = jnp.sum(squares[0] + squares[1] + (squares[2] + squares[3]), axis=1, keepdims=True) / features
    inv = lax.rsqrt(var + epsilon)
    normed_ref[...] = (centered[0] * inv).T
    inv_ref[...] = jnp.broadcast_to(inv, centered[0].shape).T[:8]
    for block, mask in zip(centered, BLOCK_MASKS):
        at = pl.multiple_of((me ^ mask) * LANES, LANES)
        hidden_ref[:, pl.ds(at, LANES)] = (block * inv).astype(bf16)
    weight = jnp.concatenate([weight_ref[t] for t in range(3)], axis=1)
    projected = dot(hidden_ref[...], weight).astype(bf16)
    key_ref[...] = projected[:, LANES : 2 * LANES]
    query = projected[:, :LANES].astype(f32).T * score_scale
    query_t_ref[...] = query.astype(bf16)
    base2_t_ref[...] = (query * log2_e).astype(bf16)
    key_t_ref[...] = projected[:, LANES : 2 * LANES].astype(f32).T.astype(bf16)
    value_t_ref[...] = projected[:, 2 * LANES :].astype(f32).T.astype(bf16)


def project(blocks, weight, column, hidden_space, space):
    row_count = blocks[0].shape[0]
    step_rows = row_count
    features = weight.shape[1]
    width = pl.BlockSpec((step_rows, LANES), lambda i, c: (i, 0))
    tall = pl.BlockSpec((LANES, step_rows), lambda i, c: (0, i))
    normal = lambda t: space((row_count, LANES), t)
    turned = space((LANES, row_count), bf16)
    return pl.pallas_call(
        project_body,
        grid_spec=pltpu.PrefetchScalarGridSpec(
            num_scalar_prefetch=1,
            grid=(row_count // step_rows,),
            in_specs=[width] * 4 + [pl.BlockSpec(weight.shape, lambda i, c: (0, 0, 0))],
            out_specs=[
                pl.BlockSpec((step_rows, features), lambda i, c: (i, 0)),
                tall,
                pl.BlockSpec((8, step_rows), lambda i, c: (0, i)),
                width,
            ]
            + [tall] * 4,
        ),
        out_shape=[hidden_space((row_count, features), bf16)]
        + [pltpu.HBM((LANES, row_count), f32), pltpu.HBM((8, row_count), f32)]
        + [normal(bf16)]
        + [turned] * 4,
        compiler_params=params(12),
        cost_estimate=cost(4 * row_count * features * 3 * LANES, row_count * LANES * 40),
        name="project",
    )(column, *blocks, weight)


def forward_body(
    key_ref,
    base2_t_ref,
    key_t_ref,
    value_t_ref,
    exp_ref,
    attended_ref,
    inverse_ref,
    covariance_ref,
    safe_ref,
):
    head = pl.program_id(0)
    at = pl.multiple_of(head * HD, HD)

    @pl.when(head == 0)
    def _():
        def largest(ref):
            squares = jnp.square(ref[...].astype(f32)).reshape(LANES // HD, HD, PATCH)
            return jnp.max(jnp.sum(squares, axis=1), axis=1, keepdims=True)

        bound = jnp.max(largest(base2_t_ref) * largest(key_t_ref))
        safe_ref[0] = (bound <= SAFE_SCORE * SAFE_SCORE).astype(i32)

    def attend(shifted):
        in_head = lax.broadcasted_iota(i32, (LANES, 1), 0) // HD == head
        query = jnp.where(in_head, base2_t_ref[...], jnp.zeros((), bf16))
        scores = dot(key_ref[...], query)
        if shifted:
            scores = scores - jnp.max(scores, axis=0, keepdims=True)
        weights = jnp.exp2(scores).astype(bf16)
        exp_ref[0] = weights
        keys = key_t_ref[pl.ds(at, HD), :].astype(f32)
        values = value_t_ref[pl.ds(at, HD), :].astype(f32)
        middle = jnp.mean(values, axis=1, keepdims=True)
        centered = values - middle
        features = [centered[j : j + 1] * keys for j in range(HD)]
        features += [keys, values, jnp.ones((HD, PATCH), f32)]
        sums = dot(jnp.concatenate([f.astype(bf16) for f in features], axis=0), weights)
        inverse = 1.0 / sums[(HD + 2) * HD : (HD + 2) * HD + 1]
        inverse_ref[0] = inverse
        mean_key = sums[HD * HD : (HD + 1) * HD] * inverse
        mean_value = sums[(HD + 1) * HD : (HD + 2) * HD] * inverse
        attended_ref[pl.ds(at, HD), :] = mean_value.astype(bf16)
        offset = mean_value - middle
        for j in range(HD):
            crossed = sums[j * HD : (j + 1) * HD] * inverse - offset[j : j + 1] * mean_key
            covariance_ref[0, j * HD : (j + 1) * HD, :] = crossed.astype(bf16)

    @pl.when(safe_ref[0] == 1)
    def _():
        attend(False)

    @pl.when(safe_ref[0] == 0)
    def _():
        attend(True)


def attention_forward(keys, base2_t, key_t, value_t, space):
    heads = LANES // HD
    tall = pl.BlockSpec((LANES, PATCH), lambda h: (0, 0))
    per_head = lambda h: (h, 0, 0)
    elements = heads * PATCH * PATCH
    return pl.pallas_call(
        forward_body,
        grid=(heads,),
        in_specs=[pl.BlockSpec((PATCH, LANES), lambda h: (0, 0)), tall, tall, tall],
        out_specs=[
            pl.BlockSpec((1, PATCH, PATCH), per_head),
            tall,
            pl.BlockSpec((1, 1, PATCH), per_head),
            pl.BlockSpec((1, HD * HD, PATCH), per_head),
        ],
        out_shape=[
            space((heads, PATCH, PATCH), bf16),
            space((LANES, PATCH), bf16),
            pltpu.VMEM((heads, 1, PATCH), f32),
            space((heads, HD * HD, PATCH), bf16),
        ],
        scratch_shapes=[pltpu.SMEM((1,), i32)],
        compiler_params=params(16),
        cost_estimate=cost(1360 * elements, 2 * elements, elements),
        name="attention_forward",
    )(keys, base2_t, key_t, value_t)


def backward_body(first, *refs):
    (
        column_ref,
        exp_ref,
        inverse_ref,
        query_t_ref,
        value_t_ref,
        attended_ref,
        g0_ref,
        g1_ref,
        g2_ref,
        g3_ref,
        weight_ref,
        covariance_ref,
        *refs,
    ) = refs
    if first:
        later_exp_ref, *refs = refs
    else:
        rest_ref, *refs = refs
    d_out_ref, d_query_ref, d_key_ref, d_value_ref, *refs = refs
    if first:
        staged_ref, d_attended_ref, staged_sem = refs
        staged = pltpu.make_async_copy(
            later_exp_ref.at[pl.ds(0, STAGED_HEADS)], staged_ref, staged_sem
        )
    else:
        d_attended_ref, exp_all_ref, exp_sems, covariance_all_ref, covariance_sems = refs
    head = pl.program_id(0)
    at = pl.multiple_of(head * HD, HD)

    def exp_copy(h):
        return pltpu.make_async_copy(
            rest_ref.at[h + STAGED_HEADS], exp_all_ref.at[h], exp_sems.at[h]
        )

    def covariance_copy(h):
        return pltpu.make_async_copy(
            covariance_ref.at[h], covariance_all_ref.at[h], covariance_sems.at[h]
        )

    @pl.when(head == 0)
    def _():
        if first:
            staged.start()
        else:
            for h in range(LANES // HD):
                if h >= STAGED_HEADS:
                    exp_copy(h - STAGED_HEADS).start()
                covariance_copy(h).start()
        me = column_ref[0]
        for block, mask in zip((g0_ref, g1_ref, g2_ref, g3_ref), BLOCK_MASKS):
            start = pl.multiple_of((me ^ mask) * LANES, LANES)
            d_out_ref[pl.ds(start, LANES), :] = block[...]
        d_attended_ref[...] = dot(weight_ref[...].T, d_out_ref[...]).astype(bf16)

    def one_head(weights):
        grads = d_attended_ref[pl.ds(at, HD), :].astype(f32)
        query = query_t_ref[pl.ds(at, HD), :].astype(f32)
        values = value_t_ref[pl.ds(at, HD), :].astype(f32)
        inverse = inverse_ref[0]
        middle = jnp.mean(values, axis=1, keepdims=True)
        centered = values - middle
        offset = attended_ref[pl.ds(at, HD), :].astype(f32) - middle
        scaled = grads * inverse
        delta = jnp.sum(scaled * offset, axis=0, keepdims=True)
        features = [scaled[j : j + 1] * query for j in range(HD)] + [delta * query, scaled]
        sums = dot_rows(jnp.concatenate([f.astype(bf16) for f in features], axis=0), weights())
        d_value_ref[pl.ds(at, HD), :] = sums[(HD + 1) * HD :].astype(bf16)
        if first:
            covariance = covariance_ref.at[0]
        else:
            covariance_copy(head).wait()
            covariance = covariance_all_ref.at[head]
        d_key = centered[0:1] * sums[:HD]
        d_query = grads[0:1] * covariance[:HD, :].astype(f32)
        for j in range(1, HD):
            rows = slice(j * HD, (j + 1) * HD)
            d_key += centered[j : j + 1] * sums[rows]
            d_query += grads[j : j + 1] * covariance[rows, :].astype(f32)
        d_key_ref[pl.ds(at, HD), :] = (d_key - sums[HD * HD : (HD + 1) * HD]).astype(bf16)
        d_query_ref[pl.ds(at, HD), :] = (d_query * score_scale).astype(bf16)

    if first:
        one_head(lambda: exp_ref[0])

        @pl.when(head == pl.num_programs(0) - 1)
        def _():
            staged.wait()

    else:

        @pl.when(head < STAGED_HEADS)
        def _():
            one_head(lambda: exp_ref[0])

        @pl.when(head >= STAGED_HEADS)
        def _():
            exp_copy(head - STAGED_HEADS).wait()
            one_head(lambda: exp_all_ref[head - STAGED_HEADS])


def attention_backward(
    patch, first, weights, other, inverse, covariance, query_t, value_t, attended, grads, weight, column
):
    features = weight.shape[0]
    heads = LANES // HD
    tall = pl.BlockSpec((LANES, PATCH), lambda h, c: (0, 0))
    part = pl.BlockSpec((LANES, PATCH), lambda h, c: (0, patch))
    per_head = lambda h, c: (h, 0, 0)
    kept_head = lambda h, c: (jnp.minimum(h, weights.shape[0] - 1), 0, 0)
    hbm = pl.BlockSpec(memory_space=pltpu.HBM)
    elements = heads * PATCH * PATCH
    turned = pltpu.VMEM((LANES, PATCH), bf16)
    in_specs = [
        pl.BlockSpec((1, PATCH, PATCH), kept_head),
        pl.BlockSpec((1, 1, PATCH), per_head),
        tall,
        tall,
        tall,
        part,
        part,
        part,
        part,
        pl.BlockSpec(weight.shape, lambda h, c: (0, 0)),
        pl.BlockSpec((1, HD * HD, PATCH), per_head) if first else hbm,
        hbm,
    ]
    operands = [weights, inverse, query_t, value_t, attended, *grads, weight, covariance, other]
    out_specs = [pl.BlockSpec((features, PATCH), lambda h, c: (0, 0)), tall, tall, tall]
    out_shape = [pltpu.VMEM((features, PATCH), bf16), turned, turned, turned]
    scratch = [pltpu.VMEM((LANES, PATCH), bf16)]
    if first:
        out_specs.append(pl.BlockSpec(memory_space=pl.ANY))
        out_shape.append(pltpu.VMEM((STAGED_HEADS, PATCH, PATCH), bf16))
        scratch.append(pltpu.SemaphoreType.DMA(()))
    else:
        rest = heads - STAGED_HEADS
        scratch += [pltpu.VMEM((rest, PATCH, PATCH), bf16), pltpu.SemaphoreType.DMA((rest,))]
        scratch += [pltpu.VMEM((heads, HD * HD, PATCH), bf16), pltpu.SemaphoreType.DMA((heads,))]
    return pl.pallas_call(
        functools.partial(backward_body, first),
        grid_spec=pltpu.PrefetchScalarGridSpec(
            num_scalar_prefetch=1,
            grid=(heads,),
            in_specs=in_specs,
            out_specs=out_specs,
            scratch_shapes=scratch,
        ),
        out_shape=out_shape,
        compiler_params=params(9 if first else 27),
        cost_estimate=cost(1100 * elements, 2 * elements),
        name="attention_backward",
    )(column, *operands)


def whole(shape, dtype):
    return jax.ShapeDtypeStruct(shape, dtype)


def weight_grad_body(*refs):
    d_query_ref, d_key_ref, d_value_ref, attended_ref, hidden_ref, d_out_ref, *before, out_ref = refs
    d_projected = jnp.concatenate([d_query_ref[...], d_key_ref[...], d_value_ref[...]], axis=0)
    projections = dot(d_projected, hidden_ref[...])
    output = dot_rows(attended_ref[...], d_out_ref[...])
    if before:
        out_ref[:, : 3 * LANES] = (before[0][: 3 * LANES, :] + projections).T.astype(bf16)
        out_ref[:, 3 * LANES :] = (before[0][3 * LANES :, :] + output).T.astype(bf16)
    else:
        out_ref[: 3 * LANES, :] = projections
        out_ref[3 * LANES :, :] = output


def weight_grads(*operands):
    features = operands[4].shape[1]
    work = 2 * PATCH * features * LANES
    last = len(operands) > 6
    return pl.pallas_call(
        weight_grad_body,
        out_shape=whole((features, 4 * LANES), bf16) if last else pltpu.VMEM((4 * LANES, features), f32),
        compiler_params=params(12),
        cost_estimate=cost(4 * work, 12 * PATCH * features),
        name="weight_grads",
    )(*operands)


def split_sums(sums):
    high = sums.astype(bf16)
    low = (sums - high.astype(f32)).astype(bf16)
    pad = jnp.zeros((INDEX_ROWS - 2 * sums.shape[0], sums.shape[1]), f32)
    return jnp.concatenate([high.astype(f32), low.astype(f32), pad], axis=0).astype(bf16)


def join_sums(rows):
    rows = rows.astype(f32)
    return rows[0:2] + rows[2:4]


def partial_body(
    column_ref,
    d_query_ref,
    d_key_ref,
    d_value_ref,
    query_ref,
    key_ref,
    value_ref,
    weight_ref,
    mine_ref,
    other_ref,
    sums_ref,
):
    me = column_ref[0]
    d_projected = jnp.concatenate([d_query_ref[...], d_key_ref[...], d_value_ref[...]], axis=0)
    plain = jnp.zeros((1, PATCH), f32)
    for j, mask in enumerate(BLOCK_MASKS):
        start = pl.multiple_of((me ^ mask) * LANES, LANES)
        rows = [weight_ref[t, pl.ds(start, LANES), :] for t in range(3)]
        block = dot(jnp.concatenate(rows, axis=1), d_projected).astype(bf16)
        plain += jnp.sum(block.astype(f32), axis=0, keepdims=True)
        to = mine_ref if j < 2 else other_ref
        to[(j % 2) * LANES : (j % 2 + 1) * LANES, :] = block
    crossed = (
        d_query_ref[...].astype(f32) * (query_ref[...].astype(f32) / score_scale)
        + d_key_ref[...].astype(f32) * key_ref[...].astype(f32)
        + d_value_ref[...].astype(f32) * value_ref[...].astype(f32)
    )
    sums = jnp.concatenate([plain, jnp.sum(crossed, axis=0, keepdims=True)], axis=0)
    sums_ref[...] = sums
    other_ref[2 * LANES :, :] = split_sums(sums)


def hidden_part(d_query, d_key, d_value, query, key, value, weight, column):
    features = weight.shape[1]
    return pl.pallas_call(
        partial_body,
        in_specs=[pl.BlockSpec(memory_space=pltpu.SMEM)] + [pl.BlockSpec(memory_space=pltpu.VMEM)] * 7,
        out_shape=[
            pltpu.VMEM((2 * LANES, PATCH), bf16),
            pltpu.VMEM((2 * LANES + INDEX_ROWS, PATCH), bf16),
            pltpu.VMEM((2, PATCH), f32),
        ],
        compiler_params=params(12),
        cost_estimate=cost(6 * PATCH * features * LANES, 4 * PATCH * features),
        name="hidden_part",
    )(column, d_query, d_key, d_value, query, key, value, weight)


def pair_body(mine_ref, sums_ref, got_ref, kept_ref, sums_out_ref, sent_ref):
    pair = mine_ref[...].astype(f32) + got_ref[: 2 * LANES, :].astype(f32)
    sums = sums_ref[...] + join_sums(got_ref[2 * LANES :, :])
    kept_ref[...] = pair[:LANES]
    sums_out_ref[...] = sums
    sent_ref[:LANES, :] = pair[LANES:].astype(bf16)
    sent_ref[LANES:, :] = split_sums(sums)


def pair_sum(mine, sums, got):
    return pl.pallas_call(
        pair_body,
        out_shape=[
            pltpu.VMEM((LANES, PATCH), f32),
            pltpu.VMEM((2, PATCH), f32),
            pltpu.VMEM((LANES + INDEX_ROWS, PATCH), bf16),
        ],
        compiler_params=params(6),
        cost_estimate=cost(4 * LANES * PATCH, 16 * LANES * PATCH),
        name="pair_sum",
    )(mine, sums, got)


def points_body(kept_ref, sums_ref, got_ref, d_out_ref, normed_ref, inv_ref, *rest):
    out_ref = rest[-1]
    features = 4.0 * LANES
    means = (sums_ref[...] + join_sums(got_ref[LANES:, :])) / features
    d_hidden = kept_ref[...] + got_ref[:LANES, :].astype(f32) - means[0:1]
    inner = d_hidden - normed_ref[...] * means[1:2]
    out_ref[...] = (d_out_ref[...].astype(f32) + inv_ref[0:1] * inner).T


def points_grad(patch, patches, kept, sums, got, d_out, normed, inv_scale, before):
    full = lambda a: pl.BlockSpec(a.shape, lambda i: (0, 0))
    in_specs = [full(kept), full(sums), full(got), pl.BlockSpec((LANES, PATCH), lambda i: (0, patch))]
    in_specs += [full(normed), full(inv_scale)]
    operands = [kept, sums, got, d_out, normed, inv_scale]
    if before is not None:
        in_specs.append(pl.BlockSpec(memory_space=pl.ANY))
        operands.append(before)
    return pl.pallas_call(
        points_body,
        grid=(1,),
        in_specs=in_specs,
        out_specs=pl.BlockSpec((PATCH, LANES), lambda i: (patch, 0)),
        out_shape=whole((patches * PATCH, LANES), f32),
        input_output_aliases={} if before is None else {len(operands) - 1: 0},
        compiler_params=params(8),
        cost_estimate=cost(8 * LANES * PATCH, 24 * LANES * PATCH),
        name="points_grad",
    )(*operands)


def grad_sum_body(parts_ref, qkv_ref, out_ref):
    total = parts_ref[0].astype(f32)
    for j in range(1, parts_ref.shape[0]):
        total += parts_ref[j].astype(f32)
    for t in range(3):
        qkv_ref[t] = total[:, t * LANES : (t + 1) * LANES]
    out_ref[...] = total[:, 3 * LANES :]


def grad_sum(parts):
    shards, rows, width = parts.shape
    return pl.pallas_call(
        grad_sum_body,
        out_shape=[whole((3, rows, LANES), f32), whole((rows, LANES), f32)],
        compiler_params=params(8),
        cost_estimate=cost(shards * rows * width, 4 * shards * rows * width),
        name="grad_sum",
    )(parts)


def local(
    scan_points,
    send_order,
    arrive_order,
    qkv_weight,
    out_weight,
    voxel_grads,
    voxel_shard,
    voxel_point,
):
    shards = lax.axis_size("seq")
    members = lax.axis_size("mp")
    local_rows, features = scan_points.shape
    voxels = voxel_grads.shape[0]
    capacity = 2 * voxels // shards
    patches = local_rows // PATCH
    column = lax.axis_index("mp").astype(i32).reshape(1)
    zero = jnp.zeros((1,), i32)
    weight = qkv_weight.transpose(1, 0, 2)

    def swap(rows, mask):
        return lax.ppermute(rows, "mp", [(i, i ^ mask) for i in range(members)])

    def exchange(rows):
        return lax.all_to_all(rows, "seq", split_axis=0, concat_axis=0, tiled=True)

    def after(value, first):
        return lax.optimization_barrier((value, first))

    def in_hbm(value):
        return pltpu.with_memory_space_constraint(value, pltpu.HBM)

    arrived = exchange(permute_rows(scan_points, send_order, column, 0, 1, whole, 60))
    buckets = bucket_rows(voxel_grads, voxel_shard, voxel_point, column, shards, capacity)
    owns = [
        permute_rows(arrived, arrive_order, zero, p, patches, pltpu.VMEM, 12)
        for p in range(patches)
    ]
    buckets, owns[0] = after(buckets, owns[0])
    got = exchange(buckets.reshape(shards * (capacity + INDEX_ROWS), LANES))
    across = [swap(own, 2) for own in owns]
    across[0], owns[1] = after(across[0], owns[1])

    def project_patch(p):
        columns = (owns[p], across[p], swap(owns[p], 1), swap(across[p], 1))
        return project(columns, weight, column, pltpu.HBM, pltpu.VMEM if p == 0 else pltpu.HBM)

    def forward(p, projected):
        space = pltpu.VMEM if p == patches - 1 else pltpu.HBM
        return attention_forward(projected[3], projected[4], *projected[6:], space)

    projected0 = project_patch(0)
    forward0 = forward(0, projected0)
    across[1], forward0 = after(across[1], forward0)
    projected1 = project_patch(1)
    got, projected1 = after(got, projected1)
    summed_rows = segment_rows(got.reshape(shards, capacity + INDEX_ROWS, LANES), local_rows)
    summed_across = swap(summed_rows, 2)
    projected1, summed_rows = after(projected1, summed_rows)
    forward1 = forward(1, projected1)
    summed_across, forward1 = after(summed_across, forward1)
    grads = (summed_rows, summed_across, swap(summed_rows, 1), swap(summed_across, 1))
    forwards = [(projected0, forward0), (projected1, forward1)]

    kept, sums, received = {}, {}, {}
    for p in reversed(range(patches)):
        (hidden, _, _, _, _, query_t, key_t, value_t), (weights, attended, inverse, covariance) = forwards[p]
        if p == 0:
            weights, sent = after(weights, sent)
            received[1] = swap(sent, 2)
            other_exp, covariance, weights = in_hbm(weights), in_hbm(covariance), staged[0]
        else:
            other_exp = in_hbm(forwards[0][1][0])
        d_out, d_query, d_key, d_value, *staged = attention_backward(
            p, p > 0, weights, other_exp, inverse, covariance, query_t, value_t, attended, grads, out_weight, column
        )
        if p == 0:
            received[1], d_query = after(received[1], d_query)
        grad_operands = (d_query, d_key, d_value, attended, hidden, d_out)
        if p == 0:
            weight_parts = weight_grads(*grad_operands, first_parts)
            operands = (d_query, d_key, d_value, query_t, key_t, value_t)
            operands, weight_parts = after(operands, weight_parts)
            d_query, d_key, d_value, query_t, key_t, value_t = map(in_hbm, operands)
        mine, other, own_sums = hidden_part(d_query, d_key, d_value, query_t, key_t, value_t, weight, column)
        partner = swap(other, 1)
        if p > 0:
            first_parts = weight_grads(*grad_operands)
            partner, first_parts = after(partner, first_parts)
        kept[p], sums[p], sent = pair_sum(mine, own_sums, partner)
    received[0] = swap(sent, 2)
    d_points = None
    for p in reversed(range(patches)):
        normed, inv_scale = forwards[p][0][1:3]
        if p > 0:
            normed, inv_scale = in_hbm(normed), in_hbm(inv_scale)
        d_points = points_grad(
            p, patches, kept[p], sums[p], received[p], grads[0], normed, inv_scale, d_points
        )
    parts = exchange(weight_parts).reshape(shards, features // shards, 4 * LANES)
    grad_qkv, grad_out = grad_sum(parts)
    return (d_points, grad_qkv.transpose(1, 0, 2), grad_out)


def solution(mesh):
    in_specs = (
        P("seq", None),
        P("seq"),
        P("seq"),
        P(None, None, "mp"),
        P(None, "mp"),
        P("seq", None),
        P("seq", None),
        P("seq"),
    )
    out_specs = (P("seq", "mp"), P("seq", None, "mp"), P("seq", "mp"))
    return jax.shard_map(local, mesh=mesh, in_specs=in_specs, out_specs=out_specs, check_vma=False)
```

```python
import functools

import jax
import jax.numpy as jnp
from jax import lax
from jax.experimental import pallas as pl
from jax.experimental.pallas import tpu as pltpu
from jax.sharding import PartitionSpec as P

HD = 16
PATCH = 1024
LANES = 128
INDEX_ROWS = 16
INDEX_BASE = 64
BLOCK_MASKS = (0, 2, 1, 3)
SAFE_SCORE = 60.0
STAGED_HEADS = 1
SEGMENT_SHARDS = 8
BUCKET_SHARDS = 2

score_scale = 0.25
epsilon = 1e-05
log2_e = 1.4426950408889634

f32 = jnp.float32
bf16 = jnp.bfloat16
i32 = jnp.int32

ROWS_BY_ROWS = (((1,), (1,)), ((), ()))


def params(mib):
    return pltpu.CompilerParams(vmem_limit_bytes=mib << 20)


def cost(flops, bytes_accessed, transcendentals=0):
    return pl.CostEstimate(
        flops=int(flops), bytes_accessed=int(bytes_accessed), transcendentals=int(transcendentals)
    )


def dot(a, b):
    return jnp.dot(a, b, preferred_element_type=f32)


def dot_rows(a, b):
    return lax.dot_general(a, b, ROWS_BY_ROWS, preferred_element_type=f32)


def ones_where(mask):
    return jnp.where(mask, 1.0, 0.0).astype(bf16)


def permute_body(column_ref, order_ref, block_ref, out_ref):
    step = pl.program_id(0)
    half = block_ref.shape[0] // 2
    chunks = out_ref.shape[0] // LANES
    lane = lax.broadcasted_iota(i32, (LANES, LANES), 1)
    sides = jnp.concatenate([block_ref[:half, :], block_ref[half:, :]], axis=1)
    onehots, lows = [], []
    for j in range(chunks):
        wanted = order_ref[pl.ds(step * chunks + j, 1), :].astype(f32)
        wanted = jnp.broadcast_to(wanted, (LANES, LANES)).T.astype(i32)
        low = wanted < half
        local_row = jnp.where(low, wanted, wanted - half)
        onehots.append(
            jnp.concatenate(
                [ones_where(local_row == lane + k * LANES) for k in range(half // LANES)], axis=1
            )
        )
        lows.append(low)
    both = dot(jnp.concatenate(onehots, axis=0), sides)
    for j in range(chunks):
        rows = slice(j * LANES, (j + 1) * LANES)
        out_ref[rows, :] = jnp.where(lows[j], both[rows, :LANES], both[rows, LANES:]).astype(bf16)


def permute_rows(rows, order, column, part, parts, out, mib):
    row_count = order.shape[0] // parts
    groups = row_count // LANES
    step_rows = min(1024, row_count)
    return pl.pallas_call(
        permute_body,
        grid_spec=pltpu.PrefetchScalarGridSpec(
            num_scalar_prefetch=1,
            grid=(row_count // step_rows,),
            in_specs=[
                pl.BlockSpec((groups, LANES), lambda i, c: (part, 0)),
                pl.BlockSpec((rows.shape[0], LANES), lambda i, c: (0, c[0])),
            ],
            out_specs=pl.BlockSpec((step_rows, LANES), lambda i, c: (i, 0)),
        ),
        out_shape=out((row_count, LANES), bf16),
        compiler_params=params(mib),
        cost_estimate=cost(2 * row_count * LANES, row_count),
        name="permute_rows",
    )(column, order.reshape(parts * groups, LANES), rows)


def bucket_body(shards, capacity, column_ref, shard_ref, point_ref, grads_ref, out_ref, place_ref):
    step = pl.program_id(0)
    row_count = grads_ref.shape[0]
    groups = row_count // LANES

    @pl.when(step == 0)
    def _():
        targets = shard_ref[...]
        masks = [ones_where(targets == t) for t in range(shards)]
        stacked = jnp.concatenate(masks, axis=0)
        above = ones_where(
            lax.broadcasted_iota(i32, (LANES, LANES), 0)
            < lax.broadcasted_iota(i32, (LANES, LANES), 1)
        )
        earlier = ones_where(
            lax.broadcasted_iota(i32, (groups, groups), 1)
            < lax.broadcasted_iota(i32, (groups, groups), 0)
        )
        in_row = dot(stacked, above)
        places = jnp.zeros((groups, LANES), f32)
        for t in range(shards):
            rows_before = jnp.sum(dot(earlier, masks[t]), axis=1, keepdims=True)
            place = in_row[t * groups : (t + 1) * groups] + rows_before + float(t * capacity)
            places = jnp.where(targets == t, place, places)
        place_ref[...] = places.astype(i32)

    points = jnp.concatenate([point_ref[j : j + 1, :] for j in range(groups)], axis=1)
    high = points // INDEX_BASE
    low = points - high * INDEX_BASE
    digits = jnp.concatenate(
        [high.astype(f32), low.astype(f32), jnp.zeros((INDEX_ROWS - 2, row_count), f32)], axis=0
    )
    group = out_ref.shape[0]
    chunks = capacity // LANES
    slot = lax.broadcasted_iota(i32, (group * capacity, LANES), 0) + step * (group * capacity)
    onehot = jnp.concatenate(
        [ones_where(place_ref[j : j + 1, :] == slot) for j in range(groups)], axis=1
    )
    filled = dot(onehot, grads_ref[...]).astype(bf16)
    sent = dot_rows(digits.astype(bf16), onehot)
    for shard in range(group):
        start = shard * capacity
        out_ref[shard, :capacity, :] = filled[start : start + capacity]
        rows = [
            sent[d : d + 1, start + j * LANES : start + (j + 1) * LANES]
            for d in range(2)
            for j in range(chunks)
        ]
        rows.append(jnp.zeros((INDEX_ROWS - 2 * chunks, LANES), f32))
        out_ref[shard, capacity:, :] = jnp.concatenate(rows, axis=0).astype(bf16)


def bucket_rows(grads, targets, points, column, shards, capacity):
    row_count = grads.shape[0]
    groups = row_count // LANES
    group = BUCKET_SHARDS if shards % BUCKET_SHARDS == 0 else 1
    return pl.pallas_call(
        functools.partial(bucket_body, shards, capacity),
        grid_spec=pltpu.PrefetchScalarGridSpec(
            num_scalar_prefetch=1,
            grid=(shards // group,),
            in_specs=[
                pl.BlockSpec((groups, LANES), lambda i, c: (0, 0)),
                pl.BlockSpec((groups, LANES), lambda i, c: (0, 0)),
                pl.BlockSpec((row_count, LANES), lambda i, c: (0, c[0])),
            ],
            out_specs=pl.BlockSpec((group, capacity + INDEX_ROWS, LANES), lambda i, c: (i, 0, 0)),
            scratch_shapes=[pltpu.VMEM((groups, LANES), i32)],
        ),
        out_shape=jax.ShapeDtypeStruct((shards, capacity + INDEX_ROWS, LANES), bf16),
        compiler_params=params(60),
        cost_estimate=cost(
            8 * shards * capacity * row_count * LANES, 3 * shards * capacity * LANES * 2
        ),
        name="bucket_rows",
    )(column, targets.reshape(groups, LANES), points.reshape(groups, LANES), grads)


def segment_body(got_ref, out_ref, total_ref):
    step = pl.program_id(0)
    capacity = got_ref.shape[1] - INDEX_ROWS
    chunks = capacity // LANES
    half = total_ref.shape[0]
    row = lax.broadcasted_iota(i32, (half, LANES), 0)
    onehots, sides = [], []
    for shard in range(got_ref.shape[0]):
        digits = got_ref[shard, capacity:, :].astype(f32)
        index = digits[:chunks] * float(INDEX_BASE) + digits[chunks : 2 * chunks]
        position = index.astype(i32)
        local_row = jnp.where(position < half, position, position - half)
        for j in range(chunks):
            onehots.append(ones_where(local_row[j : j + 1] == row))
            low = jnp.broadcast_to(index[j : j + 1], (LANES, LANES)).T < float(half)
            rows = got_ref[shard, j * LANES : (j + 1) * LANES, :].astype(f32)
            both = [jnp.where(low, rows, 0.0), jnp.where(low, 0.0, rows)]
            sides.append(jnp.concatenate(both, axis=1).astype(bf16))
    part = dot(jnp.concatenate(onehots, axis=1), jnp.concatenate(sides, axis=0))

    @pl.when(step == 0)
    def _():
        total_ref[...] = part

    @pl.when(step > 0)
    def _():
        total_ref[...] += part

    @pl.when(step == pl.num_programs(0) - 1)
    def _():
        out_ref[:, :half] = total_ref[:, :LANES].T.astype(bf16)
        out_ref[:, half:] = total_ref[:, LANES:].T.astype(bf16)


def segment_rows(got, row_count):
    shards, message, _ = got.shape
    group = SEGMENT_SHARDS if shards % SEGMENT_SHARDS == 0 else 1
    return pl.pallas_call(
        segment_body,
        grid=(shards // group,),
        in_specs=[pl.BlockSpec((group, message, LANES), lambda i: (i, 0, 0))],
        out_specs=pl.BlockSpec((LANES, row_count), lambda i: (0, 0)),
        out_shape=pltpu.VMEM((LANES, row_count), bf16),
        scratch_shapes=[pltpu.VMEM((row_count // 2, 2 * LANES), f32)],
        compiler_params=params(40),
        cost_estimate=cost(
            8 * shards * message * row_count * LANES, 3 * shards * message * LANES * 2
        ),
        name="segment_rows",
    )(got)


def project_body(
    column_ref,
    x0_ref,
    x1_ref,
    x2_ref,
    x3_ref,
    weight_ref,
    hidden_ref,
    normed_ref,
    inv_ref,
    key_ref,
    base2_t_ref,
    query_t_ref,
    key_t_ref,
    value_t_ref,
):
    me = column_ref[0]
    blocks = [r[...].astype(f32) for r in (x0_ref, x1_ref, x2_ref, x3_ref)]
    features = float(LANES * len(blocks))
    mean = jnp.sum(blocks[0] + blocks[1] + (blocks[2] + blocks[3]), axis=1, keepdims=True) / features
    centered = [b - mean for b in blocks]
    squares = [c * c for c in centered]
    var = jnp.sum(squares[0] + squares[1] + (squares[2] + squares[3]), axis=1, keepdims=True) / features
    inv = lax.rsqrt(var + epsilon)
    normed_ref[...] = (centered[0] * inv).T
    inv_ref[...] = jnp.broadcast_to(inv, centered[0].shape).T[:8]
    for block, mask in zip(centered, BLOCK_MASKS):
        at = pl.multiple_of((me ^ mask) * LANES, LANES)
        hidden_ref[:, pl.ds(at, LANES)] = (block * inv).astype(bf16)
    weight = jnp.concatenate([weight_ref[t] for t in range(3)], axis=1)
    projected = dot(hidden_ref[...], weight).astype(bf16)
    key_ref[...] = projected[:, LANES : 2 * LANES]
    query = projected[:, :LANES].astype(f32).T * score_scale
    query_t_ref[...] = query.astype(bf16)
    base2_t_ref[...] = (query * log2_e).astype(bf16)
    key_t_ref[...] = projected[:, LANES : 2 * LANES].astype(f32).T.astype(bf16)
    value_t_ref[...] = projected[:, 2 * LANES :].astype(f32).T.astype(bf16)


def project(blocks, weight, column, hidden_space, space):
    row_count = blocks[0].shape[0]
    step_rows = row_count
    features = weight.shape[1]
    width = pl.BlockSpec((step_rows, LANES), lambda i, c: (i, 0))
    tall = pl.BlockSpec((LANES, step_rows), lambda i, c: (0, i))
    normal = lambda t: space((row_count, LANES), t)
    turned = space((LANES, row_count), bf16)
    return pl.pallas_call(
        project_body,
        grid_spec=pltpu.PrefetchScalarGridSpec(
            num_scalar_prefetch=1,
            grid=(row_count // step_rows,),
            in_specs=[width] * 4 + [pl.BlockSpec(weight.shape, lambda i, c: (0, 0, 0))],
            out_specs=[
                pl.BlockSpec((step_rows, features), lambda i, c: (i, 0)),
                tall,
                pl.BlockSpec((8, step_rows), lambda i, c: (0, i)),
                width,
            ]
            + [tall] * 4,
        ),
        out_shape=[hidden_space((row_count, features), bf16)]
        + [pltpu.HBM((LANES, row_count), f32), pltpu.HBM((8, row_count), f32)]
        + [normal(bf16)]
        + [turned] * 4,
        compiler_params=params(12),
        cost_estimate=cost(4 * row_count * features * 3 * LANES, row_count * LANES * 40),
        name="project",
    )(column, *blocks, weight)


def forward_body(
    key_ref,
    base2_t_ref,
    query_t_ref,
    key_t_ref,
    value_t_ref,
    exp_ref,
    attended_ref,
    inverse_ref,
    covariance_ref,
    safe_ref,
):
    head = pl.program_id(0)
    at = pl.multiple_of(head * HD, HD)

    @pl.when(head == 0)
    def _():
        def largest(ref):
            squares = jnp.square(ref[...].astype(f32)).reshape(LANES // HD, HD, PATCH)
            return jnp.max(jnp.sum(squares, axis=1), axis=1, keepdims=True)

        bound = jnp.max(largest(base2_t_ref) * largest(key_t_ref))
        safe_ref[0] = (bound <= SAFE_SCORE * SAFE_SCORE).astype(i32)

    def attend(shifted):
        in_head = lax.broadcasted_iota(i32, (LANES, 1), 0) // HD == head
        query_ref = query_t_ref if shifted else base2_t_ref
        scores = dot(key_ref[...], jnp.where(in_head, query_ref[...], jnp.zeros((), bf16)))
        if shifted:
            scores = (scores - jnp.max(scores, axis=0, keepdims=True)) * log2_e
        weights = jnp.exp2(scores).astype(bf16)
        exp_ref[0] = weights
        keys = key_t_ref[pl.ds(at, HD), :].astype(f32)
        values = value_t_ref[pl.ds(at, HD), :].astype(f32)
        middle = jnp.mean(values, axis=1, keepdims=True)
        centered = values - middle
        features = [centered[j : j + 1] * keys for j in range(HD)]
        features += [keys, values, jnp.ones((HD, PATCH), f32)]
        sums = dot(jnp.concatenate([f.astype(bf16) for f in features], axis=0), weights)
        inverse = 1.0 / sums[(HD + 2) * HD : (HD + 2) * HD + 1]
        inverse_ref[0] = inverse
        mean_key = sums[HD * HD : (HD + 1) * HD] * inverse
        mean_value = sums[(HD + 1) * HD : (HD + 2) * HD] * inverse
        attended_ref[pl.ds(at, HD), :] = mean_value.astype(bf16)
        offset = mean_value - middle
        for j in range(HD):
            crossed = sums[j * HD : (j + 1) * HD] * inverse - offset[j : j + 1] * mean_key
            covariance_ref[0, j * HD : (j + 1) * HD, :] = crossed.astype(bf16)

    @pl.when(safe_ref[0] == 1)
    def _():
        attend(False)

    @pl.when(safe_ref[0] == 0)
    def _():
        attend(True)


def attention_forward(keys, base2_t, query_t, key_t, value_t, space):
    heads = LANES // HD
    tall = pl.BlockSpec((LANES, PATCH), lambda h: (0, 0))
    per_head = lambda h: (h, 0, 0)
    elements = heads * PATCH * PATCH
    return pl.pallas_call(
        forward_body,
        grid=(heads,),
        in_specs=[pl.BlockSpec((PATCH, LANES), lambda h: (0, 0))] + [tall] * 4,
        out_specs=[
            pl.BlockSpec((1, PATCH, PATCH), per_head),
            tall,
            pl.BlockSpec((1, 1, PATCH), per_head),
            pl.BlockSpec((1, HD * HD, PATCH), per_head),
        ],
        out_shape=[
            space((heads, PATCH, PATCH), bf16),
            space((LANES, PATCH), bf16),
            pltpu.VMEM((heads, 1, PATCH), f32),
            space((heads, HD * HD, PATCH), bf16),
        ],
        scratch_shapes=[pltpu.SMEM((1,), i32)],
        compiler_params=params(16),
        cost_estimate=cost(1360 * elements, 2 * elements, elements),
        name="attention_forward",
    )(keys, base2_t, query_t, key_t, value_t)


def backward_body(first, *refs):
    (
        column_ref,
        exp_ref,
        inverse_ref,
        query_t_ref,
        value_t_ref,
        attended_ref,
        g0_ref,
        g1_ref,
        g2_ref,
        g3_ref,
        weight_ref,
        covariance_ref,
        *refs,
    ) = refs
    if first:
        later_exp_ref, *refs = refs
    else:
        rest_ref, *refs = refs
    d_out_ref, d_query_ref, d_key_ref, d_value_ref, *refs = refs
    if first:
        staged_ref, d_attended_ref, staged_sem = refs
        staged = pltpu.make_async_copy(
            later_exp_ref.at[pl.ds(0, STAGED_HEADS)], staged_ref, staged_sem
        )
    else:
        d_attended_ref, exp_all_ref, exp_sems, covariance_all_ref, covariance_sems = refs
    head = pl.program_id(0)
    at = pl.multiple_of(head * HD, HD)

    def exp_copy(h):
        return pltpu.make_async_copy(
            rest_ref.at[h + STAGED_HEADS], exp_all_ref.at[h], exp_sems.at[h]
        )

    def covariance_copy(h):
        return pltpu.make_async_copy(
            covariance_ref.at[h], covariance_all_ref.at[h], covariance_sems.at[h]
        )

    @pl.when(head == 0)
    def _():
        if first:
            staged.start()
        else:
            for h in range(LANES // HD):
                if h >= STAGED_HEADS:
                    exp_copy(h - STAGED_HEADS).start()
                covariance_copy(h).start()
        me = column_ref[0]
        for block, mask in zip((g0_ref, g1_ref, g2_ref, g3_ref), BLOCK_MASKS):
            start = pl.multiple_of((me ^ mask) * LANES, LANES)
            d_out_ref[pl.ds(start, LANES), :] = block[...]
        d_attended_ref[...] = dot(weight_ref[...].T, d_out_ref[...]).astype(bf16)

    def one_head(weights):
        grads = d_attended_ref[pl.ds(at, HD), :].astype(f32)
        query = query_t_ref[pl.ds(at, HD), :].astype(f32)
        values = value_t_ref[pl.ds(at, HD), :].astype(f32)
        inverse = inverse_ref[0]
        middle = jnp.mean(values, axis=1, keepdims=True)
        centered = values - middle
        offset = attended_ref[pl.ds(at, HD), :].astype(f32) - middle
        scaled = grads * inverse
        delta = jnp.sum(scaled * offset, axis=0, keepdims=True)
        features = [scaled[j : j + 1] * query for j in range(HD)] + [delta * query, scaled]
        sums = dot_rows(jnp.concatenate([f.astype(bf16) for f in features], axis=0), weights())
        d_value_ref[pl.ds(at, HD), :] = sums[(HD + 1) * HD :].astype(bf16)
        if first:
            covariance = covariance_ref.at[0]
        else:
            covariance_copy(head).wait()
            covariance = covariance_all_ref.at[head]
        d_key = centered[0:1] * sums[:HD]
        d_query = grads[0:1] * covariance[:HD, :].astype(f32)
        for j in range(1, HD):
            rows = slice(j * HD, (j + 1) * HD)
            d_key += centered[j : j + 1] * sums[rows]
            d_query += grads[j : j + 1] * covariance[rows, :].astype(f32)
        d_key_ref[pl.ds(at, HD), :] = (d_key - sums[HD * HD : (HD + 1) * HD]).astype(bf16)
        d_query_ref[pl.ds(at, HD), :] = (d_query * score_scale).astype(bf16)

    if first:
        one_head(lambda: exp_ref[0])

        @pl.when(head == pl.num_programs(0) - 1)
        def _():
            staged.wait()

    else:

        @pl.when(head < STAGED_HEADS)
        def _():
            one_head(lambda: exp_ref[0])

        @pl.when(head >= STAGED_HEADS)
        def _():
            exp_copy(head - STAGED_HEADS).wait()
            one_head(lambda: exp_all_ref[head - STAGED_HEADS])


def attention_backward(
    patch, first, weights, other, inverse, covariance, query_t, value_t, attended, grads, weight, column
):
    features = weight.shape[0]
    heads = LANES // HD
    tall = pl.BlockSpec((LANES, PATCH), lambda h, c: (0, 0))
    part = pl.BlockSpec((LANES, PATCH), lambda h, c: (0, patch))
    per_head = lambda h, c: (h, 0, 0)
    kept_head = lambda h, c: (jnp.minimum(h, weights.shape[0] - 1), 0, 0)
    hbm = pl.BlockSpec(memory_space=pltpu.HBM)
    elements = heads * PATCH * PATCH
    turned = pltpu.VMEM((LANES, PATCH), bf16)
    in_specs = [
        pl.BlockSpec((1, PATCH, PATCH), kept_head),
        pl.BlockSpec((1, 1, PATCH), per_head),
        tall,
        tall,
        tall,
        part,
        part,
        part,
        part,
        pl.BlockSpec(weight.shape, lambda h, c: (0, 0)),
        pl.BlockSpec((1, HD * HD, PATCH), per_head) if first else hbm,
        hbm,
    ]
    operands = [weights, inverse, query_t, value_t, attended, *grads, weight, covariance, other]
    out_specs = [pl.BlockSpec((features, PATCH), lambda h, c: (0, 0)), tall, tall, tall]
    out_shape = [pltpu.VMEM((features, PATCH), bf16), turned, turned, turned]
    scratch = [pltpu.VMEM((LANES, PATCH), bf16)]
    if first:
        out_specs.append(pl.BlockSpec(memory_space=pl.ANY))
        out_shape.append(pltpu.VMEM((STAGED_HEADS, PATCH, PATCH), bf16))
        scratch.append(pltpu.SemaphoreType.DMA(()))
    else:
        rest = heads - STAGED_HEADS
        scratch += [pltpu.VMEM((rest, PATCH, PATCH), bf16), pltpu.SemaphoreType.DMA((rest,))]
        scratch += [pltpu.VMEM((heads, HD * HD, PATCH), bf16), pltpu.SemaphoreType.DMA((heads,))]
    return pl.pallas_call(
        functools.partial(backward_body, first),
        grid_spec=pltpu.PrefetchScalarGridSpec(
            num_scalar_prefetch=1,
            grid=(heads,),
            in_specs=in_specs,
            out_specs=out_specs,
            scratch_shapes=scratch,
        ),
        out_shape=out_shape,
        compiler_params=params(9 if first else 27),
        cost_estimate=cost(1100 * elements, 2 * elements),
        name="attention_backward",
    )(column, *operands)


def whole(shape, dtype):
    return jax.ShapeDtypeStruct(shape, dtype)


def weight_grad_body(*refs):
    d_query_ref, d_key_ref, d_value_ref, attended_ref, hidden_ref, d_out_ref, *before, out_ref = refs
    d_projected = jnp.concatenate([d_query_ref[...], d_key_ref[...], d_value_ref[...]], axis=0)
    projections = dot(d_projected, hidden_ref[...])
    output = dot_rows(attended_ref[...], d_out_ref[...])
    if before:
        out_ref[:, : 3 * LANES] = (before[0][: 3 * LANES, :] + projections).T.astype(bf16)
        out_ref[:, 3 * LANES :] = (before[0][3 * LANES :, :] + output).T.astype(bf16)
    else:
        out_ref[: 3 * LANES, :] = projections
        out_ref[3 * LANES :, :] = output


def weight_grads(*operands):
    features = operands[4].shape[1]
    work = 2 * PATCH * features * LANES
    last = len(operands) > 6
    return pl.pallas_call(
        weight_grad_body,
        out_shape=whole((features, 4 * LANES), bf16) if last else pltpu.VMEM((4 * LANES, features), f32),
        compiler_params=params(12),
        cost_estimate=cost(4 * work, 12 * PATCH * features),
        name="weight_grads",
    )(*operands)


def split_sums(sums):
    high = sums.astype(bf16)
    low = (sums - high.astype(f32)).astype(bf16)
    pad = jnp.zeros((INDEX_ROWS - 2 * sums.shape[0], sums.shape[1]), f32)
    return jnp.concatenate([high.astype(f32), low.astype(f32), pad], axis=0).astype(bf16)


def join_sums(rows):
    rows = rows.astype(f32)
    return rows[0:2] + rows[2:4]


def partial_body(
    column_ref,
    d_query_ref,
    d_key_ref,
    d_value_ref,
    query_ref,
    key_ref,
    value_ref,
    weight_ref,
    mine_ref,
    other_ref,
    sums_ref,
):
    me = column_ref[0]
    d_projected = jnp.concatenate([d_query_ref[...], d_key_ref[...], d_value_ref[...]], axis=0)
    plain = jnp.zeros((1, PATCH), f32)
    for j, mask in enumerate(BLOCK_MASKS):
        start = pl.multiple_of((me ^ mask) * LANES, LANES)
        rows = [weight_ref[t, pl.ds(start, LANES), :] for t in range(3)]
        block = dot(jnp.concatenate(rows, axis=1), d_projected).astype(bf16)
        plain += jnp.sum(block.astype(f32), axis=0, keepdims=True)
        to = mine_ref if j < 2 else other_ref
        to[(j % 2) * LANES : (j % 2 + 1) * LANES, :] = block
    crossed = (
        d_query_ref[...].astype(f32) * (query_ref[...].astype(f32) / score_scale)
        + d_key_ref[...].astype(f32) * key_ref[...].astype(f32)
        + d_value_ref[...].astype(f32) * value_ref[...].astype(f32)
    )
    sums = jnp.concatenate([plain, jnp.sum(crossed, axis=0, keepdims=True)], axis=0)
    sums_ref[...] = sums
    other_ref[2 * LANES :, :] = split_sums(sums)


def hidden_part(d_query, d_key, d_value, query, key, value, weight, column):
    features = weight.shape[1]
    return pl.pallas_call(
        partial_body,
        in_specs=[pl.BlockSpec(memory_space=pltpu.SMEM)] + [pl.BlockSpec(memory_space=pltpu.VMEM)] * 7,
        out_shape=[
            pltpu.VMEM((2 * LANES, PATCH), bf16),
            pltpu.VMEM((2 * LANES + INDEX_ROWS, PATCH), bf16),
            pltpu.VMEM((2, PATCH), f32),
        ],
        compiler_params=params(12),
        cost_estimate=cost(6 * PATCH * features * LANES, 4 * PATCH * features),
        name="hidden_part",
    )(column, d_query, d_key, d_value, query, key, value, weight)


def pair_body(mine_ref, sums_ref, got_ref, kept_ref, sums_out_ref, sent_ref):
    pair = mine_ref[...].astype(f32) + got_ref[: 2 * LANES, :].astype(f32)
    sums = sums_ref[...] + join_sums(got_ref[2 * LANES :, :])
    kept_ref[...] = pair[:LANES]
    sums_out_ref[...] = sums
    sent_ref[:LANES, :] = pair[LANES:].astype(bf16)
    sent_ref[LANES:, :] = split_sums(sums)


def pair_sum(mine, sums, got):
    return pl.pallas_call(
        pair_body,
        out_shape=[
            pltpu.VMEM((LANES, PATCH), f32),
            pltpu.VMEM((2, PATCH), f32),
            pltpu.VMEM((LANES + INDEX_ROWS, PATCH), bf16),
        ],
        compiler_params=params(6),
        cost_estimate=cost(4 * LANES * PATCH, 16 * LANES * PATCH),
        name="pair_sum",
    )(mine, sums, got)


def points_body(kept_ref, sums_ref, got_ref, d_out_ref, normed_ref, inv_ref, *rest):
    out_ref = rest[-1]
    features = 4.0 * LANES
    means = (sums_ref[...] + join_sums(got_ref[LANES:, :])) / features
    d_hidden = kept_ref[...] + got_ref[:LANES, :].astype(f32) - means[0:1]
    inner = d_hidden - normed_ref[...] * means[1:2]
    out_ref[...] = (d_out_ref[...].astype(f32) + inv_ref[0:1] * inner).T


def points_grad(patch, patches, kept, sums, got, d_out, normed, inv_scale, before):
    full = lambda a: pl.BlockSpec(a.shape, lambda i: (0, 0))
    in_specs = [full(kept), full(sums), full(got), pl.BlockSpec((LANES, PATCH), lambda i: (0, patch))]
    in_specs += [full(normed), full(inv_scale)]
    operands = [kept, sums, got, d_out, normed, inv_scale]
    if before is not None:
        in_specs.append(pl.BlockSpec(memory_space=pl.ANY))
        operands.append(before)
    return pl.pallas_call(
        points_body,
        grid=(1,),
        in_specs=in_specs,
        out_specs=pl.BlockSpec((PATCH, LANES), lambda i: (patch, 0)),
        out_shape=whole((patches * PATCH, LANES), f32),
        input_output_aliases={} if before is None else {len(operands) - 1: 0},
        compiler_params=params(8),
        cost_estimate=cost(8 * LANES * PATCH, 24 * LANES * PATCH),
        name="points_grad",
    )(*operands)


def grad_sum_body(parts_ref, qkv_ref, out_ref):
    total = parts_ref[0].astype(f32)
    for j in range(1, parts_ref.shape[0]):
        total += parts_ref[j].astype(f32)
    for t in range(3):
        qkv_ref[t] = total[:, t * LANES : (t + 1) * LANES]
    out_ref[...] = total[:, 3 * LANES :]


def grad_sum(parts):
    shards, rows, width = parts.shape
    return pl.pallas_call(
        grad_sum_body,
        out_shape=[whole((3, rows, LANES), f32), whole((rows, LANES), f32)],
        compiler_params=params(8),
        cost_estimate=cost(shards * rows * width, 4 * shards * rows * width),
        name="grad_sum",
    )(parts)


def local(
    scan_points,
    send_order,
    arrive_order,
    qkv_weight,
    out_weight,
    voxel_grads,
    voxel_shard,
    voxel_point,
):
    shards = lax.axis_size("seq")
    members = lax.axis_size("mp")
    local_rows, features = scan_points.shape
    voxels = voxel_grads.shape[0]
    capacity = 2 * voxels // shards
    patches = local_rows // PATCH
    column = lax.axis_index("mp").astype(i32).reshape(1)
    zero = jnp.zeros((1,), i32)
    weight = qkv_weight.transpose(1, 0, 2)

    def swap(rows, mask):
        return lax.ppermute(rows, "mp", [(i, i ^ mask) for i in range(members)])

    def exchange(rows):
        return lax.all_to_all(rows, "seq", split_axis=0, concat_axis=0, tiled=True)

    def after(value, first):
        return lax.optimization_barrier((value, first))

    def in_hbm(value):
        return pltpu.with_memory_space_constraint(value, pltpu.HBM)

    arrived = exchange(permute_rows(scan_points, send_order, column, 0, 1, whole, 60))
    buckets = bucket_rows(voxel_grads, voxel_shard, voxel_point, column, shards, capacity)
    owns = [
        permute_rows(arrived, arrive_order, zero, p, patches, pltpu.VMEM, 12)
        for p in range(patches)
    ]
    buckets, owns[0] = after(buckets, owns[0])
    got = exchange(buckets.reshape(shards * (capacity + INDEX_ROWS), LANES))
    across = [swap(own, 2) for own in owns]
    across[0], owns[1] = after(across[0], owns[1])

    def project_patch(p):
        columns = (owns[p], across[p], swap(owns[p], 1), swap(across[p], 1))
        return project(columns, weight, column, pltpu.HBM, pltpu.VMEM if p == 0 else pltpu.HBM)

    def forward(p, projected):
        space = pltpu.VMEM if p == patches - 1 else pltpu.HBM
        return attention_forward(*projected[3:], space)

    projected0 = project_patch(0)
    forward0 = forward(0, projected0)
    across[1], forward0 = after(across[1], forward0)
    projected1 = project_patch(1)
    got, projected1 = after(got, projected1)
    summed_rows = segment_rows(got.reshape(shards, capacity + INDEX_ROWS, LANES), local_rows)
    summed_across = swap(summed_rows, 2)
    projected1, summed_rows = after(projected1, summed_rows)
    forward1 = forward(1, projected1)
    summed_across, forward1 = after(summed_across, forward1)
    grads = (summed_rows, summed_across, swap(summed_rows, 1), swap(summed_across, 1))
    forwards = [(projected0, forward0), (projected1, forward1)]

    kept, sums, received = {}, {}, {}
    for p in reversed(range(patches)):
        (hidden, _, _, _, _, query_t, key_t, value_t), (weights, attended, inverse, covariance) = forwards[p]
        if p == 0:
            weights, sent = after(weights, sent)
            received[1] = swap(sent, 2)
            other_exp, covariance, weights = in_hbm(weights), in_hbm(covariance), staged[0]
        else:
            other_exp = in_hbm(forwards[0][1][0])
        d_out, d_query, d_key, d_value, *staged = attention_backward(
            p, p > 0, weights, other_exp, inverse, covariance, query_t, value_t, attended, grads, out_weight, column
        )
        if p == 0:
            received[1], d_query = after(received[1], d_query)
        grad_operands = (d_query, d_key, d_value, attended, hidden, d_out)
        if p == 0:
            weight_parts = weight_grads(*grad_operands, first_parts)
            operands = (d_query, d_key, d_value, query_t, key_t, value_t)
            operands, weight_parts = after(operands, weight_parts)
            d_query, d_key, d_value, query_t, key_t, value_t = map(in_hbm, operands)
        mine, other, own_sums = hidden_part(d_query, d_key, d_value, query_t, key_t, value_t, weight, column)
        partner = swap(other, 1)
        if p > 0:
            first_parts = weight_grads(*grad_operands)
            partner, first_parts = after(partner, first_parts)
        kept[p], sums[p], sent = pair_sum(mine, own_sums, partner)
    received[0] = swap(sent, 2)
    d_points = None
    for p in reversed(range(patches)):
        normed, inv_scale = forwards[p][0][1:3]
        if p > 0:
            normed, inv_scale = in_hbm(normed), in_hbm(inv_scale)
        d_points = points_grad(
            p, patches, kept[p], sums[p], received[p], grads[0], normed, inv_scale, d_points
        )
    parts = exchange(weight_parts).reshape(shards, features // shards, 4 * LANES)
    grad_qkv, grad_out = grad_sum(parts)
    return (d_points, grad_qkv.transpose(1, 0, 2), grad_out)


def solution(mesh):
    in_specs = (
        P("seq", None),
        P("seq"),
        P("seq"),
        P(None, None, "mp"),
        P(None, "mp"),
        P("seq", None),
        P("seq", None),
        P("seq"),
    )
    out_specs = (P("seq", "mp"), P("seq", None, "mp"), P("seq", "mp"))
    return jax.shard_map(local, mesh=mesh, in_specs=in_specs, out_specs=out_specs, check_vma=False)
```

```python
import functools

import jax
import jax.numpy as jnp
from jax import lax
from jax.experimental import pallas as pl
from jax.experimental.pallas import tpu as pltpu
from jax.sharding import PartitionSpec as P

HD = 16
PATCH = 1024
LANES = 128
INDEX_ROWS = 16
INDEX_BASE = 64
BLOCK_MASKS = (0, 2, 1, 3)
SAFE_SCORE = 60.0
QUERY_BLOCK = 256
STAGED_HEADS = 1
SEGMENT_SHARDS = 8
BUCKET_SHARDS = 2

score_scale = 0.25
epsilon = 1e-05
log2_e = 1.4426950408889634

f32 = jnp.float32
bf16 = jnp.bfloat16
i32 = jnp.int32

ROWS_BY_ROWS = (((1,), (1,)), ((), ()))


def params(mib):
    return pltpu.CompilerParams(vmem_limit_bytes=mib << 20)


def cost(flops, bytes_accessed, transcendentals=0):
    return pl.CostEstimate(
        flops=int(flops), bytes_accessed=int(bytes_accessed), transcendentals=int(transcendentals)
    )


def dot(a, b):
    return jnp.dot(a, b, preferred_element_type=f32)


def dot_rows(a, b):
    return lax.dot_general(a, b, ROWS_BY_ROWS, preferred_element_type=f32)


def ones_where(mask):
    return jnp.where(mask, 1.0, 0.0).astype(bf16)


def permute_body(column_ref, order_ref, block_ref, out_ref):
    step = pl.program_id(0)
    half = block_ref.shape[0] // 2
    chunks = out_ref.shape[0] // LANES
    lane = lax.broadcasted_iota(i32, (LANES, LANES), 1)
    sides = jnp.concatenate([block_ref[:half, :], block_ref[half:, :]], axis=1)
    onehots, lows = [], []
    for j in range(chunks):
        wanted = order_ref[pl.ds(step * chunks + j, 1), :].astype(f32)
        wanted = jnp.broadcast_to(wanted, (LANES, LANES)).T.astype(i32)
        low = wanted < half
        local_row = jnp.where(low, wanted, wanted - half)
        onehots.append(
            jnp.concatenate(
                [ones_where(local_row == lane + k * LANES) for k in range(half // LANES)], axis=1
            )
        )
        lows.append(low)
    both = dot(jnp.concatenate(onehots, axis=0), sides)
    for j in range(chunks):
        rows = slice(j * LANES, (j + 1) * LANES)
        out_ref[rows, :] = jnp.where(lows[j], both[rows, :LANES], both[rows, LANES:]).astype(bf16)


def permute_rows(rows, order, column, part, parts, out, mib):
    row_count = order.shape[0] // parts
    groups = row_count // LANES
    step_rows = min(2048, row_count)
    return pl.pallas_call(
        permute_body,
        grid_spec=pltpu.PrefetchScalarGridSpec(
            num_scalar_prefetch=1,
            grid=(row_count // step_rows,),
            in_specs=[
                pl.BlockSpec((groups, LANES), lambda i, c: (part, 0)),
                pl.BlockSpec((rows.shape[0], LANES), lambda i, c: (0, c[0])),
            ],
            out_specs=pl.BlockSpec((step_rows, LANES), lambda i, c: (i, 0)),
        ),
        out_shape=out((row_count, LANES), bf16),
        compiler_params=params(mib),
        cost_estimate=cost(2 * row_count * LANES, row_count),
        name="permute_rows",
    )(column, order.reshape(parts * groups, LANES), rows)


def bucket_body(shards, capacity, column_ref, shard_ref, point_ref, grads_ref, out_ref, place_ref):
    step = pl.program_id(0)
    row_count = grads_ref.shape[0]
    groups = row_count // LANES

    @pl.when(step == 0)
    def _():
        targets = shard_ref[...]
        masks = [ones_where(targets == t) for t in range(shards)]
        stacked = jnp.concatenate(masks, axis=0)
        above = ones_where(
            lax.broadcasted_iota(i32, (LANES, LANES), 0)
            < lax.broadcasted_iota(i32, (LANES, LANES), 1)
        )
        earlier = ones_where(
            lax.broadcasted_iota(i32, (groups, groups), 1)
            < lax.broadcasted_iota(i32, (groups, groups), 0)
        )
        in_row = dot(stacked, above)
        places = jnp.zeros((groups, LANES), f32)
        for t in range(shards):
            rows_before = jnp.sum(dot(earlier, masks[t]), axis=1, keepdims=True)
            place = in_row[t * groups : (t + 1) * groups] + rows_before + float(t * capacity)
            places = jnp.where(targets == t, place, places)
        place_ref[...] = places.astype(i32)

    points = jnp.concatenate([point_ref[j : j + 1, :] for j in range(groups)], axis=1)
    high = points // INDEX_BASE
    low = points - high * INDEX_BASE
    digits = jnp.concatenate(
        [high.astype(f32), low.astype(f32), jnp.zeros((INDEX_ROWS - 2, row_count), f32)], axis=0
    )
    group = out_ref.shape[0]
    chunks = capacity // LANES
    slot = lax.broadcasted_iota(i32, (group * capacity, LANES), 0) + step * (group * capacity)
    onehot = jnp.concatenate(
        [ones_where(place_ref[j : j + 1, :] == slot) for j in range(groups)], axis=1
    )
    filled = dot(onehot, grads_ref[...]).astype(bf16)
    sent = dot_rows(digits.astype(bf16), onehot)
    for shard in range(group):
        start = shard * capacity
        out_ref[shard, :capacity, :] = filled[start : start + capacity]
        rows = [
            sent[d : d + 1, start + j * LANES : start + (j + 1) * LANES]
            for d in range(2)
            for j in range(chunks)
        ]
        rows.append(jnp.zeros((INDEX_ROWS - 2 * chunks, LANES), f32))
        out_ref[shard, capacity:, :] = jnp.concatenate(rows, axis=0).astype(bf16)


def bucket_rows(grads, targets, points, column, shards, capacity):
    row_count = grads.shape[0]
    groups = row_count // LANES
    group = BUCKET_SHARDS if shards % BUCKET_SHARDS == 0 else 1
    return pl.pallas_call(
        functools.partial(bucket_body, shards, capacity),
        grid_spec=pltpu.PrefetchScalarGridSpec(
            num_scalar_prefetch=1,
            grid=(shards // group,),
            in_specs=[
                pl.BlockSpec((groups, LANES), lambda i, c: (0, 0)),
                pl.BlockSpec((groups, LANES), lambda i, c: (0, 0)),
                pl.BlockSpec((row_count, LANES), lambda i, c: (0, c[0])),
            ],
            out_specs=pl.BlockSpec((group, capacity + INDEX_ROWS, LANES), lambda i, c: (i, 0, 0)),
            scratch_shapes=[pltpu.VMEM((groups, LANES), i32)],
        ),
        out_shape=jax.ShapeDtypeStruct((shards, capacity + INDEX_ROWS, LANES), bf16),
        compiler_params=params(60),
        cost_estimate=cost(
            8 * shards * capacity * row_count * LANES, 3 * shards * capacity * LANES * 2
        ),
        name="bucket_rows",
    )(column, targets.reshape(groups, LANES), points.reshape(groups, LANES), grads)


def segment_body(got_ref, out_ref, total_ref):
    step = pl.program_id(0)
    capacity = got_ref.shape[1] - INDEX_ROWS
    chunks = capacity // LANES
    half = total_ref.shape[0]
    row = lax.broadcasted_iota(i32, (half, LANES), 0)
    onehots, sides = [], []
    for shard in range(got_ref.shape[0]):
        digits = got_ref[shard, capacity:, :].astype(f32)
        index = digits[:chunks] * float(INDEX_BASE) + digits[chunks : 2 * chunks]
        position = index.astype(i32)
        local_row = jnp.where(position < half, position, position - half)
        for j in range(chunks):
            onehots.append(ones_where(local_row[j : j + 1] == row))
            low = jnp.broadcast_to(index[j : j + 1], (LANES, LANES)).T < float(half)
            rows = got_ref[shard, j * LANES : (j + 1) * LANES, :].astype(f32)
            both = [jnp.where(low, rows, 0.0), jnp.where(low, 0.0, rows)]
            sides.append(jnp.concatenate(both, axis=1).astype(bf16))
    part = dot(jnp.concatenate(onehots, axis=1), jnp.concatenate(sides, axis=0))

    @pl.when(step == 0)
    def _():
        total_ref[...] = part

    @pl.when(step > 0)
    def _():
        total_ref[...] += part

    @pl.when(step == pl.num_programs(0) - 1)
    def _():
        out_ref[:, :half] = total_ref[:, :LANES].T.astype(bf16)
        out_ref[:, half:] = total_ref[:, LANES:].T.astype(bf16)


def segment_rows(got, row_count):
    shards, message, _ = got.shape
    group = SEGMENT_SHARDS if shards % SEGMENT_SHARDS == 0 else 1
    return pl.pallas_call(
        segment_body,
        grid=(shards // group,),
        in_specs=[pl.BlockSpec((group, message, LANES), lambda i: (i, 0, 0))],
        out_specs=pl.BlockSpec((LANES, row_count), lambda i: (0, 0)),
        out_shape=pltpu.VMEM((LANES, row_count), bf16),
        scratch_shapes=[pltpu.VMEM((row_count // 2, 2 * LANES), f32)],
        compiler_params=params(40),
        cost_estimate=cost(
            8 * shards * message * row_count * LANES, 3 * shards * message * LANES * 2
        ),
        name="segment_rows",
    )(got)


def project_body(
    column_ref,
    x0_ref,
    x1_ref,
    x2_ref,
    x3_ref,
    weight_ref,
    hidden_ref,
    normed_ref,
    inv_ref,
    key_ref,
    base2_t_ref,
    query_t_ref,
    key_t_ref,
    value_t_ref,
):
    me = column_ref[0]
    blocks = [r[...].astype(f32) for r in (x0_ref, x1_ref, x2_ref, x3_ref)]
    features = float(LANES * len(blocks))
    mean = jnp.sum(blocks[0] + blocks[1] + (blocks[2] + blocks[3]), axis=1, keepdims=True) / features
    centered = [b - mean for b in blocks]
    squares = [c * c for c in centered]
    var = jnp.sum(squares[0] + squares[1] + (squares[2] + squares[3]), axis=1, keepdims=True) / features
    inv = lax.rsqrt(var + epsilon)
    normed_ref[...] = (centered[0] * inv).T
    inv_ref[...] = jnp.broadcast_to(inv, centered[0].shape).T[:8]
    for block, mask in zip(centered, BLOCK_MASKS):
        at = pl.multiple_of((me ^ mask) * LANES, LANES)
        hidden_ref[:, pl.ds(at, LANES)] = (block * inv).astype(bf16)
    weight = jnp.concatenate([weight_ref[t] for t in range(3)], axis=1)
    projected = dot(hidden_ref[...], weight).astype(bf16)
    key_ref[...] = projected[:, LANES : 2 * LANES]
    query = projected[:, :LANES].astype(f32).T * score_scale
    query_t_ref[...] = query.astype(bf16)
    base2_t_ref[...] = (query * log2_e).astype(bf16)
    key_t_ref[...] = projected[:, LANES : 2 * LANES].astype(f32).T.astype(bf16)
    value_t_ref[...] = projected[:, 2 * LANES :].astype(f32).T.astype(bf16)


def project(blocks, weight, column, hidden_space, space):
    row_count = blocks[0].shape[0]
    step_rows = row_count
    features = weight.shape[1]
    width = pl.BlockSpec((step_rows, LANES), lambda i, c: (i, 0))
    tall = pl.BlockSpec((LANES, step_rows), lambda i, c: (0, i))
    normal = lambda t: space((row_count, LANES), t)
    turned = space((LANES, row_count), bf16)
    return pl.pallas_call(
        project_body,
        grid_spec=pltpu.PrefetchScalarGridSpec(
            num_scalar_prefetch=1,
            grid=(row_count // step_rows,),
            in_specs=[width] * 4 + [pl.BlockSpec(weight.shape, lambda i, c: (0, 0, 0))],
            out_specs=[
                pl.BlockSpec((step_rows, features), lambda i, c: (i, 0)),
                tall,
                pl.BlockSpec((8, step_rows), lambda i, c: (0, i)),
                width,
            ]
            + [tall] * 4,
        ),
        out_shape=[hidden_space((row_count, features), bf16)]
        + [pltpu.HBM((LANES, row_count), f32), pltpu.HBM((8, row_count), f32)]
        + [normal(bf16)]
        + [turned] * 4,
        compiler_params=params(12),
        cost_estimate=cost(4 * row_count * features * 3 * LANES, row_count * LANES * 40),
        name="project",
    )(column, *blocks, weight)


def forward_body(
    key_ref,
    base2_t_ref,
    query_t_ref,
    key_t_ref,
    value_t_ref,
    exp_ref,
    attended_ref,
    inverse_ref,
    covariance_ref,
    safe_ref,
):
    head = pl.program_id(0)
    at = pl.multiple_of(head * HD, HD)

    @pl.when(head == 0)
    def _():
        def largest(ref):
            squares = jnp.square(ref[...].astype(f32)).reshape(LANES // HD, HD, PATCH)
            return jnp.max(jnp.sum(squares, axis=1), axis=1, keepdims=True)

        bound = jnp.max(largest(base2_t_ref) * largest(key_t_ref))
        safe_ref[0] = (bound <= SAFE_SCORE * SAFE_SCORE).astype(i32)

    def attend(shifted):
        in_head = lax.broadcasted_iota(i32, (LANES, 1), 0) // HD == head
        query_ref = query_t_ref if shifted else base2_t_ref
        keys = key_t_ref[pl.ds(at, HD), :].astype(f32)
        values = value_t_ref[pl.ds(at, HD), :].astype(f32)
        middle = jnp.mean(values, axis=1, keepdims=True)
        centered = values - middle
        features = [centered[j : j + 1] * keys for j in range(HD)]
        features += [keys, values, jnp.ones((HD, PATCH), f32)]
        features = jnp.concatenate([f.astype(bf16) for f in features], axis=0)

        def finish(weights, columns):
            sums = dot(features, weights)
            inverse = 1.0 / sums[(HD + 2) * HD : (HD + 2) * HD + 1]
            inverse_ref[0, :, columns] = inverse
            mean_key = sums[HD * HD : (HD + 1) * HD] * inverse
            mean_value = sums[(HD + 1) * HD : (HD + 2) * HD] * inverse
            attended_ref[pl.ds(at, HD), columns] = mean_value.astype(bf16)
            offset = mean_value - middle
            for j in range(HD):
                crossed = sums[j * HD : (j + 1) * HD] * inverse - offset[j : j + 1] * mean_key
                covariance_ref[0, j * HD : (j + 1) * HD, columns] = crossed.astype(bf16)

        before = None
        for start in range(0, PATCH, QUERY_BLOCK):
            columns = slice(start, start + QUERY_BLOCK)
            query = jnp.where(in_head, query_ref[:, columns], jnp.zeros((), bf16))
            scores = dot(key_ref[...], query)
            if shifted:
                scores = (scores - jnp.max(scores, axis=0, keepdims=True)) * log2_e
            weights = jnp.exp2(scores).astype(bf16)
            exp_ref[0, :, columns] = weights
            if before is not None:
                finish(*before)
            before = (weights, columns)
        finish(*before)

    @pl.when(safe_ref[0] == 1)
    def _():
        attend(False)

    @pl.when(safe_ref[0] == 0)
    def _():
        attend(True)


def attention_forward(keys, base2_t, query_t, key_t, value_t, space):
    heads = LANES // HD
    tall = pl.BlockSpec((LANES, PATCH), lambda h: (0, 0))
    per_head = lambda h: (h, 0, 0)
    elements = heads * PATCH * PATCH
    return pl.pallas_call(
        forward_body,
        grid=(heads,),
        in_specs=[pl.BlockSpec((PATCH, LANES), lambda h: (0, 0))] + [tall] * 4,
        out_specs=[
            pl.BlockSpec((1, PATCH, PATCH), per_head),
            tall,
            pl.BlockSpec((1, 1, PATCH), per_head),
            pl.BlockSpec((1, HD * HD, PATCH), per_head),
        ],
        out_shape=[
            space((heads, PATCH, PATCH), bf16),
            space((LANES, PATCH), bf16),
            pltpu.VMEM((heads, 1, PATCH), f32),
            space((heads, HD * HD, PATCH), bf16),
        ],
        scratch_shapes=[pltpu.SMEM((1,), i32)],
        compiler_params=params(16),
        cost_estimate=cost(1360 * elements, 2 * elements, elements),
        name="attention_forward",
    )(keys, base2_t, query_t, key_t, value_t)


def backward_body(first, *refs):
    (
        column_ref,
        exp_ref,
        inverse_ref,
        query_t_ref,
        value_t_ref,
        attended_ref,
        g0_ref,
        g1_ref,
        g2_ref,
        g3_ref,
        weight_ref,
        covariance_ref,
        *refs,
    ) = refs
    if first:
        later_exp_ref, *refs = refs
    else:
        rest_ref, *refs = refs
    d_out_ref, d_query_ref, d_key_ref, d_value_ref, *refs = refs
    if first:
        staged_ref, d_attended_ref, staged_sem = refs
        staged = pltpu.make_async_copy(
            later_exp_ref.at[pl.ds(0, STAGED_HEADS)], staged_ref, staged_sem
        )
    else:
        d_attended_ref, exp_all_ref, exp_sems, covariance_all_ref, covariance_sems = refs
    head = pl.program_id(0)
    at = pl.multiple_of(head * HD, HD)

    def exp_copy(h):
        return pltpu.make_async_copy(
            rest_ref.at[h + STAGED_HEADS], exp_all_ref.at[h], exp_sems.at[h]
        )

    def covariance_copy(h):
        return pltpu.make_async_copy(
            covariance_ref.at[h], covariance_all_ref.at[h], covariance_sems.at[h]
        )

    @pl.when(head == 0)
    def _():
        if first:
            staged.start()
        else:
            for h in range(LANES // HD):
                if h >= STAGED_HEADS:
                    exp_copy(h - STAGED_HEADS).start()
                covariance_copy(h).start()
        me = column_ref[0]
        for block, mask in zip((g0_ref, g1_ref, g2_ref, g3_ref), BLOCK_MASKS):
            start = pl.multiple_of((me ^ mask) * LANES, LANES)
            d_out_ref[pl.ds(start, LANES), :] = block[...]
        d_attended_ref[...] = dot(weight_ref[...].T, d_out_ref[...]).astype(bf16)

    def one_head(weights):
        grads = d_attended_ref[pl.ds(at, HD), :].astype(f32)
        query = query_t_ref[pl.ds(at, HD), :].astype(f32)
        values = value_t_ref[pl.ds(at, HD), :].astype(f32)
        inverse = inverse_ref[0]
        middle = jnp.mean(values, axis=1, keepdims=True)
        centered = values - middle
        offset = attended_ref[pl.ds(at, HD), :].astype(f32) - middle
        scaled = grads * inverse
        delta = jnp.sum(scaled * offset, axis=0, keepdims=True)
        features = [scaled[j : j + 1] * query for j in range(HD)] + [delta * query, scaled]
        sums = dot_rows(jnp.concatenate([f.astype(bf16) for f in features], axis=0), weights())
        d_value_ref[pl.ds(at, HD), :] = sums[(HD + 1) * HD :].astype(bf16)
        if first:
            covariance = covariance_ref.at[0]
        else:
            covariance_copy(head).wait()
            covariance = covariance_all_ref.at[head]
        d_key = centered[0:1] * sums[:HD]
        d_query = grads[0:1] * covariance[:HD, :].astype(f32)
        for j in range(1, HD):
            rows = slice(j * HD, (j + 1) * HD)
            d_key += centered[j : j + 1] * sums[rows]
            d_query += grads[j : j + 1] * covariance[rows, :].astype(f32)
        d_key_ref[pl.ds(at, HD), :] = (d_key - sums[HD * HD : (HD + 1) * HD]).astype(bf16)
        d_query_ref[pl.ds(at, HD), :] = (d_query * score_scale).astype(bf16)

    if first:
        one_head(lambda: exp_ref[0])

        @pl.when(head == pl.num_programs(0) - 1)
        def _():
            staged.wait()

    else:

        @pl.when(head < STAGED_HEADS)
        def _():
            one_head(lambda: exp_ref[0])

        @pl.when(head >= STAGED_HEADS)
        def _():
            exp_copy(head - STAGED_HEADS).wait()
            one_head(lambda: exp_all_ref[head - STAGED_HEADS])


def attention_backward(
    patch, first, weights, other, inverse, covariance, query_t, value_t, attended, grads, weight, column
):
    features = weight.shape[0]
    heads = LANES // HD
    tall = pl.BlockSpec((LANES, PATCH), lambda h, c: (0, 0))
    part = pl.BlockSpec((LANES, PATCH), lambda h, c: (0, patch))
    per_head = lambda h, c: (h, 0, 0)
    kept_head = lambda h, c: (jnp.minimum(h, weights.shape[0] - 1), 0, 0)
    hbm = pl.BlockSpec(memory_space=pltpu.HBM)
    elements = heads * PATCH * PATCH
    turned = pltpu.VMEM((LANES, PATCH), bf16)
    in_specs = [
        pl.BlockSpec((1, PATCH, PATCH), kept_head),
        pl.BlockSpec((1, 1, PATCH), per_head),
        tall,
        tall,
        tall,
        part,
        part,
        part,
        part,
        pl.BlockSpec(weight.shape, lambda h, c: (0, 0)),
        pl.BlockSpec((1, HD * HD, PATCH), per_head) if first else hbm,
        hbm,
    ]
    operands = [weights, inverse, query_t, value_t, attended, *grads, weight, covariance, other]
    out_specs = [pl.BlockSpec((features, PATCH), lambda h, c: (0, 0)), tall, tall, tall]
    out_shape = [pltpu.VMEM((features, PATCH), bf16), turned, turned, turned]
    scratch = [pltpu.VMEM((LANES, PATCH), bf16)]
    if first:
        out_specs.append(pl.BlockSpec(memory_space=pl.ANY))
        out_shape.append(pltpu.VMEM((STAGED_HEADS, PATCH, PATCH), bf16))
        scratch.append(pltpu.SemaphoreType.DMA(()))
    else:
        rest = heads - STAGED_HEADS
        scratch += [pltpu.VMEM((rest, PATCH, PATCH), bf16), pltpu.SemaphoreType.DMA((rest,))]
        scratch += [pltpu.VMEM((heads, HD * HD, PATCH), bf16), pltpu.SemaphoreType.DMA((heads,))]
    return pl.pallas_call(
        functools.partial(backward_body, first),
        grid_spec=pltpu.PrefetchScalarGridSpec(
            num_scalar_prefetch=1,
            grid=(heads,),
            in_specs=in_specs,
            out_specs=out_specs,
            scratch_shapes=scratch,
        ),
        out_shape=out_shape,
        compiler_params=params(9 if first else 27),
        cost_estimate=cost(1100 * elements, 2 * elements),
        name="attention_backward",
    )(column, *operands)


def whole(shape, dtype):
    return jax.ShapeDtypeStruct(shape, dtype)


def weight_grad_body(*refs):
    d_query_ref, d_key_ref, d_value_ref, attended_ref, hidden_ref, d_out_ref, *before, out_ref = refs
    d_projected = jnp.concatenate([d_query_ref[...], d_key_ref[...], d_value_ref[...]], axis=0)
    projections = dot(d_projected, hidden_ref[...])
    output = dot_rows(attended_ref[...], d_out_ref[...])
    if before:
        out_ref[:, : 3 * LANES] = (before[0][: 3 * LANES, :] + projections).T.astype(bf16)
        out_ref[:, 3 * LANES :] = (before[0][3 * LANES :, :] + output).T.astype(bf16)
    else:
        out_ref[: 3 * LANES, :] = projections
        out_ref[3 * LANES :, :] = output


def weight_grads(*operands):
    features = operands[4].shape[1]
    work = 2 * PATCH * features * LANES
    last = len(operands) > 6
    return pl.pallas_call(
        weight_grad_body,
        out_shape=whole((features, 4 * LANES), bf16) if last else pltpu.VMEM((4 * LANES, features), f32),
        compiler_params=params(12),
        cost_estimate=cost(4 * work, 12 * PATCH * features),
        name="weight_grads",
    )(*operands)


def split_sums(sums):
    high = sums.astype(bf16)
    low = (sums - high.astype(f32)).astype(bf16)
    pad = jnp.zeros((INDEX_ROWS - 2 * sums.shape[0], sums.shape[1]), f32)
    return jnp.concatenate([high.astype(f32), low.astype(f32), pad], axis=0).astype(bf16)


def join_sums(rows):
    rows = rows.astype(f32)
    return rows[0:2] + rows[2:4]


def partial_body(
    column_ref,
    d_query_ref,
    d_key_ref,
    d_value_ref,
    query_ref,
    key_ref,
    value_ref,
    weight_ref,
    mine_ref,
    other_ref,
    sums_ref,
):
    me = column_ref[0]
    d_projected = jnp.concatenate([d_query_ref[...], d_key_ref[...], d_value_ref[...]], axis=0)
    plain = jnp.zeros((1, PATCH), f32)
    for j, mask in enumerate(BLOCK_MASKS):
        start = pl.multiple_of((me ^ mask) * LANES, LANES)
        rows = [weight_ref[t, pl.ds(start, LANES), :] for t in range(3)]
        block = dot(jnp.concatenate(rows, axis=1), d_projected).astype(bf16)
        plain += jnp.sum(block.astype(f32), axis=0, keepdims=True)
        to = mine_ref if j < 2 else other_ref
        to[(j % 2) * LANES : (j % 2 + 1) * LANES, :] = block
    crossed = (
        d_query_ref[...].astype(f32) * (query_ref[...].astype(f32) / score_scale)
        + d_key_ref[...].astype(f32) * key_ref[...].astype(f32)
        + d_value_ref[...].astype(f32) * value_ref[...].astype(f32)
    )
    sums = jnp.concatenate([plain, jnp.sum(crossed, axis=0, keepdims=True)], axis=0)
    sums_ref[...] = sums
    other_ref[2 * LANES :, :] = split_sums(sums)


def hidden_part(d_query, d_key, d_value, query, key, value, weight, column):
    features = weight.shape[1]
    return pl.pallas_call(
        partial_body,
        in_specs=[pl.BlockSpec(memory_space=pltpu.SMEM)] + [pl.BlockSpec(memory_space=pltpu.VMEM)] * 7,
        out_shape=[
            pltpu.VMEM((2 * LANES, PATCH), bf16),
            pltpu.VMEM((2 * LANES + INDEX_ROWS, PATCH), bf16),
            pltpu.VMEM((2, PATCH), f32),
        ],
        compiler_params=params(12),
        cost_estimate=cost(6 * PATCH * features * LANES, 4 * PATCH * features),
        name="hidden_part",
    )(column, d_query, d_key, d_value, query, key, value, weight)


def pair_body(mine_ref, sums_ref, got_ref, kept_ref, sums_out_ref, sent_ref):
    pair = mine_ref[...].astype(f32) + got_ref[: 2 * LANES, :].astype(f32)
    sums = sums_ref[...] + join_sums(got_ref[2 * LANES :, :])
    kept_ref[...] = pair[:LANES]
    sums_out_ref[...] = sums
    sent_ref[:LANES, :] = pair[LANES:].astype(bf16)
    sent_ref[LANES:, :] = split_sums(sums)


def pair_sum(mine, sums, got):
    return pl.pallas_call(
        pair_body,
        out_shape=[
            pltpu.VMEM((LANES, PATCH), f32),
            pltpu.VMEM((2, PATCH), f32),
            pltpu.VMEM((LANES + INDEX_ROWS, PATCH), bf16),
        ],
        compiler_params=params(6),
        cost_estimate=cost(4 * LANES * PATCH, 16 * LANES * PATCH),
        name="pair_sum",
    )(mine, sums, got)


def points_body(kept_ref, sums_ref, got_ref, d_out_ref, normed_ref, inv_ref, *rest):
    out_ref = rest[-1]
    features = 4.0 * LANES
    means = (sums_ref[...] + join_sums(got_ref[LANES:, :])) / features
    d_hidden = kept_ref[...] + got_ref[:LANES, :].astype(f32) - means[0:1]
    inner = d_hidden - normed_ref[...] * means[1:2]
    out_ref[...] = (d_out_ref[...].astype(f32) + inv_ref[0:1] * inner).T


def points_grad(patch, patches, kept, sums, got, d_out, normed, inv_scale, before):
    full = lambda a: pl.BlockSpec(a.shape, lambda i: (0, 0))
    in_specs = [full(kept), full(sums), full(got), pl.BlockSpec((LANES, PATCH), lambda i: (0, patch))]
    in_specs += [full(normed), full(inv_scale)]
    operands = [kept, sums, got, d_out, normed, inv_scale]
    if before is not None:
        in_specs.append(pl.BlockSpec(memory_space=pl.ANY))
        operands.append(before)
    return pl.pallas_call(
        points_body,
        grid=(1,),
        in_specs=in_specs,
        out_specs=pl.BlockSpec((PATCH, LANES), lambda i: (patch, 0)),
        out_shape=whole((patches * PATCH, LANES), f32),
        input_output_aliases={} if before is None else {len(operands) - 1: 0},
        compiler_params=params(8),
        cost_estimate=cost(8 * LANES * PATCH, 24 * LANES * PATCH),
        name="points_grad",
    )(*operands)


def grad_sum_body(parts_ref, qkv_ref, out_ref):
    total = parts_ref[0].astype(f32)
    for j in range(1, parts_ref.shape[0]):
        total += parts_ref[j].astype(f32)
    for t in range(3):
        qkv_ref[t] = total[:, t * LANES : (t + 1) * LANES]
    out_ref[...] = total[:, 3 * LANES :]


def grad_sum(parts):
    shards, rows, width = parts.shape
    return pl.pallas_call(
        grad_sum_body,
        out_shape=[whole((3, rows, LANES), f32), whole((rows, LANES), f32)],
        compiler_params=params(8),
        cost_estimate=cost(shards * rows * width, 4 * shards * rows * width),
        name="grad_sum",
    )(parts)


def local(
    scan_points,
    send_order,
    arrive_order,
    qkv_weight,
    out_weight,
    voxel_grads,
    voxel_shard,
    voxel_point,
):
    shards = lax.axis_size("seq")
    members = lax.axis_size("mp")
    local_rows, features = scan_points.shape
    voxels = voxel_grads.shape[0]
    capacity = 2 * voxels // shards
    patches = local_rows // PATCH
    column = lax.axis_index("mp").astype(i32).reshape(1)
    zero = jnp.zeros((1,), i32)
    weight = qkv_weight.transpose(1, 0, 2)

    def swap(rows, mask):
        return lax.ppermute(rows, "mp", [(i, i ^ mask) for i in range(members)])

    def exchange(rows):
        return lax.all_to_all(rows, "seq", split_axis=0, concat_axis=0, tiled=True)

    def after(value, first):
        return lax.optimization_barrier((value, first))

    def in_hbm(value):
        return pltpu.with_memory_space_constraint(value, pltpu.HBM)

    arrived = exchange(permute_rows(scan_points, send_order, column, 0, 1, whole, 60))
    buckets = bucket_rows(voxel_grads, voxel_shard, voxel_point, column, shards, capacity)
    owns = [
        permute_rows(arrived, arrive_order, zero, p, patches, pltpu.VMEM, 12)
        for p in range(patches)
    ]
    buckets, owns[0] = after(buckets, owns[0])
    got = exchange(buckets.reshape(shards * (capacity + INDEX_ROWS), LANES))
    across = [swap(own, 2) for own in owns]
    across[0], owns[1] = after(across[0], owns[1])

    def project_patch(p):
        columns = (owns[p], across[p], swap(owns[p], 1), swap(across[p], 1))
        return project(columns, weight, column, pltpu.HBM, pltpu.VMEM if p == 0 else pltpu.HBM)

    def forward(p, projected):
        space = pltpu.VMEM if p == patches - 1 else pltpu.HBM
        return attention_forward(*projected[3:], space)

    projected0 = project_patch(0)
    forward0 = forward(0, projected0)
    across[1], forward0 = after(across[1], forward0)
    projected1 = project_patch(1)
    got, projected1 = after(got, projected1)
    summed_rows = segment_rows(got.reshape(shards, capacity + INDEX_ROWS, LANES), local_rows)
    summed_across = swap(summed_rows, 2)
    projected1, summed_rows = after(projected1, summed_rows)
    forward1 = forward(1, projected1)
    summed_across, forward1 = after(summed_across, forward1)
    grads = (summed_rows, summed_across, swap(summed_rows, 1), swap(summed_across, 1))
    forwards = [(projected0, forward0), (projected1, forward1)]

    kept, sums, received = {}, {}, {}
    for p in reversed(range(patches)):
        (hidden, _, _, _, _, query_t, key_t, value_t), (weights, attended, inverse, covariance) = forwards[p]
        if p == 0:
            weights, sent = after(weights, sent)
            received[1] = swap(sent, 2)
            other_exp, covariance, weights = in_hbm(weights), in_hbm(covariance), staged[0]
        else:
            other_exp = in_hbm(forwards[0][1][0])
        d_out, d_query, d_key, d_value, *staged = attention_backward(
            p, p > 0, weights, other_exp, inverse, covariance, query_t, value_t, attended, grads, out_weight, column
        )
        if p == 0:
            received[1], d_query = after(received[1], d_query)
        grad_operands = (d_query, d_key, d_value, attended, hidden, d_out)
        if p == 0:
            weight_parts = weight_grads(*grad_operands, first_parts)
            operands = (d_query, d_key, d_value, query_t, key_t, value_t)
            operands, weight_parts = after(operands, weight_parts)
            d_query, d_key, d_value, query_t, key_t, value_t = map(in_hbm, operands)
        mine, other, own_sums = hidden_part(d_query, d_key, d_value, query_t, key_t, value_t, weight, column)
        partner = swap(other, 1)
        if p > 0:
            first_parts = weight_grads(*grad_operands)
            partner, first_parts = after(partner, first_parts)
        kept[p], sums[p], sent = pair_sum(mine, own_sums, partner)
    received[0] = swap(sent, 2)
    d_points = None
    for p in reversed(range(patches)):
        normed, inv_scale = forwards[p][0][1:3]
        if p > 0:
            normed, inv_scale = in_hbm(normed), in_hbm(inv_scale)
        d_points = points_grad(
            p, patches, kept[p], sums[p], received[p], grads[0], normed, inv_scale, d_points
        )
    parts = exchange(weight_parts).reshape(shards, features // shards, 4 * LANES)
    grad_qkv, grad_out = grad_sum(parts)
    return (d_points, grad_qkv.transpose(1, 0, 2), grad_out)


def solution(mesh):
    in_specs = (
        P("seq", None),
        P("seq"),
        P("seq"),
        P(None, None, "mp"),
        P(None, "mp"),
        P("seq", None),
        P("seq", None),
        P("seq"),
    )
    out_specs = (P("seq", "mp"), P("seq", None, "mp"), P("seq", "mp"))
    return jax.shard_map(local, mesh=mesh, in_specs=in_specs, out_specs=out_specs, check_vma=False)
```

```python
import functools

import jax
import jax.numpy as jnp
from jax import lax
from jax.experimental import pallas as pl
from jax.experimental.pallas import tpu as pltpu
from jax.sharding import PartitionSpec as P

HD = 16
PATCH = 1024
LANES = 128
INDEX_ROWS = 16
INDEX_BASE = 64
BLOCK_MASKS = (0, 2, 1, 3)
SAFE_SCORE = 60.0
QUERY_BLOCK = 256
STAGED_HEADS = 1
SEGMENT_SHARDS = 8
BUCKET_SHARDS = 4

score_scale = 0.25
epsilon = 1e-05
log2_e = 1.4426950408889634

f32 = jnp.float32
bf16 = jnp.bfloat16
i32 = jnp.int32

ROWS_BY_ROWS = (((1,), (1,)), ((), ()))


def params(mib):
    return pltpu.CompilerParams(vmem_limit_bytes=mib << 20)


def cost(flops, bytes_accessed, transcendentals=0):
    return pl.CostEstimate(
        flops=int(flops), bytes_accessed=int(bytes_accessed), transcendentals=int(transcendentals)
    )


def dot(a, b):
    return jnp.dot(a, b, preferred_element_type=f32)


def dot_rows(a, b):
    return lax.dot_general(a, b, ROWS_BY_ROWS, preferred_element_type=f32)


def ones_where(mask):
    return jnp.where(mask, 1.0, 0.0).astype(bf16)


def permute_body(column_ref, order_ref, block_ref, out_ref):
    step = pl.program_id(0)
    half = block_ref.shape[0] // 2
    chunks = out_ref.shape[0] // LANES
    lane = lax.broadcasted_iota(i32, (LANES, LANES), 1)
    sides = jnp.concatenate([block_ref[:half, :], block_ref[half:, :]], axis=1)
    onehots, lows = [], []
    for j in range(chunks):
        wanted = order_ref[pl.ds(step * chunks + j, 1), :].astype(f32)
        wanted = jnp.broadcast_to(wanted, (LANES, LANES)).T.astype(i32)
        low = wanted < half
        local_row = jnp.where(low, wanted, wanted - half)
        onehots.append(
            jnp.concatenate(
                [ones_where(local_row == lane + k * LANES) for k in range(half // LANES)], axis=1
            )
        )
        lows.append(low)
    both = dot(jnp.concatenate(onehots, axis=0), sides)
    for j in range(chunks):
        rows = slice(j * LANES, (j + 1) * LANES)
        out_ref[rows, :] = jnp.where(lows[j], both[rows, :LANES], both[rows, LANES:]).astype(bf16)


def permute_rows(rows, order, column, part, parts, out, mib):
    row_count = order.shape[0] // parts
    groups = row_count // LANES
    step_rows = min(2048, row_count)
    return pl.pallas_call(
        permute_body,
        grid_spec=pltpu.PrefetchScalarGridSpec(
            num_scalar_prefetch=1,
            grid=(row_count // step_rows,),
            in_specs=[
                pl.BlockSpec((groups, LANES), lambda i, c: (part, 0)),
                pl.BlockSpec((rows.shape[0], LANES), lambda i, c: (0, c[0])),
            ],
            out_specs=pl.BlockSpec((step_rows, LANES), lambda i, c: (i, 0)),
        ),
        out_shape=out((row_count, LANES), bf16),
        compiler_params=params(mib),
        cost_estimate=cost(2 * row_count * LANES, row_count),
        name="permute_rows",
    )(column, order.reshape(parts * groups, LANES), rows)


def bucket_body(shards, capacity, column_ref, shard_ref, point_ref, grads_ref, out_ref, place_ref):
    step = pl.program_id(0)
    row_count = grads_ref.shape[0]
    groups = row_count // LANES

    @pl.when(step == 0)
    def _():
        targets = shard_ref[...]
        masks = [ones_where(targets == t) for t in range(shards)]
        stacked = jnp.concatenate(masks, axis=0)
        above = ones_where(
            lax.broadcasted_iota(i32, (LANES, LANES), 0)
            < lax.broadcasted_iota(i32, (LANES, LANES), 1)
        )
        earlier = ones_where(
            lax.broadcasted_iota(i32, (groups, groups), 1)
            < lax.broadcasted_iota(i32, (groups, groups), 0)
        )
        in_row = dot(stacked, above)
        places = jnp.zeros((groups, LANES), f32)
        for t in range(shards):
            rows_before = jnp.sum(dot(earlier, masks[t]), axis=1, keepdims=True)
            place = in_row[t * groups : (t + 1) * groups] + rows_before + float(t * capacity)
            places = jnp.where(targets == t, place, places)
        place_ref[...] = places.astype(i32)

    points = jnp.concatenate([point_ref[j : j + 1, :] for j in range(groups)], axis=1)
    high = points // INDEX_BASE
    low = points - high * INDEX_BASE
    digits = jnp.concatenate(
        [high.astype(f32), low.astype(f32), jnp.zeros((INDEX_ROWS - 2, row_count), f32)], axis=0
    )
    group = out_ref.shape[0]
    chunks = capacity // LANES
    slot = lax.broadcasted_iota(i32, (group * capacity, LANES), 0) + step * (group * capacity)
    onehot = jnp.concatenate(
        [ones_where(place_ref[j : j + 1, :] == slot) for j in range(groups)], axis=1
    )
    filled = dot(onehot, grads_ref[...]).astype(bf16)
    sent = dot_rows(digits.astype(bf16), onehot)
    for shard in range(group):
        start = shard * capacity
        out_ref[shard, :capacity, :] = filled[start : start + capacity]
        rows = [
            sent[d : d + 1, start + j * LANES : start + (j + 1) * LANES]
            for d in range(2)
            for j in range(chunks)
        ]
        rows.append(jnp.zeros((INDEX_ROWS - 2 * chunks, LANES), f32))
        out_ref[shard, capacity:, :] = jnp.concatenate(rows, axis=0).astype(bf16)


def bucket_rows(grads, targets, points, column, shards, capacity):
    row_count = grads.shape[0]
    groups = row_count // LANES
    group = BUCKET_SHARDS if shards % BUCKET_SHARDS == 0 else 1
    return pl.pallas_call(
        functools.partial(bucket_body, shards, capacity),
        grid_spec=pltpu.PrefetchScalarGridSpec(
            num_scalar_prefetch=1,
            grid=(shards // group,),
            in_specs=[
                pl.BlockSpec((groups, LANES), lambda i, c: (0, 0)),
                pl.BlockSpec((groups, LANES), lambda i, c: (0, 0)),
                pl.BlockSpec((row_count, LANES), lambda i, c: (0, c[0])),
            ],
            out_specs=pl.BlockSpec((group, capacity + INDEX_ROWS, LANES), lambda i, c: (i, 0, 0)),
            scratch_shapes=[pltpu.VMEM((groups, LANES), i32)],
        ),
        out_shape=jax.ShapeDtypeStruct((shards, capacity + INDEX_ROWS, LANES), bf16),
        compiler_params=params(60),
        cost_estimate=cost(
            8 * shards * capacity * row_count * LANES, 3 * shards * capacity * LANES * 2
        ),
        name="bucket_rows",
    )(column, targets.reshape(groups, LANES), points.reshape(groups, LANES), grads)


def segment_body(got_ref, out_ref, total_ref):
    step = pl.program_id(0)
    capacity = got_ref.shape[1] - INDEX_ROWS
    chunks = capacity // LANES
    half = total_ref.shape[0]
    row = lax.broadcasted_iota(i32, (half, LANES), 0)
    onehots, sides = [], []
    for shard in range(got_ref.shape[0]):
        digits = got_ref[shard, capacity:, :].astype(f32)
        index = digits[:chunks] * float(INDEX_BASE) + digits[chunks : 2 * chunks]
        position = index.astype(i32)
        local_row = jnp.where(position < half, position, position - half)
        for j in range(chunks):
            onehots.append(ones_where(local_row[j : j + 1] == row))
            low = jnp.broadcast_to(index[j : j + 1], (LANES, LANES)).T < float(half)
            rows = got_ref[shard, j * LANES : (j + 1) * LANES, :].astype(f32)
            both = [jnp.where(low, rows, 0.0), jnp.where(low, 0.0, rows)]
            sides.append(jnp.concatenate(both, axis=1).astype(bf16))
    part = dot(jnp.concatenate(onehots, axis=1), jnp.concatenate(sides, axis=0))

    @pl.when(step == 0)
    def _():
        total_ref[...] = part

    @pl.when(step > 0)
    def _():
        total_ref[...] += part

    @pl.when(step == pl.num_programs(0) - 1)
    def _():
        out_ref[:, :half] = total_ref[:, :LANES].T.astype(bf16)
        out_ref[:, half:] = total_ref[:, LANES:].T.astype(bf16)


def segment_rows(got, row_count):
    shards, message, _ = got.shape
    group = SEGMENT_SHARDS if shards % SEGMENT_SHARDS == 0 else 1
    return pl.pallas_call(
        segment_body,
        grid=(shards // group,),
        in_specs=[pl.BlockSpec((group, message, LANES), lambda i: (i, 0, 0))],
        out_specs=pl.BlockSpec((LANES, row_count), lambda i: (0, 0)),
        out_shape=pltpu.VMEM((LANES, row_count), bf16),
        scratch_shapes=[pltpu.VMEM((row_count // 2, 2 * LANES), f32)],
        compiler_params=params(40),
        cost_estimate=cost(
            8 * shards * message * row_count * LANES, 3 * shards * message * LANES * 2
        ),
        name="segment_rows",
    )(got)


def project_body(
    column_ref,
    x0_ref,
    x1_ref,
    x2_ref,
    x3_ref,
    weight_ref,
    hidden_ref,
    normed_ref,
    inv_ref,
    key_ref,
    base2_t_ref,
    query_t_ref,
    key_t_ref,
    value_t_ref,
):
    me = column_ref[0]
    blocks = [r[...].astype(f32) for r in (x0_ref, x1_ref, x2_ref, x3_ref)]
    features = float(LANES * len(blocks))
    mean = jnp.sum(blocks[0] + blocks[1] + (blocks[2] + blocks[3]), axis=1, keepdims=True) / features
    centered = [b - mean for b in blocks]
    squares = [c * c for c in centered]
    var = jnp.sum(squares[0] + squares[1] + (squares[2] + squares[3]), axis=1, keepdims=True) / features
    inv = lax.rsqrt(var + epsilon)
    normed_ref[...] = (centered[0] * inv).T
    inv_ref[...] = jnp.broadcast_to(inv, centered[0].shape).T[:8]
    for block, mask in zip(centered, BLOCK_MASKS):
        at = pl.multiple_of((me ^ mask) * LANES, LANES)
        hidden_ref[:, pl.ds(at, LANES)] = (block * inv).astype(bf16)
    weight = jnp.concatenate([weight_ref[t] for t in range(3)], axis=1)
    projected = dot(hidden_ref[...], weight).astype(bf16)
    key_ref[...] = projected[:, LANES : 2 * LANES]
    query = projected[:, :LANES].astype(f32).T * score_scale
    query_t_ref[...] = query.astype(bf16)
    base2_t_ref[...] = (query * log2_e).astype(bf16)
    key_t_ref[...] = projected[:, LANES : 2 * LANES].astype(f32).T.astype(bf16)
    value_t_ref[...] = projected[:, 2 * LANES :].astype(f32).T.astype(bf16)


def project(blocks, weight, column, hidden_space, space):
    row_count = blocks[0].shape[0]
    step_rows = row_count
    features = weight.shape[1]
    width = pl.BlockSpec((step_rows, LANES), lambda i, c: (i, 0))
    tall = pl.BlockSpec((LANES, step_rows), lambda i, c: (0, i))
    normal = lambda t: space((row_count, LANES), t)
    turned = space((LANES, row_count), bf16)
    return pl.pallas_call(
        project_body,
        grid_spec=pltpu.PrefetchScalarGridSpec(
            num_scalar_prefetch=1,
            grid=(row_count // step_rows,),
            in_specs=[width] * 4 + [pl.BlockSpec(weight.shape, lambda i, c: (0, 0, 0))],
            out_specs=[
                pl.BlockSpec((step_rows, features), lambda i, c: (i, 0)),
                tall,
                pl.BlockSpec((8, step_rows), lambda i, c: (0, i)),
                width,
            ]
            + [tall] * 4,
        ),
        out_shape=[hidden_space((row_count, features), bf16)]
        + [pltpu.HBM((LANES, row_count), f32), pltpu.HBM((8, row_count), f32)]
        + [normal(bf16)]
        + [turned] * 4,
        compiler_params=params(12),
        cost_estimate=cost(4 * row_count * features * 3 * LANES, row_count * LANES * 40),
        name="project",
    )(column, *blocks, weight)


def forward_body(
    key_ref,
    base2_t_ref,
    query_t_ref,
    key_t_ref,
    value_t_ref,
    exp_ref,
    attended_ref,
    inverse_ref,
    covariance_ref,
    safe_ref,
):
    head = pl.program_id(0)
    at = pl.multiple_of(head * HD, HD)

    @pl.when(head == 0)
    def _():
        def largest(ref):
            squares = jnp.square(ref[...].astype(f32)).reshape(LANES // HD, HD, PATCH)
            return jnp.max(jnp.sum(squares, axis=1), axis=1, keepdims=True)

        bound = jnp.max(largest(base2_t_ref) * largest(key_t_ref))
        safe_ref[0] = (bound <= SAFE_SCORE * SAFE_SCORE).astype(i32)

    def attend(shifted):
        in_head = lax.broadcasted_iota(i32, (LANES, 1), 0) // HD == head
        query_ref = query_t_ref if shifted else base2_t_ref
        keys = key_t_ref[pl.ds(at, HD), :].astype(f32)
        values = value_t_ref[pl.ds(at, HD), :].astype(f32)
        middle = jnp.mean(values, axis=1, keepdims=True)
        centered = values - middle
        features = [centered[j : j + 1] * keys for j in range(HD)]
        features += [keys, values, jnp.ones((HD, PATCH), f32)]
        features = jnp.concatenate([f.astype(bf16) for f in features], axis=0)

        def finish(weights, columns):
            sums = dot(features, weights)
            inverse = 1.0 / sums[(HD + 2) * HD : (HD + 2) * HD + 1]
            inverse_ref[0, :, columns] = inverse
            mean_key = sums[HD * HD : (HD + 1) * HD] * inverse
            mean_value = sums[(HD + 1) * HD : (HD + 2) * HD] * inverse
            attended_ref[pl.ds(at, HD), columns] = mean_value.astype(bf16)
            offset = mean_value - middle
            for j in range(HD):
                crossed = sums[j * HD : (j + 1) * HD] * inverse - offset[j : j + 1] * mean_key
                covariance_ref[0, j * HD : (j + 1) * HD, columns] = crossed.astype(bf16)

        before = None
        for start in range(0, PATCH, QUERY_BLOCK):
            columns = slice(start, start + QUERY_BLOCK)
            query = jnp.where(in_head, query_ref[:, columns], jnp.zeros((), bf16))
            scores = dot(key_ref[...], query)
            if shifted:
                scores = (scores - jnp.max(scores, axis=0, keepdims=True)) * log2_e
            weights = jnp.exp2(scores).astype(bf16)
            exp_ref[0, :, columns] = weights
            if before is not None:
                finish(*before)
            before = (weights, columns)
        finish(*before)

    @pl.when(safe_ref[0] == 1)
    def _():
        attend(False)

    @pl.when(safe_ref[0] == 0)
    def _():
        attend(True)


def attention_forward(keys, base2_t, query_t, key_t, value_t, space):
    heads = LANES // HD
    tall = pl.BlockSpec((LANES, PATCH), lambda h: (0, 0))
    per_head = lambda h: (h, 0, 0)
    elements = heads * PATCH * PATCH
    return pl.pallas_call(
        forward_body,
        grid=(heads,),
        in_specs=[pl.BlockSpec((PATCH, LANES), lambda h: (0, 0))] + [tall] * 4,
        out_specs=[
            pl.BlockSpec((1, PATCH, PATCH), per_head),
            tall,
            pl.BlockSpec((1, 1, PATCH), per_head),
            pl.BlockSpec((1, HD * HD, PATCH), per_head),
        ],
        out_shape=[
            space((heads, PATCH, PATCH), bf16),
            space((LANES, PATCH), bf16),
            pltpu.VMEM((heads, 1, PATCH), f32),
            space((heads, HD * HD, PATCH), bf16),
        ],
        scratch_shapes=[pltpu.SMEM((1,), i32)],
        compiler_params=params(16),
        cost_estimate=cost(1360 * elements, 2 * elements, elements),
        name="attention_forward",
    )(keys, base2_t, query_t, key_t, value_t)


def backward_body(first, *refs):
    (
        column_ref,
        exp_ref,
        inverse_ref,
        query_t_ref,
        value_t_ref,
        attended_ref,
        g0_ref,
        g1_ref,
        g2_ref,
        g3_ref,
        weight_ref,
        covariance_ref,
        *refs,
    ) = refs
    if first:
        later_exp_ref, *refs = refs
    else:
        rest_ref, *refs = refs
    d_out_ref, d_query_ref, d_key_ref, d_value_ref, *refs = refs
    if first:
        staged_ref, d_attended_ref, staged_sem = refs
        staged = pltpu.make_async_copy(
            later_exp_ref.at[pl.ds(0, STAGED_HEADS)], staged_ref, staged_sem
        )
    else:
        d_attended_ref, exp_all_ref, exp_sems, covariance_all_ref, covariance_sems = refs
    head = pl.program_id(0)
    at = pl.multiple_of(head * HD, HD)

    def exp_copy(h):
        return pltpu.make_async_copy(
            rest_ref.at[h + STAGED_HEADS], exp_all_ref.at[h], exp_sems.at[h]
        )

    def covariance_copy(h):
        return pltpu.make_async_copy(
            covariance_ref.at[h], covariance_all_ref.at[h], covariance_sems.at[h]
        )

    @pl.when(head == 0)
    def _():
        if first:
            staged.start()
        else:
            for h in range(LANES // HD):
                if h >= STAGED_HEADS:
                    exp_copy(h - STAGED_HEADS).start()
                covariance_copy(h).start()
        me = column_ref[0]
        for block, mask in zip((g0_ref, g1_ref, g2_ref, g3_ref), BLOCK_MASKS):
            start = pl.multiple_of((me ^ mask) * LANES, LANES)
            d_out_ref[pl.ds(start, LANES), :] = block[...]
        d_attended_ref[...] = dot(weight_ref[...].T, d_out_ref[...]).astype(bf16)

    def one_head(weights):
        grads = d_attended_ref[pl.ds(at, HD), :].astype(f32)
        query = query_t_ref[pl.ds(at, HD), :].astype(f32)
        values = value_t_ref[pl.ds(at, HD), :].astype(f32)
        inverse = inverse_ref[0]
        middle = jnp.mean(values, axis=1, keepdims=True)
        centered = values - middle
        offset = attended_ref[pl.ds(at, HD), :].astype(f32) - middle
        scaled = grads * inverse
        delta = jnp.sum(scaled * offset, axis=0, keepdims=True)
        features = [scaled[j : j + 1] * query for j in range(HD)] + [delta * query, scaled]
        sums = dot_rows(jnp.concatenate([f.astype(bf16) for f in features], axis=0), weights())
        d_value_ref[pl.ds(at, HD), :] = sums[(HD + 1) * HD :].astype(bf16)
        if first:
            covariance = covariance_ref.at[0]
        else:
            covariance_copy(head).wait()
            covariance = covariance_all_ref.at[head]
        d_key = centered[0:1] * sums[:HD]
        d_query = grads[0:1] * covariance[:HD, :].astype(f32)
        for j in range(1, HD):
            rows = slice(j * HD, (j + 1) * HD)
            d_key += centered[j : j + 1] * sums[rows]
            d_query += grads[j : j + 1] * covariance[rows, :].astype(f32)
        d_key_ref[pl.ds(at, HD), :] = (d_key - sums[HD * HD : (HD + 1) * HD]).astype(bf16)
        d_query_ref[pl.ds(at, HD), :] = (d_query * score_scale).astype(bf16)

    if first:
        one_head(lambda: exp_ref[0])

        @pl.when(head == pl.num_programs(0) - 1)
        def _():
            staged.wait()

    else:

        @pl.when(head < STAGED_HEADS)
        def _():
            one_head(lambda: exp_ref[0])

        @pl.when(head >= STAGED_HEADS)
        def _():
            exp_copy(head - STAGED_HEADS).wait()
            one_head(lambda: exp_all_ref[head - STAGED_HEADS])


def attention_backward(
    patch, first, weights, other, inverse, covariance, query_t, value_t, attended, grads, weight, column
):
    features = weight.shape[0]
    heads = LANES // HD
    tall = pl.BlockSpec((LANES, PATCH), lambda h, c: (0, 0))
    part = pl.BlockSpec((LANES, PATCH), lambda h, c: (0, patch))
    per_head = lambda h, c: (h, 0, 0)
    kept_head = lambda h, c: (jnp.minimum(h, weights.shape[0] - 1), 0, 0)
    hbm = pl.BlockSpec(memory_space=pltpu.HBM)
    elements = heads * PATCH * PATCH
    turned = pltpu.VMEM((LANES, PATCH), bf16)
    in_specs = [
        pl.BlockSpec((1, PATCH, PATCH), kept_head),
        pl.BlockSpec((1, 1, PATCH), per_head),
        tall,
        tall,
        tall,
        part,
        part,
        part,
        part,
        pl.BlockSpec(weight.shape, lambda h, c: (0, 0)),
        pl.BlockSpec((1, HD * HD, PATCH), per_head) if first else hbm,
        hbm,
    ]
    operands = [weights, inverse, query_t, value_t, attended, *grads, weight, covariance, other]
    out_specs = [pl.BlockSpec((features, PATCH), lambda h, c: (0, 0)), tall, tall, tall]
    out_shape = [pltpu.VMEM((features, PATCH), bf16), turned, turned, turned]
    scratch = [pltpu.VMEM((LANES, PATCH), bf16)]
    if first:
        out_specs.append(pl.BlockSpec(memory_space=pl.ANY))
        out_shape.append(pltpu.VMEM((STAGED_HEADS, PATCH, PATCH), bf16))
        scratch.append(pltpu.SemaphoreType.DMA(()))
    else:
        rest = heads - STAGED_HEADS
        scratch += [pltpu.VMEM((rest, PATCH, PATCH), bf16), pltpu.SemaphoreType.DMA((rest,))]
        scratch += [pltpu.VMEM((heads, HD * HD, PATCH), bf16), pltpu.SemaphoreType.DMA((heads,))]
    return pl.pallas_call(
        functools.partial(backward_body, first),
        grid_spec=pltpu.PrefetchScalarGridSpec(
            num_scalar_prefetch=1,
            grid=(heads,),
            in_specs=in_specs,
            out_specs=out_specs,
            scratch_shapes=scratch,
        ),
        out_shape=out_shape,
        compiler_params=params(9 if first else 27),
        cost_estimate=cost(1100 * elements, 2 * elements),
        name="attention_backward",
    )(column, *operands)


def whole(shape, dtype):
    return jax.ShapeDtypeStruct(shape, dtype)


def weight_grad_body(*refs):
    d_query_ref, d_key_ref, d_value_ref, attended_ref, hidden_ref, d_out_ref, *before, out_ref = refs
    d_projected = jnp.concatenate([d_query_ref[...], d_key_ref[...], d_value_ref[...]], axis=0)
    projections = dot(d_projected, hidden_ref[...])
    output = dot_rows(attended_ref[...], d_out_ref[...])
    if before:
        out_ref[:, : 3 * LANES] = (before[0][: 3 * LANES, :] + projections).T.astype(bf16)
        out_ref[:, 3 * LANES :] = (before[0][3 * LANES :, :] + output).T.astype(bf16)
    else:
        out_ref[: 3 * LANES, :] = projections
        out_ref[3 * LANES :, :] = output


def weight_grads(*operands):
    features = operands[4].shape[1]
    work = 2 * PATCH * features * LANES
    last = len(operands) > 6
    return pl.pallas_call(
        weight_grad_body,
        out_shape=whole((features, 4 * LANES), bf16) if last else pltpu.VMEM((4 * LANES, features), f32),
        compiler_params=params(12),
        cost_estimate=cost(4 * work, 12 * PATCH * features),
        name="weight_grads",
    )(*operands)


def split_sums(sums):
    high = sums.astype(bf16)
    low = (sums - high.astype(f32)).astype(bf16)
    pad = jnp.zeros((INDEX_ROWS - 2 * sums.shape[0], sums.shape[1]), f32)
    return jnp.concatenate([high.astype(f32), low.astype(f32), pad], axis=0).astype(bf16)


def join_sums(rows):
    rows = rows.astype(f32)
    return rows[0:2] + rows[2:4]


def partial_body(
    column_ref,
    d_query_ref,
    d_key_ref,
    d_value_ref,
    query_ref,
    key_ref,
    value_ref,
    weight_ref,
    mine_ref,
    other_ref,
    sums_ref,
):
    me = column_ref[0]
    d_projected = jnp.concatenate([d_query_ref[...], d_key_ref[...], d_value_ref[...]], axis=0)
    plain = jnp.zeros((1, PATCH), f32)
    for j, mask in enumerate(BLOCK_MASKS):
        start = pl.multiple_of((me ^ mask) * LANES, LANES)
        rows = [weight_ref[t, pl.ds(start, LANES), :] for t in range(3)]
        block = dot(jnp.concatenate(rows, axis=1), d_projected).astype(bf16)
        plain += jnp.sum(block.astype(f32), axis=0, keepdims=True)
        to = mine_ref if j < 2 else other_ref
        to[(j % 2) * LANES : (j % 2 + 1) * LANES, :] = block
    crossed = (
        d_query_ref[...].astype(f32) * (query_ref[...].astype(f32) / score_scale)
        + d_key_ref[...].astype(f32) * key_ref[...].astype(f32)
        + d_value_ref[...].astype(f32) * value_ref[...].astype(f32)
    )
    sums = jnp.concatenate([plain, jnp.sum(crossed, axis=0, keepdims=True)], axis=0)
    sums_ref[...] = sums
    other_ref[2 * LANES :, :] = split_sums(sums)


def hidden_part(d_query, d_key, d_value, query, key, value, weight, column):
    features = weight.shape[1]
    return pl.pallas_call(
        partial_body,
        in_specs=[pl.BlockSpec(memory_space=pltpu.SMEM)] + [pl.BlockSpec(memory_space=pltpu.VMEM)] * 7,
        out_shape=[
            pltpu.VMEM((2 * LANES, PATCH), bf16),
            pltpu.VMEM((2 * LANES + INDEX_ROWS, PATCH), bf16),
            pltpu.VMEM((2, PATCH), f32),
        ],
        compiler_params=params(12),
        cost_estimate=cost(6 * PATCH * features * LANES, 4 * PATCH * features),
        name="hidden_part",
    )(column, d_query, d_key, d_value, query, key, value, weight)


def pair_body(mine_ref, sums_ref, got_ref, kept_ref, sums_out_ref, sent_ref):
    pair = mine_ref[...].astype(f32) + got_ref[: 2 * LANES, :].astype(f32)
    sums = sums_ref[...] + join_sums(got_ref[2 * LANES :, :])
    kept_ref[...] = pair[:LANES]
    sums_out_ref[...] = sums
    sent_ref[:LANES, :] = pair[LANES:].astype(bf16)
    sent_ref[LANES:, :] = split_sums(sums)


def pair_sum(mine, sums, got):
    return pl.pallas_call(
        pair_body,
        out_shape=[
            pltpu.VMEM((LANES, PATCH), f32),
            pltpu.VMEM((2, PATCH), f32),
            pltpu.VMEM((LANES + INDEX_ROWS, PATCH), bf16),
        ],
        compiler_params=params(6),
        cost_estimate=cost(4 * LANES * PATCH, 16 * LANES * PATCH),
        name="pair_sum",
    )(mine, sums, got)


def points_body(kept_ref, sums_ref, got_ref, d_out_ref, normed_ref, inv_ref, *rest):
    out_ref = rest[-1]
    features = 4.0 * LANES
    means = (sums_ref[...] + join_sums(got_ref[LANES:, :])) / features
    d_hidden = kept_ref[...] + got_ref[:LANES, :].astype(f32) - means[0:1]
    inner = d_hidden - normed_ref[...] * means[1:2]
    out_ref[...] = (d_out_ref[...].astype(f32) + inv_ref[0:1] * inner).T


def points_grad(patch, patches, kept, sums, got, d_out, normed, inv_scale, before):
    full = lambda a: pl.BlockSpec(a.shape, lambda i: (0, 0))
    in_specs = [full(kept), full(sums), full(got), pl.BlockSpec((LANES, PATCH), lambda i: (0, patch))]
    in_specs += [full(normed), full(inv_scale)]
    operands = [kept, sums, got, d_out, normed, inv_scale]
    if before is not None:
        in_specs.append(pl.BlockSpec(memory_space=pl.ANY))
        operands.append(before)
    return pl.pallas_call(
        points_body,
        grid=(1,),
        in_specs=in_specs,
        out_specs=pl.BlockSpec((PATCH, LANES), lambda i: (patch, 0)),
        out_shape=whole((patches * PATCH, LANES), f32),
        input_output_aliases={} if before is None else {len(operands) - 1: 0},
        compiler_params=params(8),
        cost_estimate=cost(8 * LANES * PATCH, 24 * LANES * PATCH),
        name="points_grad",
    )(*operands)


def grad_sum_body(parts_ref, qkv_ref, out_ref):
    total = parts_ref[0].astype(f32)
    for j in range(1, parts_ref.shape[0]):
        total += parts_ref[j].astype(f32)
    for t in range(3):
        qkv_ref[t] = total[:, t * LANES : (t + 1) * LANES]
    out_ref[...] = total[:, 3 * LANES :]


def grad_sum(parts):
    shards, rows, width = parts.shape
    return pl.pallas_call(
        grad_sum_body,
        out_shape=[whole((3, rows, LANES), f32), whole((rows, LANES), f32)],
        compiler_params=params(8),
        cost_estimate=cost(shards * rows * width, 4 * shards * rows * width),
        name="grad_sum",
    )(parts)


def local(
    scan_points,
    send_order,
    arrive_order,
    qkv_weight,
    out_weight,
    voxel_grads,
    voxel_shard,
    voxel_point,
):
    shards = lax.axis_size("seq")
    members = lax.axis_size("mp")
    local_rows, features = scan_points.shape
    voxels = voxel_grads.shape[0]
    capacity = 2 * voxels // shards
    patches = local_rows // PATCH
    column = lax.axis_index("mp").astype(i32).reshape(1)
    zero = jnp.zeros((1,), i32)
    weight = qkv_weight.transpose(1, 0, 2)

    def swap(rows, mask):
        return lax.ppermute(rows, "mp", [(i, i ^ mask) for i in range(members)])

    def exchange(rows):
        return lax.all_to_all(rows, "seq", split_axis=0, concat_axis=0, tiled=True)

    def after(value, first):
        return lax.optimization_barrier((value, first))

    def in_hbm(value):
        return pltpu.with_memory_space_constraint(value, pltpu.HBM)

    arrived = exchange(permute_rows(scan_points, send_order, column, 0, 1, whole, 60))
    buckets = bucket_rows(voxel_grads, voxel_shard, voxel_point, column, shards, capacity)
    owns = [
        permute_rows(arrived, arrive_order, zero, p, patches, pltpu.VMEM, 12)
        for p in range(patches)
    ]
    buckets, owns[0] = after(buckets, owns[0])
    got = exchange(buckets.reshape(shards * (capacity + INDEX_ROWS), LANES))
    across = [swap(own, 2) for own in owns]
    across[0], owns[1] = after(across[0], owns[1])

    def project_patch(p):
        columns = (owns[p], across[p], swap(owns[p], 1), swap(across[p], 1))
        return project(columns, weight, column, pltpu.HBM, pltpu.VMEM if p == 0 else pltpu.HBM)

    def forward(p, projected):
        space = pltpu.VMEM if p == patches - 1 else pltpu.HBM
        return attention_forward(*projected[3:], space)

    projected0 = project_patch(0)
    forward0 = forward(0, projected0)
    across[1], forward0 = after(across[1], forward0)
    projected1 = project_patch(1)
    got, projected1 = after(got, projected1)
    summed_rows = segment_rows(got.reshape(shards, capacity + INDEX_ROWS, LANES), local_rows)
    summed_across = swap(summed_rows, 2)
    projected1, summed_rows = after(projected1, summed_rows)
    forward1 = forward(1, projected1)
    summed_across, forward1 = after(summed_across, forward1)
    grads = (summed_rows, summed_across, swap(summed_rows, 1), swap(summed_across, 1))
    forwards = [(projected0, forward0), (projected1, forward1)]

    kept, sums, received = {}, {}, {}
    for p in reversed(range(patches)):
        (hidden, _, _, _, _, query_t, key_t, value_t), (weights, attended, inverse, covariance) = forwards[p]
        if p == 0:
            weights, sent = after(weights, sent)
            received[1] = swap(sent, 2)
            other_exp, covariance, weights = in_hbm(weights), in_hbm(covariance), staged[0]
        else:
            other_exp = in_hbm(forwards[0][1][0])
        d_out, d_query, d_key, d_value, *staged = attention_backward(
            p, p > 0, weights, other_exp, inverse, covariance, query_t, value_t, attended, grads, out_weight, column
        )
        if p == 0:
            received[1], d_query = after(received[1], d_query)
        grad_operands = (d_query, d_key, d_value, attended, hidden, d_out)
        if p == 0:
            weight_parts = weight_grads(*grad_operands, first_parts)
            operands = (d_query, d_key, d_value, query_t, key_t, value_t)
            operands, weight_parts = after(operands, weight_parts)
            d_query, d_key, d_value, query_t, key_t, value_t = map(in_hbm, operands)
        mine, other, own_sums = hidden_part(d_query, d_key, d_value, query_t, key_t, value_t, weight, column)
        partner = swap(other, 1)
        if p > 0:
            first_parts = weight_grads(*grad_operands)
            partner, first_parts = after(partner, first_parts)
        kept[p], sums[p], sent = pair_sum(mine, own_sums, partner)
    received[0] = swap(sent, 2)
    d_points = None
    for p in reversed(range(patches)):
        normed, inv_scale = forwards[p][0][1:3]
        if p > 0:
            normed, inv_scale = in_hbm(normed), in_hbm(inv_scale)
        d_points = points_grad(
            p, patches, kept[p], sums[p], received[p], grads[0], normed, inv_scale, d_points
        )
    parts = exchange(weight_parts).reshape(shards, features // shards, 4 * LANES)
    grad_qkv, grad_out = grad_sum(parts)
    return (d_points, grad_qkv.transpose(1, 0, 2), grad_out)


def solution(mesh):
    in_specs = (
        P("seq", None),
        P("seq"),
        P("seq"),
        P(None, None, "mp"),
        P(None, "mp"),
        P("seq", None),
        P("seq", None),
        P("seq"),
    )
    out_specs = (P("seq", "mp"), P("seq", None, "mp"), P("seq", "mp"))
    return jax.shard_map(local, mesh=mesh, in_specs=in_specs, out_specs=out_specs, check_vma=False)
```
